256 devices in a mesh: expert: 32 (over z, y), tensor: 8 (over x, core).
Axes of the slice: x: 4, y: 4, z: 8, core: 2. Of those that a mesh axis runs over, the one named last changes fastest.
Arguments:
- tokens: bfloat16 [2048, 5120], P(('expert', 'tensor')), may hold values from -6 to 6
- routes: int32 [2048, 6], P(('expert', 'tensor')), may hold values from 0 to 31, all different within a row; in each aligned block of 64 rows (0 to 63, 64 to 127, ...) at most 16 rows name the same one
- gate_num: int32 [2048, 6], P(('expert', 'tensor')), may hold values from 1 to 64
- cotangent: bfloat16 [2048, 5120], P(('expert', 'tensor')), may hold values from -6 to 6
- w_in: bfloat16 [32, 2, 768, 5120], P('expert', None, 'tensor'), may hold values from -0.078125 to 0.078125
- w_out: bfloat16 [32, 768, 5120], P('expert', 'tensor'), may hold values from -0.21875 to 0.21875
- shared_in: bfloat16 [2, 1536, 5120], P(None, 'tensor'), may hold values from -0.078125 to 0.078125
- shared_out: bfloat16 [1536, 5120], P('tensor'), may hold values from -0.15625 to 0.15625
Outputs:
- output: bfloat16 [2048, 5120], P(('expert', 'tensor'))
- grad_tokens: bfloat16 [2048, 5120], P(('expert', 'tensor'))
- grad_in: bfloat16 [32, 2, 768, 5120], P('expert', None, 'tensor')
- grad_out: bfloat16 [32, 768, 5120], P('expert', 'tensor')
The draws below stay inside these ranges and needn't reach their ends.
Inputs may be any that keep to these rules, and one draw needn't show every extreme that they name: `routes`: each row names 6 different experts. In each group of 64 tokens no expert is named by more than 16 tokens, a bound that some block reaches.
All inputs are finite; a program needn't handle non-finite values.
Results may differ from the reference program's by a relative error of at most 0.019.
Values may be sent and summed in bfloat16 or wider, within the bound.
A program may use at most 128 MiB of HBM per device.

```python
import math
import jax
import jax.numpy as jnp
import numpy as np
from jax import lax

D = 5120
HID = 768
SHID = 1536
TOPK = 6
TOK_DEV = 8
EXPERTS = 32
GROUP = 64
CAP = 16
TOKENS = 2048
N_EXPERT = 32
N_TENSOR = 8


def set_ends(result, key, low, high):
    place = [jax.random.randint(jax.random.fold_in(key, axis), (), 0, length) for axis, length in enumerate(result.shape)]
    main_axis = result.shape.index(max(result.shape))
    neighbour = place[:main_axis] + [(place[main_axis] + 1) % result.shape[main_axis]] + place[main_axis + 1:]
    return result.at[tuple(place)].set(low).at[tuple(neighbour)].set(high)


def block_levels(stream_key, dims, shards, smallest, top_value):
    level, own = 1.0, jax.random.fold_in(stream_key, 6)
    for axis_at, blocks in shards:
        heights = jnp.exp(jax.random.uniform(jax.random.fold_in(own, axis_at), (blocks,), jnp.float32, smallest / len(shards), top_value / len(shards)))
        level = level * jnp.repeat(heights, dims[axis_at] // blocks).reshape([-1 if axis == axis_at else 1 for axis in range(len(dims))])
    return level


def deal_out(key, own, number, rows, amount, top, limit, slope):
    order = jax.random.permutation(key, amount)
    heavy_load, ordinary = shares(amount, rows * top, limit, slope, True), shares(amount, rows * top, limit, slope, False)
    places = jnp.arange(amount)

    def named(lengths, rotation):
        used = int((lengths > 0).sum())
        fixed = max(1, used // 4)
        shifted = fixed + (places - fixed + rotation * (used - fixed)) % max(1, amount - fixed)
        return jnp.zeros((amount,), jnp.int32).at[order[jnp.where(places < fixed, places, shifted)]].set(jnp.asarray(lengths, jnp.int32))

    lengths = jnp.where(number % 4 == 0, named(heavy_load, number // 4), named(ordinary, number - number // 4 - 1))
    mixed = jax.random.permutation(jax.random.fold_in(own, 3), amount)
    donor, receiver = mixed[0:amount // 2 * 2:2], mixed[1:amount // 2 * 2:2]
    margin = jnp.minimum(lengths[donor] - 1, limit - lengths[receiver]) // 2
    margin = jnp.where((donor == order[0]) | (receiver == order[0]) | (lengths[receiver] == 0), 0, jnp.maximum(margin, 0))
    shifted = jax.random.randint(jax.random.fold_in(own, 4), (amount // 2,), 0, 1 << 20) % (margin + 1)
    lengths = lengths.at[donor].add(-shifted).at[receiver].add(shifted)
    members = jnp.searchsorted(jnp.cumsum(lengths), jnp.arange(rows * top), side="right").astype(jnp.int32)
    listing = members.reshape(top, rows).T
    listing = listing[jax.random.permutation(jax.random.fold_in(own, 1), rows)]
    rotation = jax.random.randint(jax.random.fold_in(own, 2), (rows, 1), 0, top)
    return jnp.take_along_axis(listing, (jnp.arange(top)[None, :] + rotation) % top, axis=1)


def shares(amount, total, limit, slope, full):
    loads = [(1 << 20) // math.isqrt(standing ** slope) + 1 for standing in range(1, amount + 1)]
    largest = limit if full else min(limit, max(-(-total // amount), total * loads[0] // sum(loads)))
    least = 1 if total - largest >= amount - 1 else 0
    holding, spare = [largest] + [least] * (amount - 1), total - largest - least * (amount - 1)
    while spare > 0:
        candidates = [i for i in range(1, amount) if holding[i] < largest] or [i for i in range(1, amount) if holding[i] < limit]
        pool, budget = sum([loads[i] for i in candidates]), spare
        for i in candidates:
            addition = min(limit - holding[i], max(1, budget * loads[i] // pool), spare)
            holding[i] = holding[i] + addition
            spare = spare - addition
    return np.array(holding)


def normal_values(key, extent, scale, most, pieces=(), kind=jnp.bfloat16):
    entries = scale * jax.random.normal(key, extent, jnp.float32)
    if pieces:
        entries = entries * block_levels(key, extent, pieces, -0.22, 0.18)
    return jnp.clip(entries, -most, most).astype(kind)


def setup_inputs(seed: int = 0) -> dict:
    key_list = jax.random.split(jax.random.key(seed), 9)
    tokens = normal_values(key_list[0], (TOKENS, D), 1.0, 6.0, ((0, 256),))
    routes_keys = jax.random.split(jax.random.fold_in(key_list[1], 1), TOKENS // GROUP)
    routes_turns = jax.random.permutation(jax.random.fold_in(key_list[1], 3), TOKENS // GROUP)
    routes = jax.vmap(lambda own, number: deal_out(jax.random.fold_in(key_list[1], 2), own, number, GROUP, EXPERTS, TOPK, CAP, 1))(routes_keys, routes_turns).reshape((TOKENS, TOPK))
    gate_num = set_ends(jax.random.randint(key_list[2], (TOKENS, TOPK), 1, 65), jax.random.fold_in(key_list[2], 1), 1, 64).astype(jnp.int32)
    cotangent = normal_values(key_list[3], (TOKENS, D), 1.0, 6.0, ((0, 256),))
    w_in = normal_values(key_list[4], (EXPERTS, 2, HID, D), D ** -0.5, 0.078125, ((0, 32), (2, 8)))
    w_out = normal_values(key_list[5], (EXPERTS, HID, D), HID ** -0.5, 0.21875, ((0, 32), (1, 8)))
    shared_in = normal_values(key_list[6], (2, SHID, D), D ** -0.5, 0.078125, ((1, 8),))
    shared_out = normal_values(key_list[7], (SHID, D), SHID ** -0.5, 0.15625, ((0, 8),))
    return {"tokens": tokens, "routes": routes, "gate_num": gate_num, "cotangent": cotangent, "w_in": w_in, "w_out": w_out, "shared_in": shared_in, "shared_out": shared_out}


denominator = 64.0


def silu_parts(preact):
    sig_value = jax.nn.sigmoid(preact)
    return preact * sig_value, sig_value * (1.0 + preact * (1.0 - sig_value))


def slot_tables(route_rows, gate_rows, experts, capacity):
    row_count, top_count = route_rows.shape
    flat_ids = route_rows.reshape(row_count * top_count)
    expert_ids = jnp.arange(experts, dtype=jnp.int32)
    onehot = (flat_ids[:, None] == expert_ids[None, :]).astype(jnp.int32)
    before = jnp.cumsum(onehot, axis=0, dtype=jnp.int32) - onehot
    slot_rank = jnp.sum(before * onehot, axis=1, dtype=jnp.int32)
    slot_index = (flat_ids * capacity + slot_rank).reshape(row_count, top_count)
    positions = jnp.arange(experts * capacity, dtype=jnp.int32)
    matches = slot_index[None, :, :] == positions[:, None, None]
    select = jnp.sum(jnp.where(matches, jnp.float32(1.0), jnp.float32(0.0)), axis=2).astype(jnp.float32)
    gate_share = gate_rows.astype(jnp.float32) / denominator
    weight = jnp.sum(jnp.where(matches, gate_share[None, :, :], jnp.float32(0.0)), axis=2).astype(jnp.float32)
    return select, weight


def reference(tokens, routes, gate_num, cotangent, w_in, w_out, shared_in, shared_out):
    groups = N_EXPERT
    row_count = TOK_DEV * N_TENSOR
    features = tokens.shape[1]
    blocks = N_TENSOR
    highest = lax.Precision.HIGHEST

    def per_group(route_rows, gate_rows):
        return slot_tables(route_rows, gate_rows, EXPERTS, CAP)

    select, weight = jax.vmap(per_group)(routes.reshape(groups, row_count, TOPK), gate_num.reshape(groups, row_count, TOPK))
    group_x = tokens.reshape(groups, row_count, features).astype(jnp.float32)
    group_dy = cotangent.reshape(groups, row_count, features).astype(jnp.float32)
    send_x = jnp.einsum('gst,gtd->gsd', select, group_x, precision=highest).astype(jnp.bfloat16)
    send_dy = jnp.einsum('gst,gtd->gsd', weight, group_dy, precision=highest).astype(jnp.bfloat16)
    send_x = send_x.reshape(groups, EXPERTS, CAP, features).transpose(1, 0, 2, 3).reshape(EXPERTS, groups * CAP, features)
    send_dy = send_dy.reshape(groups, EXPERTS, CAP, features).transpose(1, 0, 2, 3).reshape(EXPERTS, groups * CAP, features)

    def expert(operands):
        rows_x, rows_dy, w_pair, w_down = operands
        hidden_width = w_down.shape[0]
        block_width = hidden_width // blocks
        gate_pre = jnp.dot(rows_x, w_pair[0].T, preferred_element_type=jnp.float32)
        up_pre = jnp.dot(rows_x, w_pair[1].T, preferred_element_type=jnp.float32)
        active, slopes = silu_parts(gate_pre)
        hidden = (active * up_pre).astype(jnp.bfloat16)
        out_blocks = jnp.einsum('rbh,bhd->brd', hidden.reshape(-1, blocks, block_width).astype(jnp.float32),
                                w_down.reshape(blocks, block_width, features).astype(jnp.float32), precision=highest)
        out_sum = jnp.sum(lax.optimization_barrier(out_blocks.astype(jnp.bfloat16)).astype(jnp.float32), axis=0)
        back_grad = jnp.dot(rows_dy, w_down.T, preferred_element_type=jnp.float32)
        d_gate = (back_grad * up_pre * slopes).astype(jnp.bfloat16)
        d_up = (back_grad * active).astype(jnp.bfloat16)
        x_blocks = jnp.einsum('rbh,bhd->brd', d_gate.reshape(-1, blocks, block_width).astype(jnp.float32),
                              w_pair[0].reshape(blocks, block_width, features).astype(jnp.float32), precision=highest)
        x_blocks = x_blocks + jnp.einsum('rbh,bhd->brd', d_up.reshape(-1, blocks, block_width).astype(jnp.float32),
                                         w_pair[1].reshape(blocks, block_width, features).astype(jnp.float32), precision=highest)
        x_sum = jnp.sum(lax.optimization_barrier(x_blocks.astype(jnp.bfloat16)).astype(jnp.float32), axis=0)
        grad_down = jnp.dot(hidden.T, rows_dy, preferred_element_type=jnp.float32).astype(jnp.bfloat16)
        grad_pair = jnp.stack([jnp.dot(d_gate.T, rows_x, preferred_element_type=jnp.float32),
                               jnp.dot(d_up.T, rows_x, preferred_element_type=jnp.float32)]).astype(jnp.bfloat16)
        return out_sum, x_sum, grad_pair, grad_down

    out_sum, x_sum, grad_in, grad_out = lax.map(expert, (send_x, send_dy, w_in, w_out))
    out_sum = out_sum.reshape(EXPERTS, groups, CAP, features).transpose(1, 0, 2, 3).reshape(groups, EXPERTS * CAP, features)
    x_sum = x_sum.reshape(EXPERTS, groups, CAP, features).transpose(1, 0, 2, 3).reshape(groups, EXPERTS * CAP, features)
    routed_y = jnp.einsum('gst,gsd->gtd', weight, out_sum, precision=highest).reshape(TOKENS, features)
    routed_dx = jnp.einsum('gst,gsd->gtd', select, x_sum, precision=highest).reshape(TOKENS, features)
    shared_gate = jnp.dot(tokens, shared_in[0].T, preferred_element_type=jnp.float32)
    shared_up = jnp.dot(tokens, shared_in[1].T, preferred_element_type=jnp.float32)
    shared_act, shared_slope = silu_parts(shared_gate)
    shared_hidden = (shared_act * shared_up).astype(jnp.bfloat16)
    shared_y = jnp.dot(shared_hidden, shared_out, preferred_element_type=jnp.float32)
    shared_back = jnp.dot(cotangent, shared_out.T, preferred_element_type=jnp.float32)
    shared_dgate = (shared_back * shared_up * shared_slope).astype(jnp.bfloat16)
    shared_dup = (shared_back * shared_act).astype(jnp.bfloat16)
    shared_dx = jnp.dot(shared_dgate, shared_in[0], preferred_element_type=jnp.float32)
    shared_dx = shared_dx + jnp.dot(shared_dup, shared_in[1], preferred_element_type=jnp.float32)
    output = (shared_y + routed_y).astype(jnp.bfloat16)
    grad_tokens = (shared_dx + routed_dx).astype(jnp.bfloat16)
    return output, grad_tokens, grad_in, grad_out
```

```python
import functools

import jax
import jax.numpy as jnp
from jax import lax
from jax.experimental import pallas as pl
from jax.experimental.pallas import tpu as pltpu
from jax.sharding import PartitionSpec as P

MESH = pl.DeviceIdType.MESH
BF = jnp.bfloat16
F32 = jnp.float32
SLOTS = 16
NT = (((1,), (1,)), ((), ()))
TN = (((0,), (0,)), ((), ()))

TAB, SLICE, TOKENS, WEIGHT, DISPATCH, PARTNER, PRE, ACT, GRAD_IN, GRAD_OUT, SHARED, FINAL, BACK = range(13)
HALF = 13
COUNT = 17


def dot(left, right, dims=None):
    dims = dims or (((1,), (0,)), ((), ()))
    return lax.dot_general(left, right, dims, preferred_element_type=F32)


def silu_parts(preact):
    sig_value = jax.nn.sigmoid(preact)
    return preact * sig_value, sig_value * (1.0 + preact * (1.0 - sig_value))


def kernel(
    topk,
    pair_ref, table_ref, w_in, w_out, sh_in, sh_out,
    out_ref, gtok_ref, gin_ref, gout_ref,
    tabs, gs, g, wt, sw_in, sw_out, t2, snd, xr, pf, pb, rs, act, ps, pr, ret, bk, gb, shs, shr, fs, fr,
    ssem, rsem, lsem,
):
    ne, nt = lax.axis_size("expert"), lax.axis_size("tensor")
    e, t = lax.axis_index("expert"), lax.axis_index("tensor")
    chip, core = t // 2, t % 2
    chips = nt // 2
    d8 = gs.shape[1]
    hid = w_out.shape[0]
    half = chips * hid
    gc = ne // chips
    rows = gc * SLOTS
    m32 = 2 * SLOTS

    def rcopy(src, dst, which, dev):
        return pltpu.make_async_remote_copy(
            src_ref=src, dst_ref=dst, send_sem=ssem.at[which], recv_sem=rsem.at[which],
            device_id=dev, device_id_type=MESH,
        )

    def recv(ref, which):
        pltpu.make_async_copy(ref, ref, rsem.at[which]).wait()

    def sent(ref, which):
        pltpu.make_async_copy(ref, ref, ssem.at[which]).wait()

    def cols(piece):
        return pl.ds(pl.multiple_of(piece * d8, 128), d8)

    def block(index, size):
        return pl.ds(pl.multiple_of(index * size, 16), size)

    own_shared = [
        pltpu.make_async_copy(sh_in, sw_in, lsem.at[0]),
        pltpu.make_async_copy(sh_out, sw_out, lsem.at[1]),
    ]
    own_weights = []
    for h in range(2):
        for m in range(3):
            source = w_out if m == 2 else w_in.at[m]
            own_weights.append(pltpu.make_async_copy(
                source.at[:, cols(2 * chip + h)], wt.at[h, m, block(chip, hid)], lsem.at[2 + 3 * h + m]))
    for copy in own_weights + own_shared:
        copy.start()

    barrier = pltpu.get_barrier_semaphore()

    @pl.loop(1, ne)
    def _(k):
        pl.semaphore_signal(barrier, inc=1, device_id=(lax.rem(e + k, ne), t), device_id_type=MESH)

    @pl.loop(1, nt)
    def _(k):
        pl.semaphore_signal(barrier, inc=1, device_id=(e, lax.rem(t + k, nt)), device_id_type=MESH)

    pl.semaphore_wait(barrier, ne + nt - 2)

    @pl.loop(1, nt)
    def _(k):
        p = lax.rem(t + k, nt)
        rcopy(table_ref, tabs.at[block(t, 16)], TAB, (e, p)).start()
        rcopy(pair_ref.at[:, cols(p)], gs.at[block(t, 16)], SLICE, (e, p)).start()

    @pl.loop(1, nt)
    def _(k):
        rcopy(pair_ref, g.at[block(t, 16)], TOKENS, (e, lax.rem(t + k, nt))).start()

    @pl.loop(1, chips)
    def _(k):
        q = lax.rem(t + 2 * k, nt)
        for h in range(2):
            for m in range(3):
                source = w_out if m == 2 else w_in.at[m]
                rcopy(source.at[:, cols(2 * (q // 2) + h)], wt.at[h, m, block(chip, hid)], WEIGHT, (e, q)).start()

    tabs[block(t, 16), :] = table_ref[...]
    gs[block(t, 16), :] = pair_ref[:, cols(t)]
    g[block(t, 16), :] = pair_ref[...]

    recv(tabs.at[pl.ds(0, (nt - 1) * 16)], TAB)
    recv(gs.at[pl.ds(0, (nt - 1) * 16)], SLICE)
    lanes = nt * 16
    chosen = tabs[...].astype(F32).T
    lane_a = lax.broadcasted_iota(jnp.int32, (lanes, lanes), 0)
    lane_b = lax.broadcasted_iota(jnp.int32, (lanes, lanes), 1)
    token_a, token_b = (lane_a // 16) * 8 + lane_a % 8, (lane_b // 16) * 8 + lane_b % 8
    earlier = jnp.where((lane_a % 16 < 8) & (token_a < token_b), 1.0, 0.0).astype(BF)
    tokens_here = gs[...]
    for chunk in range(chips):
        size = gc * m32
        row = lax.broadcasted_iota(jnp.int32, (size, lanes), 0) + chunk * size
        lane = lax.broadcasted_iota(jnp.int32, (size, lanes), 1)
        kind, slot = (row // SLOTS) % 2, (row % SLOTS).astype(F32)
        expert = (row // m32).astype(F32)
        named = jnp.zeros((size, lanes), F32)
        gate = jnp.zeros((size, lanes), F32)
        for k in range(topk):
            hit = chosen[k:k + 1, :] == expert
            named = jnp.where(hit, 1.0, named)
            gate = jnp.where(hit, chosen[topk + k:topk + k + 1, :] * (1.0 / 64.0), gate)
        rank = dot(named.astype(BF), earlier)
        here = jnp.where((rank == slot) & ((lane // 8) % 2 == kind), named, 0.0)
        there = jnp.where(kind == 1, here * gate, here).astype(BF)
        t2[pl.ds(chunk * size, size), :] = jnp.where(kind == 1, here, here * gate).astype(BF)
        snd[pl.ds(chunk * gc, gc)] = dot(there, tokens_here).astype(BF).reshape(gc, m32, d8)

    @pl.loop(1, ne)
    def _(k):
        p = lax.rem(e + k, ne)
        rcopy(snd.at[p], xr.at[core, e], DISPATCH, (p, t)).start()

    xr[core, e] = snd[e]

    recv(g.at[pl.ds(0, (nt - 1) * 16)], TOKENS)
    for copy in own_shared:
        copy.wait()
    sh = sw_out.shape[0]

    def shared_step(n, sums):
        piece = g[:, cols(n)]
        return tuple(
            total + dot(piece, weight[:, cols(n)], NT)
            for total, weight in zip(sums, (sw_in.at[0], sw_in.at[1], sw_out)))

    zero = jnp.zeros((nt * 16, sh), F32)
    sums = lax.fori_loop(0, nt, shared_step, (zero, zero, zero))
    s_gate, s_up = [v.reshape(nt, 16, sh)[:, :8].reshape(nt * 8, sh) for v in sums[:2]]
    s_back = sums[2].reshape(nt, 16, sh)[:, 8:].reshape(nt * 8, sh)
    s_act, s_slope = silu_parts(s_gate)
    s_hidden = (s_act * s_up).astype(BF)
    s_dgate = (s_back * s_up * s_slope).astype(BF)
    s_dup = (s_back * s_act).astype(BF)

    @pl.loop(0, nt)
    def _(n):
        y = dot(s_hidden, sw_out[:, cols(n)]).reshape(nt, 8, d8)
        dx = (dot(s_dgate, sw_in[0, :, cols(n)]) + dot(s_dup, sw_in[1, :, cols(n)])).reshape(nt, 8, d8)
        shs[:, :, cols(n)] = jnp.concatenate([y, dx], axis=1).astype(BF)

    partner = t + 1 - 2 * core
    recv(xr.at[core, pl.ds(0, ne - 1)], DISPATCH)
    rcopy(xr.at[core], xr.at[core], PARTNER, (e, partner)).start()
    for copy in own_weights:
        copy.wait()
    recv(wt.at[:, :, pl.ds(0, (chips - 1) * hid)], WEIGHT)

    def products(h, j):
        part = xr[h, pl.ds(j * gc, gc)]
        x_rows = part[:, :SLOTS].reshape(rows, d8)
        dy_rows = part[:, SLOTS:].reshape(rows, d8)
        return dot(x_rows, wt[h, 0], NT), dot(x_rows, wt[h, 1], NT), dot(dy_rows, wt[h, 2], NT)

    @pl.loop(0, chips)
    def _(j):
        for m, value in enumerate(products(core, j)):
            pf[j, :, m * half:(m + 1) * half] = value

    recv(xr.at[1 - core], PARTNER)

    @pl.loop(1, chips + 1)
    def _(k):
        j = lax.rem(chip + k, chips)
        for m, value in enumerate(products(1 - core, j)):
            span = slice(m * half, (m + 1) * half)
            total = pf[j, :, span] + value
            pf[j, :, span] = total
            pb[j, :, span] = total.astype(BF)

        @pl.when(k < chips)
        def _():
            rcopy(pb.at[j], rs.at[chip], PRE, (e, 2 * j + core)).start()

    recv(rs.at[pl.ds(0, chips - 1)], PRE)
    total = pf[chip]
    for k in range(1, chips):
        total = total + rs[lax.rem(chip + k, chips)].astype(F32)
    gate_pre, up_pre, back = total[:, :half], total[:, half:2 * half], total[:, 2 * half:]
    active, slope = silu_parts(gate_pre)
    act[chip, :, :half] = (active * up_pre).astype(BF)
    act[chip, :, half:2 * half] = (back * up_pre * slope).astype(BF)
    act[chip, :, 2 * half:] = (back * active).astype(BF)

    @pl.loop(1, chips)
    def _(k):
        rcopy(act.at[chip], act.at[chip], ACT, (e, lax.rem(t + 2 * k, nt))).start()

    recv(act.at[pl.ds(0, chips - 1)], ACT)

    @pl.loop(1, nt)
    def _(k):
        p = lax.rem(t + k, nt)
        rcopy(shs.at[p], shr.at[t], SHARED, (e, p)).start()

    def results(h, j):
        y = dot(act[j, :, :half], wt[h, 2])
        dx = dot(act[j, :, half:], wt[h, 0:2].reshape(2 * half, d8))
        return jnp.concatenate([y.reshape(gc, SLOTS, d8), dx.reshape(gc, SLOTS, d8)], axis=1)

    first = (e * chips) // ne

    @pl.loop(0, chips)
    def _(k):
        j = lax.rem(first + k, chips)
        ps[pl.ds(j * gc, gc)] = results(1 - core, j).astype(BF)
        rcopy(ps.at[pl.ds(j * gc, gc)], pr.at[pl.ds(j * gc, gc)], HALF + k, (e, partner)).start()

    @pl.loop(0, chips)
    def _(k):
        j = lax.rem(first + k, chips)
        value = results(core, j)
        recv(pr.at[pl.ds(j * gc, gc)], HALF + k)
        ret[pl.ds(j * gc, gc)] = (value + pr[pl.ds(j * gc, gc)].astype(F32)).astype(BF)

        @pl.loop(0, gc)
        def _(n):
            p = j * gc + n

            @pl.when(p != e)
            def _():
                rcopy(ret.at[p], bk.at[e], BACK, (p, t)).start()

    bk[e] = ret[e]

    own_grads = []
    for h in range(2):
        for m in range(3):
            right = (xr[h, :, SLOTS:] if m == 2 else xr[h, :, :SLOTS]).reshape(ne * SLOTS, d8)
            if m == 2:
                left = act[:, :, :half].reshape(chips * rows, half)
            else:
                left = act[:, :, (m + 1) * half:(m + 2) * half].reshape(chips * rows, half)
            gb[h, m] = dot(left, right, TN).astype(BF)
            target = gout_ref if m == 2 else gin_ref.at[m]
            which = GRAD_OUT if m == 2 else GRAD_IN
            own = pltpu.make_async_copy(
                gb.at[h, m, block(chip, hid)], target.at[:, cols(2 * chip + h)], lsem.at[2 + 3 * h + m])
            own.start()
            own_grads.append(own)

            @pl.loop(1, chips)
            def _(k):
                q = lax.rem(t + 2 * k, nt)
                rcopy(gb.at[h, m, block(q // 2, hid)], target.at[:, cols(2 * chip + h)], which, (e, q)).start()

    recv(bk.at[pl.ds(0, ne - 1)], BACK)
    routed = dot(t2[...], bk[...].reshape(ne * m32, d8), TN)
    fs[...] = routed.astype(BF).reshape(nt, 16, d8)

    @pl.loop(1, nt)
    def _(k):
        p = lax.rem(t + k, nt)
        rcopy(fs.at[p], fr.at[t], FINAL, (e, p)).start()

    fr[t] = fs[t]
    shr[t] = shs[t]
    recv(shr.at[pl.ds(0, nt - 1)], SHARED)
    recv(fr.at[pl.ds(0, nt - 1)], FINAL)

    for n in range(nt):
        span = slice(n * d8, (n + 1) * d8)
        total = fr[n].astype(F32) + jnp.sum(shr[:, :, span].astype(F32), axis=0)
        out_ref[:, span] = total[:8].astype(BF)
        gtok_ref[:, span] = total[8:].astype(BF)

    recv(gin_ref.at[:, :, pl.ds(0, 2 * (chips - 1) * d8)], GRAD_IN)
    recv(gout_ref.at[:, pl.ds(0, 2 * (chips - 1) * d8)], GRAD_OUT)
    for copy in own_grads:
        copy.wait()
    sent(tabs.at[pl.ds(0, (nt - 1) * 16)], TAB)
    sent(gs.at[pl.ds(0, (nt - 1) * 16)], SLICE)
    sent(g.at[pl.ds(0, (nt - 1) * 16)], TOKENS)
    sent(wt.at[:, :, pl.ds(0, (chips - 1) * hid)], WEIGHT)
    sent(snd.at[pl.ds(0, ne - 1)], DISPATCH)
    sent(xr.at[core], PARTNER)
    sent(pb.at[pl.ds(0, chips - 1)], PRE)
    sent(rs.at[pl.ds(0, chips - 1)], ACT)
    for k in range(chips):
        sent(ps.at[pl.ds(0, gc)], HALF + k)
    sent(ret.at[pl.ds(0, ne - 1)], BACK)
    sent(gin_ref.at[:, :, pl.ds(0, 2 * (chips - 1) * d8)], GRAD_IN)
    sent(gout_ref.at[:, pl.ds(0, 2 * (chips - 1) * d8)], GRAD_OUT)
    sent(shs.at[pl.ds(0, nt - 1)], SHARED)
    sent(fs.at[pl.ds(0, nt - 1)], FINAL)


def on_device(tokens, routes, gate_num, cotangent, w_in, w_out, shared_in, shared_out):
    ne, nt = lax.axis_size("expert"), lax.axis_size("tensor")
    chips = nt // 2
    own, features = tokens.shape
    topk = routes.shape[1]
    hid, sh = w_out.shape[1], shared_out.shape[0]
    d8, half, gc = features // nt, chips * hid, ne // chips
    rows, m32 = gc * SLOTS, 2 * SLOTS
    pair = jnp.concatenate([tokens, cotangent], axis=0)
    table = jnp.concatenate([routes, gate_num], axis=1)
    table = jnp.pad(jnp.concatenate([table, table], axis=0), ((0, 0), (0, 128 - 2 * topk)))
    vm = pl.BlockSpec(memory_space=pltpu.VMEM)
    hbm = pl.BlockSpec(memory_space=pl.ANY)
    scratch = [
        pltpu.VMEM((nt * 16, 128), jnp.int32),
        pltpu.VMEM((nt * 16, d8), BF),
        pltpu.VMEM((nt * 16, features), BF),
        pltpu.VMEM((2, 3, half, d8), BF),
        pltpu.VMEM((2, sh, features), BF),
        pltpu.VMEM((sh, features), BF),
        pltpu.VMEM((ne * m32, nt * 16), BF),
        pltpu.VMEM((ne, m32, d8), BF),
        pltpu.VMEM((2, ne, m32, d8), BF),
        pltpu.VMEM((chips, rows, 3 * half), F32),
        pltpu.VMEM((chips, rows, 3 * half), BF),
        pltpu.VMEM((chips, rows, 3 * half), BF),
        pltpu.VMEM((chips, rows, 3 * half), BF),
        pltpu.VMEM((ne, m32, d8), BF),
        pltpu.VMEM((ne, m32, d8), BF),
        pltpu.VMEM((ne, m32, d8), BF),
        pltpu.VMEM((ne, m32, d8), BF),
        pltpu.VMEM((2, 3, half, d8), BF),
        pltpu.VMEM((nt, 16, features), BF),
        pltpu.VMEM((nt, 16, features), BF),
        pltpu.VMEM((nt, 16, d8), BF),
        pltpu.VMEM((nt, 16, d8), BF),
        pltpu.SemaphoreType.DMA((COUNT,)),
        pltpu.SemaphoreType.DMA((COUNT,)),
        pltpu.SemaphoreType.DMA((8,)),
    ]
    out, gtok, gin, gout = pl.pallas_call(
        functools.partial(kernel, topk),
        out_shape=(
            jax.ShapeDtypeStruct((own, features), BF),
            jax.ShapeDtypeStruct((own, features), BF),
            jax.ShapeDtypeStruct((2, hid, features), BF),
            jax.ShapeDtypeStruct((hid, features), BF),
        ),
        in_specs=[vm, vm, hbm, hbm, hbm, hbm],
        out_specs=(vm, vm, hbm, hbm),
        scratch_shapes=scratch,
        compiler_params=pltpu.CompilerParams(
            collective_id=0, has_side_effects=True, vmem_limit_bytes=56 * 2**20
        ),
    )(pair, table, w_in[0], w_out[0], shared_in, shared_out)
    return out, gtok, gin[None], gout[None]


def solution(mesh):
    in_specs = (
        P(("expert", "tensor"), None),
        P(("expert", "tensor"), None),
        P(("expert", "tensor"), None),
        P(("expert", "tensor"), None),
        P("expert", None, "tensor", None),
        P("expert", "tensor", None),
        P(None, "tensor", None),
        P("tensor", None),
    )
    out_specs = (
        P(("expert", "tensor"), None),
        P(("expert", "tensor"), None),
        P("expert", None, "tensor", None),
        P("expert", "tensor", None),
    )
    return jax.shard_map(
        on_device, mesh=mesh, in_specs=in_specs, out_specs=out_specs, check_vma=False
    )
```

```python
import functools

import jax
import jax.numpy as jnp
from jax import lax
from jax.experimental import pallas as pl
from jax.experimental.pallas import tpu as pltpu
from jax.sharding import PartitionSpec as P

MESH = pl.DeviceIdType.MESH
BF = jnp.bfloat16
F32 = jnp.float32
SLOTS = 16
NT = (((1,), (1,)), ((), ()))
TN = (((0,), (0,)), ((), ()))

TAB, SLICE, TOKX, TOKP, WPART, XP, PRE, ACT, ACTP, BACK, GRAD_IN, GRAD_OUT, SHP, SHARED, FINAL = range(15)
WX, WF, DISP, PAIR, HALF = 15, 17, 19, 23, 27
COUNT = 31


def dot(left, right, dims=None):
    dims = dims or (((1,), (0,)), ((), ()))
    return lax.dot_general(left, right, dims, preferred_element_type=F32)


def silu_parts(preact):
    sig_value = jax.nn.sigmoid(preact)
    return preact * sig_value, sig_value * (1.0 + preact * (1.0 - sig_value))


def kernel(
    topk,
    tok_ref, cot_ref, routes_ref, gates_ref, w_in, w_out, sh_in, sh_out,
    out_ref, gtok_ref, gin_ref, gout_ref,
    pair, table, tabs, gs, g, wt, sw_in, sw_out, t2, snd, xr, xp, pf, pb, rs, act, actp, ps, pr, po, ret, bk, gb,
    shs, shp, shr, fs, fr, ssem, rsem, lsem,
):
    ne, nt = lax.axis_size("expert"), lax.axis_size("tensor")
    e, t = lax.axis_index("expert"), lax.axis_index("tensor")
    chip, core = t // 2, t % 2
    chips = nt // 2
    a, q = chip // 2, chip % 2
    partner = t + 1 - 2 * core
    row_chip = 2 * a + 1 - q
    weight_chip = chips - 1 - chip
    row_dev, weight_dev = (e, 2 * row_chip + core), (e, 2 * weight_chip + core)
    first = (e * chips) // ne
    stays = e % 2 == core
    d8 = gs.shape[1]
    hid = w_out.shape[0]
    half = 4 * hid
    gl_count = ne // 2
    gq = gl_count // 4
    rows = 2 * gq * SLOTS
    m32 = 2 * SLOTS

    def rcopy(src, dst, which, dev):
        return pltpu.make_async_remote_copy(
            src_ref=src, dst_ref=dst, send_sem=ssem.at[which], recv_sem=rsem.at[which],
            device_id=dev, device_id_type=MESH,
        )

    def recv(ref, which):
        pltpu.make_async_copy(ref, ref, rsem.at[which]).wait()

    def sent(ref, which):
        pltpu.make_async_copy(ref, ref, ssem.at[which]).wait()

    def cols(piece):
        return pl.ds(pl.multiple_of(piece * d8, 128), d8)

    def block(index, size):
        return pl.ds(pl.multiple_of(index * size, 16), size)

    def source(m):
        return w_out if m == 2 else w_in.at[m]

    place = 2 * a + core
    own_shared = [
        pltpu.make_async_copy(sh_in, sw_in, lsem.at[0]),
        pltpu.make_async_copy(sh_out, sw_out, lsem.at[1]),
    ]
    own_weights = [
        pltpu.make_async_copy(
            source(m).at[:, cols(4 * a + 2 * n + h)], wt.at[n, h, m, block(place, hid)], lsem.at[2 + 6 * n + 3 * h + m])
        for n in range(2) for h in range(2) for m in range(3)]

    barrier = pltpu.get_barrier_semaphore()

    @pl.loop(1, nt)
    def _(k):
        pl.semaphore_signal(barrier, inc=1, device_id=(e, lax.rem(t + k, nt)), device_id_type=MESH)

    @pl.loop(1, ne)
    def _(k):
        for h in range(2):
            pl.semaphore_signal(barrier, inc=1, device_id=(lax.rem(e + k, ne), 2 * chip + h), device_id_type=MESH)

    for copy in own_weights + own_shared:
        copy.start()
    for n in range(nt):
        span = slice(n * d8, (n + 1) * d8)
        pair[:, span] = jnp.concatenate(
            [tok_ref[:, span].astype(F32), cot_ref[:, span].astype(F32)], axis=0).astype(BF)
    table[...] = jnp.zeros_like(table)
    for n in range(2):
        table[8 * n:8 * n + 8, :topk] = routes_ref[...]
        table[8 * n:8 * n + 8, topk:2 * topk] = gates_ref[...]

    pl.semaphore_wait(barrier, 2 * (ne - 1) + nt - 1)

    @pl.loop(1, nt)
    def _(k):
        p = lax.rem(t + k, nt)
        rcopy(table, tabs.at[block(t, 16)], TAB, (e, p)).start()
        rcopy(pair.at[:, cols(p)], gs.at[block(t, 16)], SLICE, (e, p)).start()

    @pl.loop(1, chips)
    def _(k):
        rcopy(pair, g.at[block(t, 16)], TOKX, (e, lax.rem(t + 2 * k, nt))).start()

    rcopy(pair, g.at[block(t, 16)], TOKP, (e, partner)).start()
    for n in range(2):
        there = n * q + (1 - n) * (1 - q)
        for h in range(2):
            for m in range(3):
                rcopy(source(m).at[:, cols(4 * (1 - a) + 2 * there + h)], wt.at[there, h, m, block(place, hid)],
                      WX + n, weight_dev).start()
    for n in range(2):
        for h in range(2):
            for m in range(3):
                rcopy(source(m).at[:, cols(4 * a + 2 * n + h)], wt.at[n, h, m, block(place, hid)],
                      WPART, (e, partner)).start()

    tabs[block(t, 16), :] = table[...]
    gs[block(t, 16), :] = pair[:, cols(t)]
    g[block(t, 16), :] = pair[...]

    recv(tabs.at[pl.ds(0, (nt - 1) * 16)], TAB)
    lanes = nt * 16
    chosen = tabs[...].astype(F32).T
    lane_a = lax.broadcasted_iota(jnp.int32, (lanes, lanes), 0)
    lane_b = lax.broadcasted_iota(jnp.int32, (lanes, lanes), 1)
    token_a, token_b = (lane_a // 16) * 8 + lane_a % 8, (lane_b // 16) * 8 + lane_b % 8
    earlier = jnp.where((lane_a % 16 < 8) & (token_a < token_b), 1.0, 0.0).astype(BF)
    recv(gs.at[pl.ds(0, (nt - 1) * 16)], SLICE)
    tokens_here = gs[...]
    ec = ne // 4
    size = ec * m32
    for turn in range(4):
        chunk = lax.rem(first + turn, 4)
        row = lax.broadcasted_iota(jnp.int32, (size, lanes), 0)
        lane = lax.broadcasted_iota(jnp.int32, (size, lanes), 1)
        kind, slot = (row // SLOTS) % 2, (row % SLOTS).astype(F32)
        expert = (row // m32 + chunk * ec).astype(F32)
        named = jnp.zeros((size, lanes), F32)
        gate = jnp.zeros((size, lanes), F32)
        for k in range(topk):
            hit = chosen[k:k + 1, :] == expert
            named = jnp.where(hit, 1.0, named)
            gate = jnp.where(hit, chosen[topk + k:topk + k + 1, :] * (1.0 / 64.0), gate)
        rank = dot(named.astype(BF), earlier)
        here = jnp.where((rank == slot) & ((lane // 8) % 2 == kind), named, 0.0)
        weighted = jnp.where(kind == 1, here * gate, here).astype(BF)
        t2[block(chunk, size), :] = jnp.where(kind == 1, here, here * gate).astype(BF)
        snd[pl.ds(chunk * ec, ec)] = dot(weighted, tokens_here).astype(BF).reshape(ec, m32, d8)

        @pl.loop(0, ec)
        def _(n):
            p = chunk * ec + n
            target = xr.at[q, core, e // 2]

            @pl.when(jnp.logical_and(p == e, stays))
            def _():
                pltpu.make_async_copy(snd.at[p], target, rsem.at[DISP + first]).start()

            @pl.when(jnp.logical_not(jnp.logical_and(p == e, stays)))
            def _():
                rcopy(snd.at[p], target, DISP + first, (p, 2 * chip + e % 2)).start()

    def pass_rows(k):
        chunk = lax.rem(first + 4 - k, 4)
        part = xr.at[q, :, pl.ds(chunk * gq, gq)]
        recv(part, DISP + chunk)
        rcopy(part, part, PAIR + k, row_dev).start()

    def pass_weights(n):
        there = n * (1 - q) + (1 - n) * q
        part = wt.at[there, :, :, block(2 * (1 - a) + core, hid)]
        recv(part, WX + n)
        rcopy(part, part, WF + n, (e, partner)).start()

    recv(g.at[pl.ds(0, (chips - 1) * 16)], TOKX)

    @pl.loop(1, chips)
    def _(k):
        part = g.at[block(lax.rem(t + 2 * k, nt), 16)]
        rcopy(part, part, TOKP, (e, partner)).start()

    pass_rows(0)
    recv(g.at[pl.ds(0, chips * 16)], TOKP)
    for copy in own_shared:
        copy.wait()
    sh = sw_out.shape[0]

    def shared_step(n, sums):
        piece = g[:, cols(n)]
        return tuple(
            total + dot(piece, weight[:, cols(n)], NT)
            for total, weight in zip(sums, (sw_in.at[0], sw_in.at[1], sw_out)))

    zero = jnp.zeros((nt * 16, sh), F32)
    sums = lax.fori_loop(0, nt, shared_step, (zero, zero, zero))
    pass_rows(1)
    s_gate, s_up = [v.reshape(nt, 16, sh)[:, :8].reshape(nt * 8, sh) for v in sums[:2]]
    s_back = sums[2].reshape(nt, 16, sh)[:, 8:].reshape(nt * 8, sh)
    s_act, s_slope = silu_parts(s_gate)
    s_hidden = (s_act * s_up).astype(BF)
    s_dgate = (s_back * s_up * s_slope).astype(BF)
    s_dup = (s_back * s_act).astype(BF)

    def shared_terms(low, high):
        @pl.loop(low, high)
        def _(n):
            y = dot(s_hidden, sw_out[:, cols(n)]).reshape(nt, 8, d8)
            dx = (dot(s_dgate, sw_in[0, :, cols(n)]) + dot(s_dup, sw_in[1, :, cols(n)])).reshape(nt, 8, d8)
            shs[:, :, :, cols(n)] = jnp.concatenate([y, dx], axis=1).astype(BF).reshape(chips, 2, 16, d8)

    shared_terms(0, nt // 2)
    pass_weights(0)
    pass_rows(2)
    shared_terms(nt // 2, nt)
    rcopy(shs.at[:, 1 - core], shp, SHP, (e, partner)).start()
    pass_rows(3)
    pass_weights(1)

    def products(quarter, n):
        value = [None] * 3
        for h in range(2):
            part = xr[quarter, h, pl.ds(n * 2 * gq, 2 * gq)]
            x_rows = part[:, :SLOTS].reshape(rows, d8)
            dy_rows = part[:, SLOTS:].reshape(rows, d8)
            for m in range(3):
                term = dot(dy_rows if m == 2 else x_rows, wt[quarter, h, m], NT)
                value[m] = term if h == 0 else value[m] + term
        return value

    for copy in own_weights:
        copy.wait()
    recv(wt.at[:, :, :, pl.ds(0, hid)], WPART)
    recv(wt.at[0, :, :, pl.ds(0, hid)], WF)

    @pl.loop(0, 2)
    def _(n):
        for m, value in enumerate(products(q, n)):
            pf[n, :, m * half:(m + 1) * half] = value

    recv(shp, SHP)
    for n in range(chips):
        shs[n, core] = (shs[n, core].astype(F32) + shp[n].astype(F32)).astype(BF)

    recv(wt.at[0, :, :, pl.ds(0, hid)], WF + 1)
    for k in range(4):
        recv(xr.at[0, :, pl.ds(0, gq)], PAIR + k)

    def finish(n):
        for m, value in enumerate(products(1 - q, n)):
            span = slice(m * half, (m + 1) * half)
            pf[n, :, span] = pf[n, :, span] + value

    finish(1 - a)
    pb[...] = pf[1 - a].astype(BF)
    rcopy(pb, rs, PRE, weight_dev).start()
    rcopy(xr.at[:, 1 - core], xp, XP, (e, partner)).start()

    @pl.loop(1, chips)
    def _(k):
        j = lax.rem(chip + k, chips)
        rcopy(shs.at[j, core], shr.at[chip], SHARED, (e, 2 * j + core)).start()

    finish(a)
    recv(rs, PRE)
    total = pf[a] + rs[...].astype(F32)
    gate_pre, up_pre, back = total[:, :half], total[:, half:2 * half], total[:, 2 * half:]
    active, slope = silu_parts(gate_pre)
    act[a, :, :half] = (active * up_pre).astype(BF)
    act[a, :, half:2 * half] = (back * up_pre * slope).astype(BF)
    act[a, :, 2 * half:] = (back * active).astype(BF)
    rcopy(act.at[a], act.at[a], ACT, weight_dev).start()
    recv(act.at[1 - a], ACT)
    rcopy(act, actp, ACTP, (e, partner)).start()

    def results(quarter, h, n):
        y = dot(act[n, :, :half], wt[quarter, h, 2])
        dx = dot(act[n, :, half:], wt[quarter, h, 0:2].reshape(2 * half, d8))
        return jnp.concatenate([y.reshape(2 * gq, SLOTS, d8), dx.reshape(2 * gq, SLOTS, d8)], axis=1)

    def order(k):
        n = lax.rem(first // 2 + k // 2, 2)
        return 2 * n + lax.rem(first + k, 2)

    for k in range(2):
        n = lax.rem(first // 2 + k, 2)
        for h in range(2):
            ps[h, pl.ds(n * 2 * gq, 2 * gq)] = results(1 - q, h, n).astype(BF)
        for i in range(2):
            part = pl.ds(order(2 * k + i) * gq, gq)
            rcopy(ps.at[:, part], pr.at[:, part], HALF + 2 * k + i, row_dev).start()

    @pl.loop(0, 2)
    def _(n):
        for h in range(2):
            po[h, pl.ds(n * 2 * gq, 2 * gq)] = results(q, h, n)

    recv(xp, XP)
    recv(actp, ACTP)
    own_grads = []

    def gradient(n, m):
        span = slice(0, half) if m == 2 else slice((m + 1) * half, (m + 2) * half)
        kind = slice(SLOTS, m32) if m == 2 else slice(0, SLOTS)
        here = act[:, :, span].reshape(2 * rows, half)
        there = actp[:, :, span].reshape(2 * rows, half)
        x_here = xr[n, core, :, kind].reshape(2 * rows, d8)
        x_there = xp[n, :, kind].reshape(2 * rows, d8)
        gb[n, m] = (dot(here, x_here, TN) + dot(there, x_there, TN)).astype(BF)
        target = (gout_ref if m == 2 else gin_ref.at[m]).at[:, cols(4 * a + 2 * n + core)]
        which = GRAD_OUT if m == 2 else GRAD_IN
        for c in range(2):
            rcopy(gb.at[n, m, block(2 * (1 - a) + c, hid)], target, which, (e, 2 * weight_chip + c)).start()
        rcopy(gb.at[n, m, block(2 * a + 1 - core, hid)], target, which, (e, partner)).start()
        own = pltpu.make_async_copy(gb.at[n, m, block(place, hid)], target, lsem.at[2 + 3 * n + m])
        own.start()
        own_grads.append(own)

    def give_back(k):
        chunk = order(k)
        part = pl.ds(chunk * gq, gq)
        recv(pr.at[:, part], HALF + k)
        ret[:, part] = (po[:, part] + pr[:, part].astype(F32)).astype(BF)

        @pl.loop(0, gq)
        def _(n):
            place_here = chunk * gq + n
            p = 2 * place_here + core
            for h in range(2):
                local = jnp.logical_and(p == e, core == h)

                @pl.when(local)
                def _():
                    pltpu.make_async_copy(ret.at[h, place_here], bk.at[e], rsem.at[BACK]).start()

                @pl.when(jnp.logical_not(local))
                def _():
                    rcopy(ret.at[h, place_here], bk.at[e], BACK, (p, 2 * chip + h)).start()

    for m in range(3):
        gradient(0, m)
    give_back(0)
    gradient(1, 0)
    gradient(1, 1)
    give_back(1)
    gradient(1, 2)
    give_back(2)
    give_back(3)

    recv(bk, BACK)
    routed = dot(t2[...], bk[...].reshape(ne * m32, d8), TN)
    fs[...] = routed.astype(BF).reshape(nt, 16, d8)

    @pl.loop(1, nt)
    def _(k):
        p = lax.rem(t + k, nt)
        rcopy(fs.at[p], fr.at[t], FINAL, (e, p)).start()

    fr[t] = fs[t]
    shr[chip] = shs[chip, core]
    recv(shr.at[pl.ds(0, chips - 1)], SHARED)
    recv(fr.at[pl.ds(0, nt - 1)], FINAL)

    for n in range(nt):
        span = slice(n * d8, (n + 1) * d8)
        total = fr[n].astype(F32) + jnp.sum(shr[:, :, span].astype(F32), axis=0)
        out_ref[:, span] = total[:8].astype(BF)
        gtok_ref[:, span] = total[8:].astype(BF)

    recv(gin_ref.at[:, :, pl.ds(0, 6 * d8)], GRAD_IN)
    recv(gout_ref.at[:, pl.ds(0, 6 * d8)], GRAD_OUT)
    for copy in own_grads:
        copy.wait()
    sent(tabs.at[pl.ds(0, (nt - 1) * 16)], TAB)
    sent(gs.at[pl.ds(0, (nt - 1) * 16)], SLICE)
    sent(g.at[pl.ds(0, (chips - 1) * 16)], TOKX)
    sent(g.at[pl.ds(0, chips * 16)], TOKP)
    sent(wt.at[:, :, :, pl.ds(0, hid)], WPART)
    for n in range(2):
        sent(wt.at[n, :, :, pl.ds(0, hid)], WX + n)
        sent(wt.at[n, :, :, pl.ds(0, hid)], WF + n)
    for k in range(4):
        sent(xr.at[0, :, pl.ds(0, gq)], PAIR + k)
        sent(ps.at[:, pl.ds(0, gq)], HALF + k)
    sent(xp, XP)
    sent(rs, PRE)
    sent(act.at[0], ACT)
    sent(actp, ACTP)
    sent(shp, SHP)
    sent(shr.at[pl.ds(0, chips - 1)], SHARED)
    sent(gin_ref.at[:, :, pl.ds(0, 6 * d8)], GRAD_IN)
    sent(gout_ref.at[:, pl.ds(0, 6 * d8)], GRAD_OUT)
    sent(fs.at[pl.ds(0, nt - 1)], FINAL)

    @pl.when(stays)
    def _():
        sent(bk.at[pl.ds(0, ne - 1)], BACK)
        sent(bk.at[pl.ds(0, ne - 1)], DISP + first)

    @pl.when(jnp.logical_not(stays))
    def _():
        sent(bk, BACK)
        sent(bk, DISP + first)


def on_device(tokens, routes, gate_num, cotangent, w_in, w_out, shared_in, shared_out):
    ne, nt = lax.axis_size("expert"), lax.axis_size("tensor")
    chips = nt // 2
    own, features = tokens.shape
    topk = routes.shape[1]
    hid, sh = w_out.shape[1], shared_out.shape[0]
    d8, half, gl_count = features // nt, 4 * hid, ne // 2
    rows, m32 = gl_count * SLOTS // 2, 2 * SLOTS
    vm = pl.BlockSpec(memory_space=pltpu.VMEM)
    hbm = pl.BlockSpec(memory_space=pl.ANY)
    scratch = [
        pltpu.VMEM((16, features), BF),
        pltpu.VMEM((16, 128), jnp.int32),
        pltpu.VMEM((nt * 16, 128), jnp.int32),
        pltpu.VMEM((nt * 16, d8), BF),
        pltpu.VMEM((nt * 16, features), BF),
        pltpu.VMEM((2, 2, 3, half, d8), BF),
        pltpu.VMEM((2, sh, features), BF),
        pltpu.VMEM((sh, features), BF),
        pltpu.VMEM((ne * m32, nt * 16), BF),
        pltpu.VMEM((ne, m32, d8), BF),
        pltpu.VMEM((2, 2, gl_count, m32, d8), BF),
        pltpu.VMEM((2, gl_count, m32, d8), BF),
        pltpu.VMEM((2, rows, 3 * half), F32),
        pltpu.VMEM((rows, 3 * half), BF),
        pltpu.VMEM((rows, 3 * half), BF),
        pltpu.VMEM((2, rows, 3 * half), BF),
        pltpu.VMEM((2, rows, 3 * half), BF),
        pltpu.VMEM((2, gl_count, m32, d8), BF),
        pltpu.VMEM((2, gl_count, m32, d8), BF),
        pltpu.VMEM((2, gl_count, m32, d8), F32),
        pltpu.VMEM((2, gl_count, m32, d8), BF),
        pltpu.VMEM((ne, m32, d8), BF),
        pltpu.VMEM((2, 3, half, d8), BF),
        pltpu.VMEM((chips, 2, 16, features), BF),
        pltpu.VMEM((chips, 16, features), BF),
        pltpu.VMEM((chips, 16, features), BF),
        pltpu.VMEM((nt, 16, d8), BF),
        pltpu.VMEM((nt, 16, d8), BF),
        pltpu.SemaphoreType.DMA((COUNT,)),
        pltpu.SemaphoreType.DMA((COUNT,)),
        pltpu.SemaphoreType.DMA((14,)),
    ]
    shapes = (
        jax.ShapeDtypeStruct((own, features), BF),
        jax.ShapeDtypeStruct((own, features), BF),
        jax.ShapeDtypeStruct((2, hid, features), BF),
        jax.ShapeDtypeStruct((hid, features), BF),
    )
    results = pl.pallas_call(
        functools.partial(kernel, topk),
        out_shape=shapes,
        in_specs=[vm, vm, vm, vm, hbm, hbm, hbm, hbm],
        out_specs=(vm, vm, hbm, hbm),
        scratch_shapes=scratch,
        compiler_params=pltpu.CompilerParams(
            collective_id=0, has_side_effects=True, vmem_limit_bytes=56 * 2**20
        ),
    )(tokens, cotangent, routes, gate_num, w_in[0], w_out[0], shared_in, shared_out)
    out, gtok, gin, gout = results
    return out, gtok, gin[None], gout[None]


def solution(mesh):
    in_specs = (
        P(("expert", "tensor"), None),
        P(("expert", "tensor"), None),
        P(("expert", "tensor"), None),
        P(("expert", "tensor"), None),
        P("expert", None, "tensor", None),
        P("expert", "tensor", None),
        P(None, "tensor", None),
        P("tensor", None),
    )
    out_specs = (
        P(("expert", "tensor"), None),
        P(("expert", "tensor"), None),
        P("expert", None, "tensor", None),
        P("expert", "tensor", None),
    )
    return jax.shard_map(
        on_device, mesh=mesh, in_specs=in_specs, out_specs=out_specs, check_vma=False
    )
```

```python
import functools

import jax
import jax.numpy as jnp
from jax import lax
from jax.experimental import pallas as pl
from jax.experimental.pallas import tpu as pltpu
from jax.sharding import PartitionSpec as P

MESH = pl.DeviceIdType.MESH
BF = jnp.bfloat16
F32 = jnp.float32
SLOTS = 16
NT = (((1,), (1,)), ((), ()))
TN = (((0,), (0,)), ((), ()))

TAB, SLICE, TOKX, TOKP, WPART, XP, ACTP, BACK, GRAD_IN, GRAD_OUT, SHP, SHARED, FINAL = range(13)
PRE, ACT, WX, WF, DISP, PAIR, HALF = 13, 15, 17, 19, 21, 25, 29
COUNT = 33


def dot(left, right, dims=None):
    dims = dims or (((1,), (0,)), ((), ()))
    return lax.dot_general(left, right, dims, preferred_element_type=F32)


def silu_parts(preact):
    sig_value = jax.nn.sigmoid(preact)
    return preact * sig_value, sig_value * (1.0 + preact * (1.0 - sig_value))


def kernel(
    topk,
    tok_ref, cot_ref, routes_ref, gates_ref, w_in, w_out, sh_in, sh_out,
    out_ref, gtok_ref, gin_ref, gout_ref,
    pair, table, tabs, gs, g, wt, sw_in, sw_out, t2, snd, xr, xp, pf, pb, rs, act, actp, ps, pr, po, ret, bk, gb,
    shs, shp, shr, fs, fr, ssem, rsem, lsem,
):
    ne, nt = lax.axis_size("expert"), lax.axis_size("tensor")
    e, t = lax.axis_index("expert"), lax.axis_index("tensor")
    chip, core = t // 2, t % 2
    chips = nt // 2
    a, q = chip // 2, chip % 2
    partner = t + 1 - 2 * core
    row_chip = 2 * a + 1 - q
    weight_chip = chips - 1 - chip
    row_dev, weight_dev = (e, 2 * row_chip + core), (e, 2 * weight_chip + core)
    first = e % 4
    stays = (e // 4) % 2 == core
    home = (e % 4) * (ne // 4) + e // 4
    local_group = (e % 4) * (ne // 8) + e // 8
    d8 = gs.shape[1]
    hid = w_out.shape[0]
    half = 4 * hid
    gl_count = ne // 2
    gq = gl_count // 4
    rows = 2 * gq * SLOTS
    m32 = 2 * SLOTS

    def rcopy(src, dst, which, dev):
        return pltpu.make_async_remote_copy(
            src_ref=src, dst_ref=dst, send_sem=ssem.at[which], recv_sem=rsem.at[which],
            device_id=dev, device_id_type=MESH,
        )

    def recv(ref, which):
        pltpu.make_async_copy(ref, ref, rsem.at[which]).wait()

    def sent(ref, which):
        pltpu.make_async_copy(ref, ref, ssem.at[which]).wait()

    def cols(piece):
        return pl.ds(pl.multiple_of(piece * d8, 128), d8)

    def block(index, size):
        return pl.ds(pl.multiple_of(index * size, 16), size)

    def source(m):
        return w_out if m == 2 else w_in.at[m]

    place = 2 * a + core
    own_shared = [
        pltpu.make_async_copy(sh_in, sw_in, lsem.at[0]),
        pltpu.make_async_copy(sh_out, sw_out, lsem.at[1]),
    ]
    own_weights = [
        pltpu.make_async_copy(
            source(m).at[:, cols(4 * a + 2 * n + h)], wt.at[n, h, m, block(place, hid)], lsem.at[2 + 6 * n + 3 * h + m])
        for n in range(2) for h in range(2) for m in range(3)]

    barrier = pltpu.get_barrier_semaphore()

    @pl.loop(1, nt)
    def _(k):
        pl.semaphore_signal(barrier, inc=1, device_id=(e, lax.rem(t + k, nt)), device_id_type=MESH)

    @pl.loop(1, ne)
    def _(k):
        for h in range(2):
            pl.semaphore_signal(barrier, inc=1, device_id=(lax.rem(e + k, ne), 2 * chip + h), device_id_type=MESH)

    for copy in own_weights + own_shared:
        copy.start()
    for n in range(nt):
        span = slice(n * d8, (n + 1) * d8)
        pair[:, span] = jnp.concatenate(
            [tok_ref[:, span].astype(F32), cot_ref[:, span].astype(F32)], axis=0).astype(BF)
    table[...] = jnp.zeros_like(table)
    for n in range(2):
        table[8 * n:8 * n + 8, :topk] = routes_ref[...]
        table[8 * n:8 * n + 8, topk:2 * topk] = gates_ref[...]

    pl.semaphore_wait(barrier, 2 * (ne - 1) + nt - 1)

    @pl.loop(1, nt)
    def _(k):
        p = lax.rem(t + k, nt)
        rcopy(table, tabs.at[block(t, 16)], TAB, (e, p)).start()
        rcopy(pair.at[:, cols(p)], gs.at[block(t, 16)], SLICE, (e, p)).start()

    @pl.loop(1, chips)
    def _(k):
        rcopy(pair, g.at[block(t, 16)], TOKX, (e, lax.rem(t + 2 * k, nt))).start()

    rcopy(pair, g.at[block(t, 16)], TOKP, (e, partner)).start()
    for n in range(2):
        there = n * q + (1 - n) * (1 - q)
        for h in range(2):
            for m in range(3):
                rcopy(source(m).at[:, cols(4 * (1 - a) + 2 * there + h)], wt.at[there, h, m, block(place, hid)],
                      WX + n, weight_dev).start()
    for n in range(2):
        for h in range(2):
            for m in range(3):
                rcopy(source(m).at[:, cols(4 * a + 2 * n + h)], wt.at[n, h, m, block(place, hid)],
                      WPART, (e, partner)).start()

    tabs[block(t, 16), :] = table[...]
    gs[block(t, 16), :] = pair[:, cols(t)]
    g[block(t, 16), :] = pair[...]

    recv(tabs.at[pl.ds(0, (nt - 1) * 16)], TAB)
    lanes = nt * 16
    chosen = tabs[...].astype(F32).T
    lane_a = lax.broadcasted_iota(jnp.int32, (lanes, lanes), 0)
    lane_b = lax.broadcasted_iota(jnp.int32, (lanes, lanes), 1)
    token_a, token_b = (lane_a // 16) * 8 + lane_a % 8, (lane_b // 16) * 8 + lane_b % 8
    earlier = jnp.where((lane_a % 16 < 8) & (token_a < token_b), 1.0, 0.0).astype(BF)
    recv(gs.at[pl.ds(0, (nt - 1) * 16)], SLICE)
    tokens_here = gs[...]
    ec = ne // 4
    size = ec * m32
    for turn in range(4):
        chunk = lax.rem(first + turn, 4)
        row = lax.broadcasted_iota(jnp.int32, (size, lanes), 0)
        lane = lax.broadcasted_iota(jnp.int32, (size, lanes), 1)
        kind, slot = (row // SLOTS) % 2, (row % SLOTS).astype(F32)
        expert = (row // m32 * 4 + chunk).astype(F32)
        named = jnp.zeros((size, lanes), F32)
        gate = jnp.zeros((size, lanes), F32)
        for k in range(topk):
            hit = chosen[k:k + 1, :] == expert
            named = jnp.where(hit, 1.0, named)
            gate = jnp.where(hit, chosen[topk + k:topk + k + 1, :] * (1.0 / 64.0), gate)
        rank = dot(named.astype(BF), earlier)
        here = jnp.where((rank == slot) & ((lane // 8) % 2 == kind), named, 0.0)
        weighted = jnp.where(kind == 1, here * gate, here).astype(BF)
        t2[block(chunk, size), :] = jnp.where(kind == 1, here, here * gate).astype(BF)
        snd[pl.ds(chunk * ec, ec)] = dot(weighted, tokens_here).astype(BF).reshape(ec, m32, d8)

        @pl.loop(0, ec)
        def _(n):
            p = n * 4 + chunk
            from_here = snd.at[chunk * ec + n]
            target = xr.at[q, core, local_group]

            @pl.when(jnp.logical_and(p == e, stays))
            def _():
                pltpu.make_async_copy(from_here, target, rsem.at[DISP + first]).start()

            @pl.when(jnp.logical_not(jnp.logical_and(p == e, stays)))
            def _():
                rcopy(from_here, target, DISP + first, (p, 2 * chip + (e // 4) % 2)).start()

    def pass_rows(k):
        chunk = lax.rem(first + 4 - k, 4)
        part = xr.at[q, :, pl.ds(chunk * gq, gq)]
        recv(part, DISP + chunk)
        rcopy(part, part, PAIR + k, row_dev).start()

    def pass_weights(n):
        there = n * (1 - q) + (1 - n) * q
        part = wt.at[there, :, :, block(2 * (1 - a) + core, hid)]
        recv(part, WX + n)
        rcopy(part, part, WF + n, (e, partner)).start()

    recv(g.at[pl.ds(0, (chips - 1) * 16)], TOKX)

    @pl.loop(1, chips)
    def _(k):
        part = g.at[block(lax.rem(t + 2 * k, nt), 16)]
        rcopy(part, part, TOKP, (e, partner)).start()

    pass_rows(0)
    recv(g.at[pl.ds(0, chips * 16)], TOKP)
    for copy in own_shared:
        copy.wait()
    sh = sw_out.shape[0]

    def shared_step(n, sums):
        piece = g[:, cols(n)]
        return tuple(
            total + dot(piece, weight[:, cols(n)], NT)
            for total, weight in zip(sums, (sw_in.at[0], sw_in.at[1], sw_out)))

    zero = jnp.zeros((nt * 16, sh), F32)
    sums = lax.fori_loop(0, nt, shared_step, (zero, zero, zero))
    pass_rows(1)
    s_gate, s_up = [v.reshape(nt, 16, sh)[:, :8].reshape(nt * 8, sh) for v in sums[:2]]
    s_back = sums[2].reshape(nt, 16, sh)[:, 8:].reshape(nt * 8, sh)
    s_act, s_slope = silu_parts(s_gate)
    s_hidden = (s_act * s_up).astype(BF)
    s_dgate = (s_back * s_up * s_slope).astype(BF)
    s_dup = (s_back * s_act).astype(BF)

    def shared_terms(low, high):
        @pl.loop(low, high)
        def _(n):
            y = dot(s_hidden, sw_out[:, cols(n)]).reshape(nt, 8, d8)
            dx = (dot(s_dgate, sw_in[0, :, cols(n)]) + dot(s_dup, sw_in[1, :, cols(n)])).reshape(nt, 8, d8)
            shs[:, :, :, cols(n)] = jnp.concatenate([y, dx], axis=1).astype(BF).reshape(chips, 2, 16, d8)

    shared_terms(0, nt // 2)
    pass_weights(0)
    pass_rows(2)
    shared_terms(nt // 2, nt)
    rcopy(shs.at[:, 1 - core], shp, SHP, (e, partner)).start()
    pass_rows(3)
    pass_weights(1)

    def products(quarter, n):
        value = [None] * 3
        for h in range(2):
            part = xr[quarter, h, pl.ds(n * 2 * gq, 2 * gq)]
            x_rows = part[:, :SLOTS].reshape(rows, d8)
            dy_rows = part[:, SLOTS:].reshape(rows, d8)
            for m in range(3):
                term = dot(dy_rows if m == 2 else x_rows, wt[quarter, h, m], NT)
                value[m] = term if h == 0 else value[m] + term
        return value

    for copy in own_weights:
        copy.wait()
    recv(wt.at[:, :, :, pl.ds(0, hid)], WPART)
    recv(wt.at[0, :, :, pl.ds(0, hid)], WF)

    @pl.loop(0, 2)
    def _(n):
        for m, value in enumerate(products(q, n)):
            pf[n, :, m * half:(m + 1) * half] = value

    recv(shp, SHP)
    for n in range(chips):
        shs[n, core] = (shs[n, core].astype(F32) + shp[n].astype(F32)).astype(BF)

    for j in (weight_chip, lax.rem(chip + 2, chips)):
        rcopy(shs.at[j, core], shr.at[chip], SHARED, (e, 2 * j + core)).start()
    recv(wt.at[0, :, :, pl.ds(0, hid)], WF + 1)
    for k in range(4):
        recv(xr.at[0, :, pl.ds(0, gq)], PAIR + k)

    def finish(n):
        for m, value in enumerate(products(1 - q, n)):
            span = slice(m * half, (m + 1) * half)
            pf[n, :, span] = pf[n, :, span] + value

    finish(1 - a)
    pb[...] = pf[1 - a].astype(BF)
    for i in range(2):
        part = pl.ds(i * (rows // 2), rows // 2)
        rcopy(pb.at[part], rs.at[part], PRE + i, weight_dev).start()
    rcopy(xr.at[:, 1 - core], xp, XP, (e, partner)).start()

    rcopy(shs.at[row_chip, core], shr.at[chip], SHARED, row_dev).start()
    finish(a)
    for i in range(2):
        part = pl.ds(i * (rows // 2), rows // 2)
        recv(rs.at[part], PRE + i)
        total = pf[a, part] + rs[part].astype(F32)
        gate_pre, up_pre, back = total[:, :half], total[:, half:2 * half], total[:, 2 * half:]
        active, slope = silu_parts(gate_pre)
        act[a, part, :half] = (active * up_pre).astype(BF)
        act[a, part, half:2 * half] = (back * up_pre * slope).astype(BF)
        act[a, part, 2 * half:] = (back * active).astype(BF)
        rcopy(act.at[a, part], act.at[a, part], ACT + i, weight_dev).start()
    for i in range(2):
        recv(act.at[1 - a, pl.ds(i * (rows // 2), rows // 2)], ACT + i)
    rcopy(act, actp, ACTP, (e, partner)).start()

    def results(quarter, h, n):
        y = dot(act[n, :, :half], wt[quarter, h, 2])
        dx = dot(act[n, :, half:], wt[quarter, h, 0:2].reshape(2 * half, d8))
        return jnp.concatenate([y.reshape(2 * gq, SLOTS, d8), dx.reshape(2 * gq, SLOTS, d8)], axis=1)

    def order(k):
        n = lax.rem(first // 2 + k // 2, 2)
        return 2 * n + lax.rem(first + k, 2)

    for k in range(2):
        n = lax.rem(first // 2 + k, 2)
        for h in range(2):
            ps[h, pl.ds(n * 2 * gq, 2 * gq)] = results(1 - q, h, n).astype(BF)
        for i in range(2):
            part = pl.ds(order(2 * k + i) * gq, gq)
            rcopy(ps.at[:, part], pr.at[:, part], HALF + 2 * k + i, row_dev).start()

    @pl.loop(0, 2)
    def _(n):
        for h in range(2):
            po[h, pl.ds(n * 2 * gq, 2 * gq)] = results(q, h, n)

    recv(xp, XP)
    recv(actp, ACTP)
    own_grads = []

    def gradient(n, m):
        span = slice(0, half) if m == 2 else slice((m + 1) * half, (m + 2) * half)
        kind = slice(SLOTS, m32) if m == 2 else slice(0, SLOTS)
        here = act[:, :, span].reshape(2 * rows, half)
        there = actp[:, :, span].reshape(2 * rows, half)
        x_here = xr[n, core, :, kind].reshape(2 * rows, d8)
        x_there = xp[n, :, kind].reshape(2 * rows, d8)
        gb[n, m] = (dot(here, x_here, TN) + dot(there, x_there, TN)).astype(BF)
        target = (gout_ref if m == 2 else gin_ref.at[m]).at[:, cols(4 * a + 2 * n + core)]
        which = GRAD_OUT if m == 2 else GRAD_IN
        for c in range(2):
            rcopy(gb.at[n, m, block(2 * (1 - a) + c, hid)], target, which, (e, 2 * weight_chip + c)).start()
        rcopy(gb.at[n, m, block(2 * a + 1 - core, hid)], target, which, (e, partner)).start()
        own = pltpu.make_async_copy(gb.at[n, m, block(place, hid)], target, lsem.at[2 + 3 * n + m])
        own.start()
        own_grads.append(own)

    def give_back(k):
        chunk = order(k)
        part = pl.ds(chunk * gq, gq)
        recv(pr.at[:, part], HALF + k)
        ret[:, part] = (po[:, part] + pr[:, part].astype(F32)).astype(BF)

        @pl.loop(0, gq)
        def _(n):
            place_here = chunk * gq + n
            p = 4 * (2 * n + core) + chunk
            for h in range(2):
                local = jnp.logical_and(p == e, core == h)

                @pl.when(local)
                def _():
                    pltpu.make_async_copy(ret.at[h, place_here], bk.at[home], rsem.at[BACK]).start()

                @pl.when(jnp.logical_not(local))
                def _():
                    rcopy(ret.at[h, place_here], bk.at[home], BACK, (p, 2 * chip + h)).start()

    for m in range(3):
        gradient(0, m)
    give_back(0)
    gradient(1, 0)
    gradient(1, 1)
    give_back(1)
    gradient(1, 2)
    give_back(2)
    give_back(3)

    recv(bk, BACK)
    routed = dot(t2[...], bk[...].reshape(ne * m32, d8), TN)
    fs[...] = routed.astype(BF).reshape(nt, 16, d8)

    @pl.loop(1, nt)
    def _(k):
        p = lax.rem(t + k, nt)
        rcopy(fs.at[p], fr.at[t], FINAL, (e, p)).start()

    fr[t] = fs[t]
    shr[chip] = shs[chip, core]
    recv(shr.at[pl.ds(0, chips - 1)], SHARED)
    recv(fr.at[pl.ds(0, nt - 1)], FINAL)

    for n in range(nt):
        span = slice(n * d8, (n + 1) * d8)
        total = fr[n].astype(F32) + jnp.sum(shr[:, :, span].astype(F32), axis=0)
        out_ref[:, span] = total[:8].astype(BF)
        gtok_ref[:, span] = total[8:].astype(BF)

    recv(gin_ref.at[:, :, pl.ds(0, 6 * d8)], GRAD_IN)
    recv(gout_ref.at[:, pl.ds(0, 6 * d8)], GRAD_OUT)
    for copy in own_grads:
        copy.wait()
    sent(tabs.at[pl.ds(0, (nt - 1) * 16)], TAB)
    sent(gs.at[pl.ds(0, (nt - 1) * 16)], SLICE)
    sent(g.at[pl.ds(0, (chips - 1) * 16)], TOKX)
    sent(g.at[pl.ds(0, chips * 16)], TOKP)
    sent(wt.at[:, :, :, pl.ds(0, hid)], WPART)
    for n in range(2):
        sent(wt.at[n, :, :, pl.ds(0, hid)], WX + n)
        sent(wt.at[n, :, :, pl.ds(0, hid)], WF + n)
    for k in range(4):
        sent(xr.at[0, :, pl.ds(0, gq)], PAIR + k)
        sent(ps.at[:, pl.ds(0, gq)], HALF + k)
    sent(xp, XP)
    for i in range(2):
        sent(rs.at[pl.ds(0, rows // 2)], PRE + i)
        sent(rs.at[pl.ds(0, rows // 2)], ACT + i)
    sent(actp, ACTP)
    sent(shp, SHP)
    sent(shr.at[pl.ds(0, chips - 1)], SHARED)
    sent(gin_ref.at[:, :, pl.ds(0, 6 * d8)], GRAD_IN)
    sent(gout_ref.at[:, pl.ds(0, 6 * d8)], GRAD_OUT)
    sent(fs.at[pl.ds(0, nt - 1)], FINAL)

    @pl.when(stays)
    def _():
        sent(bk.at[pl.ds(0, ne - 1)], BACK)
        sent(bk.at[pl.ds(0, ne - 1)], DISP + first)

    @pl.when(jnp.logical_not(stays))
    def _():
        sent(bk, BACK)
        sent(bk, DISP + first)


def hand_over(*refs):
    count = len(refs) // 2
    sem = refs[-1]
    copies = []
    for n in range(count):
        source, target = refs[n], refs[count + n]
        if source.shape[0] == 2:
            pairs = [(source.at[m], target.at[m]) for m in range(2)]
        else:
            pairs = [(source, target)]
        for left, right in pairs:
            copies.append(pltpu.make_async_copy(left, right, sem.at[len(copies)]))
    for copy in copies:
        copy.start()
    for copy in copies:
        copy.wait()


def on_device(tokens, routes, gate_num, cotangent, w_in, w_out, shared_in, shared_out):
    ne, nt = lax.axis_size("expert"), lax.axis_size("tensor")
    chips = nt // 2
    own, features = tokens.shape
    topk = routes.shape[1]
    hid, sh = w_out.shape[1], shared_out.shape[0]
    d8, half, gl_count = features // nt, 4 * hid, ne // 2
    rows, m32 = gl_count * SLOTS // 2, 2 * SLOTS
    vm = pl.BlockSpec(memory_space=pltpu.VMEM)
    hbm = pl.BlockSpec(memory_space=pl.ANY)
    scratch = [
        pltpu.VMEM((16, features), BF),
        pltpu.VMEM((16, 128), jnp.int32),
        pltpu.VMEM((nt * 16, 128), jnp.int32),
        pltpu.VMEM((nt * 16, d8), BF),
        pltpu.VMEM((nt * 16, features), BF),
        pltpu.VMEM((2, 2, 3, half, d8), BF),
        pltpu.VMEM((2, sh, features), BF),
        pltpu.VMEM((sh, features), BF),
        pltpu.VMEM((ne * m32, nt * 16), BF),
        pltpu.VMEM((ne, m32, d8), BF),
        pltpu.VMEM((2, 2, gl_count, m32, d8), BF),
        pltpu.VMEM((2, gl_count, m32, d8), BF),
        pltpu.VMEM((2, rows, 3 * half), F32),
        pltpu.VMEM((rows, 3 * half), BF),
        pltpu.VMEM((rows, 3 * half), BF),
        pltpu.VMEM((2, rows, 3 * half), BF),
        pltpu.VMEM((2, rows, 3 * half), BF),
        pltpu.VMEM((2, gl_count, m32, d8), BF),
        pltpu.VMEM((2, gl_count, m32, d8), BF),
        pltpu.VMEM((2, gl_count, m32, d8), F32),
        pltpu.VMEM((2, gl_count, m32, d8), BF),
        pltpu.VMEM((ne, m32, d8), BF),
        pltpu.VMEM((2, 3, half, d8), BF),
        pltpu.VMEM((chips, 2, 16, features), BF),
        pltpu.VMEM((chips, 16, features), BF),
        pltpu.VMEM((chips, 16, features), BF),
        pltpu.VMEM((nt, 16, d8), BF),
        pltpu.VMEM((nt, 16, d8), BF),
        pltpu.SemaphoreType.DMA((COUNT,)),
        pltpu.SemaphoreType.DMA((COUNT,)),
        pltpu.SemaphoreType.DMA((14,)),
    ]
    shapes = (
        jax.ShapeDtypeStruct((own, features), BF),
        jax.ShapeDtypeStruct((own, features), BF),
        jax.ShapeDtypeStruct((2, hid, features), BF),
        jax.ShapeDtypeStruct((hid, features), BF),
    )
    results = pl.pallas_call(
        functools.partial(kernel, topk),
        out_shape=shapes,
        in_specs=[vm, vm, vm, vm, hbm, hbm, hbm, hbm],
        out_specs=(vm, vm, hbm, hbm),
        scratch_shapes=scratch,
        compiler_params=pltpu.CompilerParams(
            collective_id=0, has_side_effects=True, vmem_limit_bytes=56 * 2**20
        ),
    )(tokens, cotangent, routes, gate_num, w_in[0], w_out[0], shared_in, shared_out)
    out, gtok, gin, gout = pl.pallas_call(
        hand_over,
        out_shape=shapes,
        in_specs=[hbm] * 4,
        out_specs=(hbm,) * 4,
        scratch_shapes=[pltpu.SemaphoreType.DMA((5,))],
        compiler_params=pltpu.CompilerParams(vmem_limit_bytes=60 * 2**20),
    )(*results)
    return out, gtok, gin[None], gout[None]


def solution(mesh):
    in_specs = (
        P(("expert", "tensor"), None),
        P(("expert", "tensor"), None),
        P(("expert", "tensor"), None),
        P(("expert", "tensor"), None),
        P("expert", None, "tensor", None),
        P("expert", "tensor", None),
        P(None, "tensor", None),
        P("tensor", None),
    )
    out_specs = (
        P(("expert", "tensor"), None),
        P(("expert", "tensor"), None),
        P("expert", None, "tensor", None),
        P("expert", "tensor", None),
    )
    return jax.shard_map(
        on_device, mesh=mesh, in_specs=in_specs, out_specs=out_specs, check_vma=False
    )
```

```python
import functools

import jax
import jax.numpy as jnp
from jax import lax
from jax.experimental import pallas as pl
from jax.experimental.pallas import tpu as pltpu
from jax.sharding import PartitionSpec as P

MESH = pl.DeviceIdType.MESH
BF = jnp.bfloat16
F32 = jnp.float32
SLOTS = 16
NT = (((1,), (1,)), ((), ()))
TN = (((0,), (0,)), ((), ()))

TAB, SLICE, TOKX, TOKP, WPART, XP, ACTP, BACK, GRAD_IN, GRAD_OUT, SHP, SHARED, FINAL = range(13)
PRE, ACT, WX, WF, DISP, PAIR, HALF = 13, 15, 17, 19, 21, 25, 29
COUNT = 33


def dot(left, right, dims=None):
    dims = dims or (((1,), (0,)), ((), ()))
    return lax.dot_general(left, right, dims, preferred_element_type=F32)


def silu_parts(preact):
    sig_value = jax.nn.sigmoid(preact)
    return preact * sig_value, sig_value * (1.0 + preact * (1.0 - sig_value))


def kernel(
    topk,
    tok_ref, cot_ref, routes_ref, gates_ref, w_in, w_out, sh_in, sh_out,
    out_ref, gtok_ref, gin_ref, gout_ref,
    pair, table, tabs, gs, g, wt, sw_in, sw_out, t2, snd, xr, xp, pf, pb, rs, act, actp, ps, pr, po, ret, bk, gb,
    shs, shp, shr, fs, fr, ssem, rsem, lsem,
):
    ne, nt = lax.axis_size("expert"), lax.axis_size("tensor")
    e, t = lax.axis_index("expert"), lax.axis_index("tensor")
    chip, core = t // 2, t % 2
    chips = nt // 2
    a, q = chip // 2, chip % 2
    partner = t + 1 - 2 * core
    row_chip = 2 * a + 1 - q
    weight_chip = chips - 1 - chip
    row_dev, weight_dev = (e, 2 * row_chip + core), (e, 2 * weight_chip + core)
    first = e % 4
    stays = (e // 4) % 2 == core
    home = (e % 4) * (ne // 4) + e // 4
    local_group = (e % 4) * (ne // 8) + e // 8
    d8 = gs.shape[1]
    hid = w_out.shape[0]
    half = 4 * hid
    gl_count = ne // 2
    gq = gl_count // 4
    rows = 2 * gq * SLOTS
    m32 = 2 * SLOTS

    def rcopy(src, dst, which, dev):
        return pltpu.make_async_remote_copy(
            src_ref=src, dst_ref=dst, send_sem=ssem.at[which], recv_sem=rsem.at[which],
            device_id=dev, device_id_type=MESH,
        )

    def recv(ref, which):
        pltpu.make_async_copy(ref, ref, rsem.at[which]).wait()

    def sent(ref, which):
        pltpu.make_async_copy(ref, ref, ssem.at[which]).wait()

    def cols(piece):
        return pl.ds(pl.multiple_of(piece * d8, 128), d8)

    def block(index, size):
        return pl.ds(pl.multiple_of(index * size, 16), size)

    def source(m):
        return w_out if m == 2 else w_in.at[m]

    place = 2 * a + core
    own_shared = [
        pltpu.make_async_copy(sh_in, sw_in, lsem.at[0]),
        pltpu.make_async_copy(sh_out, sw_out, lsem.at[1]),
    ]
    own_weights = [
        pltpu.make_async_copy(
            source(m).at[:, cols(4 * a + 2 * n + h)], wt.at[n, h, m, block(place, hid)], lsem.at[2 + 6 * n + 3 * h + m])
        for n in range(2) for h in range(2) for m in range(3)]

    barrier = pltpu.get_barrier_semaphore()

    @pl.loop(1, nt)
    def _(k):
        pl.semaphore_signal(barrier, inc=1, device_id=(e, lax.rem(t + k, nt)), device_id_type=MESH)

    @pl.loop(1, ne)
    def _(k):
        for h in range(2):
            pl.semaphore_signal(barrier, inc=1, device_id=(lax.rem(e + k, ne), 2 * chip + h), device_id_type=MESH)

    for copy in own_weights + own_shared:
        copy.start()
    for n in range(nt):
        span = slice(n * d8, (n + 1) * d8)
        pair[:, span] = jnp.concatenate(
            [tok_ref[:, span].astype(F32), cot_ref[:, span].astype(F32)], axis=0).astype(BF)
    table[...] = jnp.zeros_like(table)
    for n in range(2):
        table[8 * n:8 * n + 8, :topk] = routes_ref[...]
        table[8 * n:8 * n + 8, topk:2 * topk] = gates_ref[...]

    pl.semaphore_wait(barrier, 2 * (ne - 1) + nt - 1)

    @pl.loop(1, nt)
    def _(k):
        p = lax.rem(t + k, nt)
        rcopy(table, tabs.at[block(t, 16)], TAB, (e, p)).start()
        rcopy(pair.at[:, cols(p)], gs.at[block(t, 16)], SLICE, (e, p)).start()

    @pl.loop(1, chips)
    def _(k):
        rcopy(pair, g.at[block(t, 16)], TOKX, (e, lax.rem(t + 2 * k, nt))).start()

    rcopy(pair, g.at[block(t, 16)], TOKP, (e, partner)).start()
    for n in range(2):
        there = n * q + (1 - n) * (1 - q)
        for h in range(2):
            for m in range(3):
                rcopy(source(m).at[:, cols(4 * (1 - a) + 2 * there + h)], wt.at[there, h, m, block(place, hid)],
                      WX + n, weight_dev).start()
    for n in range(2):
        for h in range(2):
            for m in range(3):
                rcopy(source(m).at[:, cols(4 * a + 2 * n + h)], wt.at[n, h, m, block(place, hid)],
                      WPART, (e, partner)).start()

    tabs[block(t, 16), :] = table[...]
    gs[block(t, 16), :] = pair[:, cols(t)]
    g[block(t, 16), :] = pair[...]

    recv(tabs.at[pl.ds(0, (nt - 1) * 16)], TAB)
    lanes = nt * 16
    chosen = tabs[...].astype(F32).T
    lane_a = lax.broadcasted_iota(jnp.int32, (lanes, lanes), 0)
    lane_b = lax.broadcasted_iota(jnp.int32, (lanes, lanes), 1)
    token_a, token_b = (lane_a // 16) * 8 + lane_a % 8, (lane_b // 16) * 8 + lane_b % 8
    earlier = jnp.where((lane_a % 16 < 8) & (token_a < token_b), 1.0, 0.0).astype(BF)
    recv(gs.at[pl.ds(0, (nt - 1) * 16)], SLICE)
    tokens_here = gs[...]
    ec = ne // 4
    size = ec * m32
    for turn in range(4):
        chunk = lax.rem(first + turn, 4)
        row = lax.broadcasted_iota(jnp.int32, (size, lanes), 0)
        lane = lax.broadcasted_iota(jnp.int32, (size, lanes), 1)
        kind, slot = (row // SLOTS) % 2, (row % SLOTS).astype(F32)
        expert = (row // m32 * 4 + chunk).astype(F32)
        named = jnp.zeros((size, lanes), F32)
        gate = jnp.zeros((size, lanes), F32)
        for k in range(topk):
            hit = chosen[k:k + 1, :] == expert
            named = jnp.where(hit, 1.0, named)
            gate = jnp.where(hit, chosen[topk + k:topk + k + 1, :] * (1.0 / 64.0), gate)
        rank = dot(named.astype(BF), earlier)
        here = jnp.where((rank == slot) & ((lane // 8) % 2 == kind), named, 0.0)
        weighted = jnp.where(kind == 1, here * gate, here).astype(BF)
        t2[block(chunk, size), :] = jnp.where(kind == 1, here, here * gate).astype(BF)
        snd[pl.ds(chunk * ec, ec)] = dot(weighted, tokens_here).astype(BF).reshape(ec, m32, d8)

        @pl.loop(0, ec)
        def _(n):
            p = n * 4 + chunk
            from_here = snd.at[chunk * ec + n]
            target = xr.at[q, core, local_group]

            @pl.when(jnp.logical_and(p == e, stays))
            def _():
                pltpu.make_async_copy(from_here, target, rsem.at[DISP + first]).start()

            @pl.when(jnp.logical_not(jnp.logical_and(p == e, stays)))
            def _():
                rcopy(from_here, target, DISP + first, (p, 2 * chip + (e // 4) % 2)).start()

    def pass_rows(k):
        chunk = lax.rem(first + 4 - k, 4)
        part = xr.at[q, :, pl.ds(chunk * gq, gq)]
        recv(part, DISP + chunk)
        rcopy(part, part, PAIR + k, row_dev).start()

    def pass_weights(n):
        there = n * (1 - q) + (1 - n) * q
        part = wt.at[there, :, :, block(2 * (1 - a) + core, hid)]
        recv(part, WX + n)
        rcopy(part, part, WF + n, (e, partner)).start()

    recv(g.at[pl.ds(0, (chips - 1) * 16)], TOKX)

    @pl.loop(1, chips)
    def _(k):
        part = g.at[block(lax.rem(t + 2 * k, nt), 16)]
        rcopy(part, part, TOKP, (e, partner)).start()

    pass_rows(0)
    recv(g.at[pl.ds(0, chips * 16)], TOKP)
    for copy in own_shared:
        copy.wait()
    sh = sw_out.shape[0]

    def shared_step(n, sums):
        piece = g[:, cols(n)]
        return tuple(
            total + dot(piece, weight[:, cols(n)], NT)
            for total, weight in zip(sums, (sw_in.at[0], sw_in.at[1], sw_out)))

    zero = jnp.zeros((nt * 16, sh), F32)
    sums = lax.fori_loop(0, nt, shared_step, (zero, zero, zero))
    pass_rows(1)
    s_gate, s_up = [v.reshape(nt, 16, sh)[:, :8].reshape(nt * 8, sh) for v in sums[:2]]
    s_back = sums[2].reshape(nt, 16, sh)[:, 8:].reshape(nt * 8, sh)
    s_act, s_slope = silu_parts(s_gate)
    s_hidden = (s_act * s_up).astype(BF)
    s_dgate = (s_back * s_up * s_slope).astype(BF)
    s_dup = (s_back * s_act).astype(BF)

    def shared_terms(low, high):
        @pl.loop(low, high)
        def _(n):
            y = dot(s_hidden, sw_out[:, cols(n)]).reshape(nt, 8, d8)
            dx = (dot(s_dgate, sw_in[0, :, cols(n)]) + dot(s_dup, sw_in[1, :, cols(n)])).reshape(nt, 8, d8)
            shs[:, :, :, cols(n)] = jnp.concatenate([y, dx], axis=1).astype(BF).reshape(chips, 2, 16, d8)

    shared_terms(0, nt // 2)
    pass_weights(0)
    pass_rows(2)
    shared_terms(nt // 2, nt)
    rcopy(shs.at[:, 1 - core], shp, SHP, (e, partner)).start()
    pass_rows(3)
    pass_weights(1)

    def products(quarter, n):
        value = [None] * 3
        for h in range(2):
            part = xr[quarter, h, pl.ds(n * 2 * gq, 2 * gq)]
            x_rows = part[:, :SLOTS].reshape(rows, d8)
            dy_rows = part[:, SLOTS:].reshape(rows, d8)
            for m in range(3):
                term = dot(dy_rows if m == 2 else x_rows, wt[quarter, h, m], NT)
                value[m] = term if h == 0 else value[m] + term
        return value

    for copy in own_weights:
        copy.wait()
    recv(wt.at[:, :, :, pl.ds(0, hid)], WPART)
    recv(wt.at[0, :, :, pl.ds(0, hid)], WF)

    @pl.loop(0, 2)
    def _(n):
        for m, value in enumerate(products(q, n)):
            pf[n, :, m * half:(m + 1) * half] = value

    recv(shp, SHP)
    for n in range(chips):
        shs[n, core] = (shs[n, core].astype(F32) + shp[n].astype(F32)).astype(BF)

    for j in (weight_chip, lax.rem(chip + 2, chips)):
        rcopy(shs.at[j, core], shr.at[chip], SHARED, (e, 2 * j + core)).start()
    recv(wt.at[0, :, :, pl.ds(0, hid)], WF + 1)
    for k in range(4):
        recv(xr.at[0, :, pl.ds(0, gq)], PAIR + k)

    def finish(n):
        for m, value in enumerate(products(1 - q, n)):
            span = slice(m * half, (m + 1) * half)
            pf[n, :, span] = pf[n, :, span] + value

    finish(1 - a)
    pb[...] = pf[1 - a].astype(BF)
    for i in range(2):
        part = pl.ds(i * (rows // 2), rows // 2)
        rcopy(pb.at[part], rs.at[part], PRE + i, weight_dev).start()
    rcopy(xr.at[:, 1 - core], xp, XP, (e, partner)).start()

    rcopy(shs.at[row_chip, core], shr.at[chip], SHARED, row_dev).start()
    finish(a)
    for i in range(2):
        part = pl.ds(i * (rows // 2), rows // 2)
        recv(rs.at[part], PRE + i)
        total = pf[a, part] + rs[part].astype(F32)
        gate_pre, up_pre, back = total[:, :half], total[:, half:2 * half], total[:, 2 * half:]
        active, slope = silu_parts(gate_pre)
        act[a, part, :half] = (active * up_pre).astype(BF)
        act[a, part, half:2 * half] = (back * up_pre * slope).astype(BF)
        act[a, part, 2 * half:] = (back * active).astype(BF)
        rcopy(act.at[a, part], act.at[a, part], ACT + i, weight_dev).start()
    for i in range(2):
        recv(act.at[1 - a, pl.ds(i * (rows // 2), rows // 2)], ACT + i)
    rcopy(act, actp, ACTP, (e, partner)).start()

    def results(quarter, h, n):
        y = dot(act[n, :, :half], wt[quarter, h, 2])
        dx = dot(act[n, :, half:], wt[quarter, h, 0:2].reshape(2 * half, d8))
        return jnp.concatenate([y.reshape(2 * gq, SLOTS, d8), dx.reshape(2 * gq, SLOTS, d8)], axis=1)

    def order(k):
        n = lax.rem(first // 2 + k // 2, 2)
        return 2 * n + lax.rem(first + k, 2)

    for k in range(2):
        n = lax.rem(first // 2 + k, 2)
        for h in range(2):
            ps[h, pl.ds(n * 2 * gq, 2 * gq)] = results(1 - q, h, n).astype(BF)
        for i in range(2):
            part = pl.ds(order(2 * k + i) * gq, gq)
            rcopy(ps.at[:, part], pr.at[:, part], HALF + 2 * k + i, row_dev).start()

    @pl.loop(0, 2)
    def _(n):
        for h in range(2):
            po[h, pl.ds(n * 2 * gq, 2 * gq)] = results(q, h, n)

    recv(xp, XP)
    recv(actp, ACTP)
    own_grads = []

    def gradient(n, m):
        span = slice(0, half) if m == 2 else slice((m + 1) * half, (m + 2) * half)
        kind = slice(SLOTS, m32) if m == 2 else slice(0, SLOTS)
        here = act[:, :, span].reshape(2 * rows, half)
        there = actp[:, :, span].reshape(2 * rows, half)
        x_here = xr[n, core, :, kind].reshape(2 * rows, d8)
        x_there = xp[n, :, kind].reshape(2 * rows, d8)
        gb[n, m] = (dot(here, x_here, TN) + dot(there, x_there, TN)).astype(BF)
        target = (gout_ref if m == 2 else gin_ref.at[m]).at[:, cols(4 * a + 2 * n + core)]
        which = GRAD_OUT if m == 2 else GRAD_IN
        for c in range(2):
            rcopy(gb.at[n, m, block(2 * (1 - a) + c, hid)], target, which, (e, 2 * weight_chip + c)).start()
        rcopy(gb.at[n, m, block(2 * a + 1 - core, hid)], target, which, (e, partner)).start()
        own = pltpu.make_async_copy(gb.at[n, m, block(place, hid)], target, lsem.at[2 + 3 * n + m])
        own.start()
        own_grads.append(own)

    def give_back(k):
        chunk = order(k)
        part = pl.ds(chunk * gq, gq)
        recv(pr.at[:, part], HALF + k)
        ret[:, part] = (po[:, part] + pr[:, part].astype(F32)).astype(BF)

        @pl.loop(0, gq)
        def _(n):
            place_here = chunk * gq + n
            p = 4 * (2 * n + core) + chunk
            for h in range(2):
                local = jnp.logical_and(p == e, core == h)

                @pl.when(local)
                def _():
                    pltpu.make_async_copy(ret.at[h, place_here], bk.at[home], rsem.at[BACK]).start()

                @pl.when(jnp.logical_not(local))
                def _():
                    rcopy(ret.at[h, place_here], bk.at[home], BACK, (p, 2 * chip + h)).start()

    for m in range(3):
        gradient(0, m)
    give_back(0)
    gradient(1, 0)
    gradient(1, 1)
    give_back(1)
    gradient(1, 2)
    give_back(2)
    give_back(3)

    recv(bk, BACK)
    routed = dot(t2[...], bk[...].reshape(ne * m32, d8), TN)
    fs[...] = routed.astype(BF).reshape(nt, 16, d8)

    @pl.loop(1, nt)
    def _(k):
        p = lax.rem(t + k, nt)
        rcopy(fs.at[p], fr.at[t], FINAL, (e, p)).start()

    fr[t] = fs[t]
    shr[chip] = shs[chip, core]
    recv(shr.at[pl.ds(0, chips - 1)], SHARED)
    recv(fr.at[pl.ds(0, nt - 1)], FINAL)

    for n in range(nt):
        span = slice(n * d8, (n + 1) * d8)
        total = fr[n].astype(F32) + jnp.sum(shr[:, :, span].astype(F32), axis=0)
        out_ref[:, span] = total[:8].astype(BF)
        gtok_ref[:, span] = total[8:].astype(BF)

    recv(gin_ref.at[:, :, pl.ds(0, 6 * d8)], GRAD_IN)
    recv(gout_ref.at[:, pl.ds(0, 6 * d8)], GRAD_OUT)
    for copy in own_grads:
        copy.wait()
    sent(tabs.at[pl.ds(0, (nt - 1) * 16)], TAB)
    sent(gs.at[pl.ds(0, (nt - 1) * 16)], SLICE)
    sent(g.at[pl.ds(0, (chips - 1) * 16)], TOKX)
    sent(g.at[pl.ds(0, chips * 16)], TOKP)
    sent(wt.at[:, :, :, pl.ds(0, hid)], WPART)
    for n in range(2):
        sent(wt.at[n, :, :, pl.ds(0, hid)], WX + n)
        sent(wt.at[n, :, :, pl.ds(0, hid)], WF + n)
    for k in range(4):
        sent(xr.at[0, :, pl.ds(0, gq)], PAIR + k)
        sent(ps.at[:, pl.ds(0, gq)], HALF + k)
    sent(xp, XP)
    for i in range(2):
        sent(rs.at[pl.ds(0, rows // 2)], PRE + i)
        sent(rs.at[pl.ds(0, rows // 2)], ACT + i)
    sent(actp, ACTP)
    sent(shp, SHP)
    sent(shr.at[pl.ds(0, chips - 1)], SHARED)
    sent(gin_ref.at[:, :, pl.ds(0, 6 * d8)], GRAD_IN)
    sent(gout_ref.at[:, pl.ds(0, 6 * d8)], GRAD_OUT)
    sent(fs.at[pl.ds(0, nt - 1)], FINAL)

    @pl.when(stays)
    def _():
        sent(bk.at[pl.ds(0, ne - 1)], BACK)
        sent(bk.at[pl.ds(0, ne - 1)], DISP + first)

    @pl.when(jnp.logical_not(stays))
    def _():
        sent(bk, BACK)
        sent(bk, DISP + first)


def hand_over(out_a, gtok_a, gin_a, gout_a, out_b, gtok_b, gin_b, gout_b, small, big, sem):
    hid = gout_a.shape[0]
    part = hid // 2
    moves = []
    for m in range(3):
        left, right = (gout_a, gout_b) if m == 2 else (gin_a.at[m], gin_b.at[m])
        for n in range(2):
            rows = pl.ds(n * part, part)
            moves.append((left.at[rows], big.at[m, rows], right.at[rows]))
    moves += [(out_a, small.at[0], out_b), (gtok_a, small.at[1], gtok_b)]
    inward = [pltpu.make_async_copy(src, mid, sem.at[0, n]) for n, (src, mid, _) in enumerate(moves)]
    outward = [pltpu.make_async_copy(mid, dst, sem.at[1, n]) for n, (_, mid, dst) in enumerate(moves)]
    for copy in inward:
        copy.start()
    for before, after in zip(inward, outward):
        before.wait()
        after.start()
    for copy in outward:
        copy.wait()


def on_device(tokens, routes, gate_num, cotangent, w_in, w_out, shared_in, shared_out):
    ne, nt = lax.axis_size("expert"), lax.axis_size("tensor")
    chips = nt // 2
    own, features = tokens.shape
    topk = routes.shape[1]
    hid, sh = w_out.shape[1], shared_out.shape[0]
    d8, half, gl_count = features // nt, 4 * hid, ne // 2
    rows, m32 = gl_count * SLOTS // 2, 2 * SLOTS
    vm = pl.BlockSpec(memory_space=pltpu.VMEM)
    hbm = pl.BlockSpec(memory_space=pl.ANY)
    scratch = [
        pltpu.VMEM((16, features), BF),
        pltpu.VMEM((16, 128), jnp.int32),
        pltpu.VMEM((nt * 16, 128), jnp.int32),
        pltpu.VMEM((nt * 16, d8), BF),
        pltpu.VMEM((nt * 16, features), BF),
        pltpu.VMEM((2, 2, 3, half, d8), BF),
        pltpu.VMEM((2, sh, features), BF),
        pltpu.VMEM((sh, features), BF),
        pltpu.VMEM((ne * m32, nt * 16), BF),
        pltpu.VMEM((ne, m32, d8), BF),
        pltpu.VMEM((2, 2, gl_count, m32, d8), BF),
        pltpu.VMEM((2, gl_count, m32, d8), BF),
        pltpu.VMEM((2, rows, 3 * half), F32),
        pltpu.VMEM((rows, 3 * half), BF),
        pltpu.VMEM((rows, 3 * half), BF),
        pltpu.VMEM((2, rows, 3 * half), BF),
        pltpu.VMEM((2, rows, 3 * half), BF),
        pltpu.VMEM((2, gl_count, m32, d8), BF),
        pltpu.VMEM((2, gl_count, m32, d8), BF),
        pltpu.VMEM((2, gl_count, m32, d8), F32),
        pltpu.VMEM((2, gl_count, m32, d8), BF),
        pltpu.VMEM((ne, m32, d8), BF),
        pltpu.VMEM((2, 3, half, d8), BF),
        pltpu.VMEM((chips, 2, 16, features), BF),
        pltpu.VMEM((chips, 16, features), BF),
        pltpu.VMEM((chips, 16, features), BF),
        pltpu.VMEM((nt, 16, d8), BF),
        pltpu.VMEM((nt, 16, d8), BF),
        pltpu.SemaphoreType.DMA((COUNT,)),
        pltpu.SemaphoreType.DMA((COUNT,)),
        pltpu.SemaphoreType.DMA((14,)),
    ]
    shapes = (
        jax.ShapeDtypeStruct((own, features), BF),
        jax.ShapeDtypeStruct((own, features), BF),
        jax.ShapeDtypeStruct((2, hid, features), BF),
        jax.ShapeDtypeStruct((hid, features), BF),
    )
    results = pl.pallas_call(
        functools.partial(kernel, topk),
        out_shape=shapes,
        in_specs=[vm, vm, vm, vm, hbm, hbm, hbm, hbm],
        out_specs=(vm, vm, hbm, hbm),
        scratch_shapes=scratch,
        compiler_params=pltpu.CompilerParams(
            collective_id=0, has_side_effects=True, vmem_limit_bytes=56 * 2**20
        ),
    )(tokens, cotangent, routes, gate_num, w_in[0], w_out[0], shared_in, shared_out)
    out, gtok, gin, gout = pl.pallas_call(
        hand_over,
        out_shape=shapes,
        in_specs=[hbm] * 4,
        out_specs=(hbm,) * 4,
        scratch_shapes=[
            pltpu.VMEM((2, own, features), BF),
            pltpu.VMEM((3, hid, features), BF),
            pltpu.SemaphoreType.DMA((2, 8)),
        ],
        compiler_params=pltpu.CompilerParams(vmem_limit_bytes=60 * 2**20),
    )(*results)
    return out, gtok, gin[None], gout[None]


def solution(mesh):
    in_specs = (
        P(("expert", "tensor"), None),
        P(("expert", "tensor"), None),
        P(("expert", "tensor"), None),
        P(("expert", "tensor"), None),
        P("expert", None, "tensor", None),
        P("expert", "tensor", None),
        P(None, "tensor", None),
        P("tensor", None),
    )
    out_specs = (
        P(("expert", "tensor"), None),
        P(("expert", "tensor"), None),
        P("expert", None, "tensor", None),
        P("expert", "tensor", None),
    )
    return jax.shard_map(
        on_device, mesh=mesh, in_specs=in_specs, out_specs=out_specs, check_vma=False
    )
```

```python
import functools

import jax
import jax.numpy as jnp
from jax import lax
from jax.experimental import pallas as pl
from jax.experimental.pallas import tpu as pltpu
from jax.sharding import PartitionSpec as P

MESH = pl.DeviceIdType.MESH
BF = jnp.bfloat16
F32 = jnp.float32
SLOTS = 16
NT = (((1,), (1,)), ((), ()))
TN = (((0,), (0,)), ((), ()))

TAB, SLICE, TOKX, TOKP, WPART, XP, ACTP, BACK, GRAD_IN, GRAD_OUT, SHP, SHARED, FINAL = range(13)
PRE, ACT, WX, WF, DISP, PAIR, HALF = 13, 17, 21, 23, 25, 29, 33
COUNT = 37


def dot(left, right, dims=None):
    dims = dims or (((1,), (0,)), ((), ()))
    return lax.dot_general(left, right, dims, preferred_element_type=F32)


def silu_parts(preact):
    sig_value = jax.nn.sigmoid(preact)
    return preact * sig_value, sig_value * (1.0 + preact * (1.0 - sig_value))


def kernel(
    topk,
    tok_ref, cot_ref, routes_ref, gates_ref, w_in, w_out, sh_in, sh_out,
    out_ref, gtok_ref, gin_ref, gout_ref,
    pair, table, tabs, gs, g, wt, sw_in, sw_out, t2, snd, xr, xp, pf, pb, rs, act, actp, ps, pr, po, ret, bk, gb,
    shs, shp, shr, fs, fr, ssem, rsem, lsem,
):
    ne, nt = lax.axis_size("expert"), lax.axis_size("tensor")
    e, t = lax.axis_index("expert"), lax.axis_index("tensor")
    chip, core = t // 2, t % 2
    chips = nt // 2
    a, q = chip // 2, chip % 2
    partner = t + 1 - 2 * core
    row_chip = 2 * a + 1 - q
    weight_chip = chips - 1 - chip
    row_dev, weight_dev = (e, 2 * row_chip + core), (e, 2 * weight_chip + core)
    first = e % 4
    stays = (e // 4) % 2 == core
    home = (e % 4) * (ne // 4) + e // 4
    local_group = (e % 4) * (ne // 8) + e // 8
    d8 = gs.shape[1]
    hid = w_out.shape[0]
    half = 4 * hid
    gl_count = ne // 2
    gq = gl_count // 4
    rows = gq * SLOTS
    own_rows = rows // 2
    m32 = 2 * SLOTS

    def rcopy(src, dst, which, dev):
        return pltpu.make_async_remote_copy(
            src_ref=src, dst_ref=dst, send_sem=ssem.at[which], recv_sem=rsem.at[which],
            device_id=dev, device_id_type=MESH,
        )

    def recv(ref, which):
        pltpu.make_async_copy(ref, ref, rsem.at[which]).wait()

    def sent(ref, which):
        pltpu.make_async_copy(ref, ref, ssem.at[which]).wait()

    def cols(piece):
        return pl.ds(pl.multiple_of(piece * d8, 128), d8)

    def block(index, size):
        return pl.ds(pl.multiple_of(index * size, 16), size)

    def source(m):
        return w_out if m == 2 else w_in.at[m]

    place = 2 * a + core
    own_shared = [
        pltpu.make_async_copy(sh_in, sw_in, lsem.at[0]),
        pltpu.make_async_copy(sh_out, sw_out, lsem.at[1]),
    ]
    own_weights = [
        pltpu.make_async_copy(
            source(m).at[:, cols(4 * a + 2 * n + h)], wt.at[n, h, m, block(place, hid)], lsem.at[2 + 6 * n + 3 * h + m])
        for n in range(2) for h in range(2) for m in range(3)]

    barrier = pltpu.get_barrier_semaphore()

    @pl.loop(1, nt)
    def _(k):
        pl.semaphore_signal(barrier, inc=1, device_id=(e, lax.rem(t + k, nt)), device_id_type=MESH)

    @pl.loop(1, ne)
    def _(k):
        for h in range(2):
            pl.semaphore_signal(barrier, inc=1, device_id=(lax.rem(e + k, ne), 2 * chip + h), device_id_type=MESH)

    for copy in own_weights + own_shared:
        copy.start()
    for n in range(nt):
        span = slice(n * d8, (n + 1) * d8)
        pair[:, span] = jnp.concatenate(
            [tok_ref[:, span].astype(F32), cot_ref[:, span].astype(F32)], axis=0).astype(BF)
    table[...] = jnp.zeros_like(table)
    for n in range(2):
        table[8 * n:8 * n + 8, :topk] = routes_ref[...]
        table[8 * n:8 * n + 8, topk:2 * topk] = gates_ref[...]

    pl.semaphore_wait(barrier, 2 * (ne - 1) + nt - 1)

    @pl.loop(1, nt)
    def _(k):
        p = lax.rem(t + k, nt)
        rcopy(table, tabs.at[block(t, 16)], TAB, (e, p)).start()
        rcopy(pair.at[:, cols(p)], gs.at[block(t, 16)], SLICE, (e, p)).start()

    @pl.loop(1, chips)
    def _(k):
        rcopy(pair, g.at[block(t, 16)], TOKX, (e, lax.rem(t + 2 * k, nt))).start()

    rcopy(pair, g.at[block(t, 16)], TOKP, (e, partner)).start()
    for n in range(2):
        there = n * q + (1 - n) * (1 - q)
        for h in range(2):
            for m in range(3):
                rcopy(source(m).at[:, cols(4 * (1 - a) + 2 * there + h)], wt.at[there, h, m, block(place, hid)],
                      WX + n, weight_dev).start()
    for n in range(2):
        for h in range(2):
            for m in range(3):
                rcopy(source(m).at[:, cols(4 * a + 2 * n + h)], wt.at[n, h, m, block(place, hid)],
                      WPART, (e, partner)).start()

    tabs[block(t, 16), :] = table[...]
    gs[block(t, 16), :] = pair[:, cols(t)]
    g[block(t, 16), :] = pair[...]

    recv(tabs.at[pl.ds(0, (nt - 1) * 16)], TAB)
    lanes = nt * 16
    chosen = tabs[...].astype(F32).T
    lane_a = lax.broadcasted_iota(jnp.int32, (lanes, lanes), 0)
    lane_b = lax.broadcasted_iota(jnp.int32, (lanes, lanes), 1)
    token_a, token_b = (lane_a // 16) * 8 + lane_a % 8, (lane_b // 16) * 8 + lane_b % 8
    earlier = jnp.where((lane_a % 16 < 8) & (token_a < token_b), 1.0, 0.0).astype(BF)
    recv(gs.at[pl.ds(0, (nt - 1) * 16)], SLICE)
    tokens_here = gs[...]
    ec = ne // 4
    size = ec * m32
    for turn in range(4):
        chunk = lax.rem(first + turn, 4)
        row = lax.broadcasted_iota(jnp.int32, (size, lanes), 0)
        lane = lax.broadcasted_iota(jnp.int32, (size, lanes), 1)
        kind, slot = (row // SLOTS) % 2, (row % SLOTS).astype(F32)
        expert = (row // m32 * 4 + chunk).astype(F32)
        named = jnp.zeros((size, lanes), F32)
        gate = jnp.zeros((size, lanes), F32)
        for k in range(topk):
            hit = chosen[k:k + 1, :] == expert
            named = jnp.where(hit, 1.0, named)
            gate = jnp.where(hit, chosen[topk + k:topk + k + 1, :] * (1.0 / 64.0), gate)
        rank = dot(named.astype(BF), earlier)
        here = jnp.where((rank == slot) & ((lane // 8) % 2 == kind), named, 0.0)
        weighted = jnp.where(kind == 1, here * gate, here).astype(BF)
        t2[block(chunk, size), :] = jnp.where(kind == 1, here, here * gate).astype(BF)
        snd[pl.ds(chunk * ec, ec)] = dot(weighted, tokens_here).astype(BF).reshape(ec, m32, d8)

        @pl.loop(0, ec)
        def _(n):
            p = n * 4 + chunk
            from_here = snd.at[chunk * ec + n]
            target = xr.at[q, core, local_group]

            @pl.when(jnp.logical_and(p == e, stays))
            def _():
                pltpu.make_async_copy(from_here, target, rsem.at[DISP + first]).start()

            @pl.when(jnp.logical_not(jnp.logical_and(p == e, stays)))
            def _():
                rcopy(from_here, target, DISP + first, (p, 2 * chip + (e // 4) % 2)).start()

    def order(k):
        return lax.rem(first + 4 - k, 4)

    def pass_rows(k):
        chunk = order(k)
        part = xr.at[q, :, pl.ds(chunk * gq, gq)]
        recv(part, DISP + chunk)
        rcopy(part, part, PAIR + k, row_dev).start()

    def pass_weights(n):
        there = n * (1 - q) + (1 - n) * q
        part = wt.at[there, :, :, block(2 * (1 - a) + core, hid)]
        recv(part, WX + n)
        rcopy(part, part, WF + n, (e, partner)).start()

    recv(g.at[pl.ds(0, (chips - 1) * 16)], TOKX)

    @pl.loop(1, chips)
    def _(k):
        part = g.at[block(lax.rem(t + 2 * k, nt), 16)]
        rcopy(part, part, TOKP, (e, partner)).start()

    pass_rows(0)
    recv(g.at[pl.ds(0, chips * 16)], TOKP)
    for copy in own_shared:
        copy.wait()
    sh = sw_out.shape[0]

    def shared_step(n, sums):
        piece = g[:, cols(n)]
        return tuple(
            total + dot(piece, weight[:, cols(n)], NT)
            for total, weight in zip(sums, (sw_in.at[0], sw_in.at[1], sw_out)))

    zero = jnp.zeros((nt * 16, sh), F32)
    sums = lax.fori_loop(0, nt, shared_step, (zero, zero, zero))
    pass_rows(1)
    s_gate, s_up = [v.reshape(nt, 16, sh)[:, :8].reshape(nt * 8, sh) for v in sums[:2]]
    s_back = sums[2].reshape(nt, 16, sh)[:, 8:].reshape(nt * 8, sh)
    s_act, s_slope = silu_parts(s_gate)
    s_hidden = (s_act * s_up).astype(BF)
    s_dgate = (s_back * s_up * s_slope).astype(BF)
    s_dup = (s_back * s_act).astype(BF)

    def shared_terms(low, high):
        @pl.loop(low, high)
        def _(n):
            y = dot(s_hidden, sw_out[:, cols(n)]).reshape(nt, 8, d8)
            dx = (dot(s_dgate, sw_in[0, :, cols(n)]) + dot(s_dup, sw_in[1, :, cols(n)])).reshape(nt, 8, d8)
            shs[:, :, :, cols(n)] = jnp.concatenate([y, dx], axis=1).astype(BF).reshape(chips, 2, 16, d8)

    shared_terms(0, nt // 2)
    pass_weights(0)
    pass_rows(2)
    shared_terms(nt // 2, nt)
    rcopy(shs.at[:, 1 - core], shp, SHP, (e, partner)).start()
    pass_weights(1)

    def products(quarter, chunk):
        value = [None] * 3
        for h in range(2):
            part = xr[quarter, h, pl.ds(chunk * gq, gq)]
            x_rows = part[:, :SLOTS].reshape(rows, d8)
            dy_rows = part[:, SLOTS:].reshape(rows, d8)
            for m in range(3):
                term = dot(dy_rows if m == 2 else x_rows, wt[quarter, h, m], NT)
                value[m] = term if h == 0 else value[m] + term
        return value

    def begin(k):
        chunk = order(k)
        for m, value in enumerate(products(q, chunk)):
            pf[chunk, :, m * half:(m + 1) * half] = value

    def finish(k):
        chunk = order(k)
        recv(xr.at[0, :, pl.ds(0, gq)], PAIR + k)
        for m, value in enumerate(products(1 - q, chunk)):
            span = slice(m * half, (m + 1) * half)
            pf[chunk, :, span] = pf[chunk, :, span] + value
        pb[chunk] = pf[chunk, block(1 - a, own_rows)].astype(BF)
        rcopy(pb.at[chunk], rs.at[chunk], PRE + k, weight_dev).start()

    def activate(k):
        chunk = order(k)
        recv(rs.at[chunk], PRE + k)
        total = pf[chunk, block(a, own_rows)] + rs[chunk].astype(F32)
        gate_pre, up_pre, back = total[:, :half], total[:, half:2 * half], total[:, 2 * half:]
        active, slope = silu_parts(gate_pre)
        act[chunk, a, :, :half] = (active * up_pre).astype(BF)
        act[chunk, a, :, half:2 * half] = (back * up_pre * slope).astype(BF)
        act[chunk, a, :, 2 * half:] = (back * active).astype(BF)
        rcopy(act.at[chunk, a], act.at[chunk, a], ACT + k, weight_dev).start()

    def results(quarter, h, chunk):
        left = act[chunk].reshape(rows, 3 * half)
        y = dot(left[:, :half], wt[quarter, h, 2])
        dx = dot(left[:, half:], wt[quarter, h, 0:2].reshape(2 * half, d8))
        return jnp.concatenate([y.reshape(gq, SLOTS, d8), dx.reshape(gq, SLOTS, d8)], axis=1)

    def answer(k):
        chunk = order(k)
        part = pl.ds(chunk * gq, gq)
        recv(act.at[chunk, 1 - a], ACT + k)
        rcopy(act.at[chunk], actp.at[chunk], ACTP, (e, partner)).start()
        for h in range(2):
            ps[h, part] = results(1 - q, h, chunk).astype(BF)
        rcopy(ps.at[:, part], pr.at[:, part], HALF + k, row_dev).start()
        for h in range(2):
            po[h, part] = results(q, h, chunk)

    def give_back(k):
        chunk = order(k)
        part = pl.ds(chunk * gq, gq)
        recv(pr.at[:, part], HALF + k)
        ret[:, part] = (po[:, part] + pr[:, part].astype(F32)).astype(BF)

        @pl.loop(0, gq)
        def _(n):
            place_here = chunk * gq + n
            p = 4 * (2 * n + core) + chunk
            for h in range(2):
                local = jnp.logical_and(p == e, core == h)

                @pl.when(local)
                def _():
                    pltpu.make_async_copy(ret.at[h, place_here], bk.at[home], rsem.at[BACK]).start()

                @pl.when(jnp.logical_not(local))
                def _():
                    rcopy(ret.at[h, place_here], bk.at[home], BACK, (p, 2 * chip + h)).start()

    for copy in own_weights:
        copy.wait()
    recv(wt.at[:, :, :, pl.ds(0, hid)], WPART)
    recv(wt.at[0, :, :, pl.ds(0, hid)], WF)
    for k in range(3):
        begin(k)
    recv(shp, SHP)
    for n in range(chips):
        shs[n, core] = (shs[n, core].astype(F32) + shp[n].astype(F32)).astype(BF)
    for j in (weight_chip, lax.rem(chip + 2, chips)):
        rcopy(shs.at[j, core], shr.at[chip], SHARED, (e, 2 * j + core)).start()
    recv(wt.at[0, :, :, pl.ds(0, hid)], WF + 1)
    finish(0)
    pass_rows(3)
    activate(0)
    begin(3)
    finish(1)
    answer(0)
    activate(1)
    finish(2)
    answer(1)
    activate(2)
    finish(3)
    rcopy(xr.at[:, 1 - core], xp, XP, (e, partner)).start()
    answer(2)
    activate(3)
    give_back(0)
    answer(3)
    rcopy(shs.at[row_chip, core], shr.at[chip], SHARED, row_dev).start()

    recv(xp, XP)
    recv(actp, ACTP)
    own_grads = []

    def gradient(n, m):
        span = slice(0, half) if m == 2 else slice((m + 1) * half, (m + 2) * half)
        kind = slice(SLOTS, m32) if m == 2 else slice(0, SLOTS)
        here = act[:, :, :, span].reshape(4 * rows, half)
        there = actp[:, :, :, span].reshape(4 * rows, half)
        x_here = xr[n, core, :, kind].reshape(4 * rows, d8)
        x_there = xp[n, :, kind].reshape(4 * rows, d8)
        gb[n, m] = (dot(here, x_here, TN) + dot(there, x_there, TN)).astype(BF)
        target = (gout_ref if m == 2 else gin_ref.at[m]).at[:, cols(4 * a + 2 * n + core)]
        which = GRAD_OUT if m == 2 else GRAD_IN
        for c in range(2):
            rcopy(gb.at[n, m, block(2 * (1 - a) + c, hid)], target, which, (e, 2 * weight_chip + c)).start()
        rcopy(gb.at[n, m, block(2 * a + 1 - core, hid)], target, which, (e, partner)).start()
        own = pltpu.make_async_copy(gb.at[n, m, block(place, hid)], target, lsem.at[2 + 3 * n + m])
        own.start()
        own_grads.append(own)

    for m in range(3):
        gradient(0, m)
    give_back(1)
    for m in range(3):
        gradient(1, m)
    give_back(2)
    give_back(3)

    recv(bk, BACK)
    routed = dot(t2[...], bk[...].reshape(ne * m32, d8), TN)
    fs[...] = routed.astype(BF).reshape(nt, 16, d8)

    @pl.loop(1, nt)
    def _(k):
        p = lax.rem(t + k, nt)
        rcopy(fs.at[p], fr.at[t], FINAL, (e, p)).start()

    fr[t] = fs[t]
    shr[chip] = shs[chip, core]
    recv(shr.at[pl.ds(0, chips - 1)], SHARED)
    recv(fr.at[pl.ds(0, nt - 1)], FINAL)

    for n in range(nt):
        span = slice(n * d8, (n + 1) * d8)
        total = fr[n].astype(F32) + jnp.sum(shr[:, :, span].astype(F32), axis=0)
        out_ref[:, span] = total[:8].astype(BF)
        gtok_ref[:, span] = total[8:].astype(BF)

    recv(gin_ref.at[:, :, pl.ds(0, 6 * d8)], GRAD_IN)
    recv(gout_ref.at[:, pl.ds(0, 6 * d8)], GRAD_OUT)
    for copy in own_grads:
        copy.wait()
    sent(tabs.at[pl.ds(0, (nt - 1) * 16)], TAB)
    sent(gs.at[pl.ds(0, (nt - 1) * 16)], SLICE)
    sent(g.at[pl.ds(0, (chips - 1) * 16)], TOKX)
    sent(g.at[pl.ds(0, chips * 16)], TOKP)
    sent(wt.at[:, :, :, pl.ds(0, hid)], WPART)
    for n in range(2):
        sent(wt.at[n, :, :, pl.ds(0, hid)], WX + n)
        sent(wt.at[n, :, :, pl.ds(0, hid)], WF + n)
    for k in range(4):
        sent(xr.at[0, :, pl.ds(0, gq)], PAIR + k)
        sent(ps.at[:, pl.ds(0, gq)], HALF + k)
    sent(xp, XP)
    for k in range(4):
        sent(rs.at[0], PRE + k)
        sent(rs.at[0], ACT + k)
    sent(actp, ACTP)
    sent(shp, SHP)
    sent(shr.at[pl.ds(0, chips - 1)], SHARED)
    sent(gin_ref.at[:, :, pl.ds(0, 6 * d8)], GRAD_IN)
    sent(gout_ref.at[:, pl.ds(0, 6 * d8)], GRAD_OUT)
    sent(fs.at[pl.ds(0, nt - 1)], FINAL)

    @pl.when(stays)
    def _():
        sent(bk.at[pl.ds(0, ne - 1)], BACK)
        sent(bk.at[pl.ds(0, ne - 1)], DISP + first)

    @pl.when(jnp.logical_not(stays))
    def _():
        sent(bk, BACK)
        sent(bk, DISP + first)


def hand_over(out_a, gtok_a, gin_a, gout_a, out_b, gtok_b, gin_b, gout_b, small, big, sem):
    hid = gout_a.shape[0]
    part = hid // 2
    moves = []
    for m in range(3):
        left, right = (gout_a, gout_b) if m == 2 else (gin_a.at[m], gin_b.at[m])
        for n in range(2):
            rows = pl.ds(n * part, part)
            moves.append((left.at[rows], big.at[m, rows], right.at[rows]))
    moves += [(out_a, small.at[0], out_b), (gtok_a, small.at[1], gtok_b)]
    inward = [pltpu.make_async_copy(src, mid, sem.at[0, n]) for n, (src, mid, _) in enumerate(moves)]
    outward = [pltpu.make_async_copy(mid, dst, sem.at[1, n]) for n, (_, mid, dst) in enumerate(moves)]
    for copy in inward:
        copy.start()
    for before, after in zip(inward, outward):
        before.wait()
        after.start()
    for copy in outward:
        copy.wait()


def on_device(tokens, routes, gate_num, cotangent, w_in, w_out, shared_in, shared_out):
    ne, nt = lax.axis_size("expert"), lax.axis_size("tensor")
    chips = nt // 2
    own, features = tokens.shape
    topk = routes.shape[1]
    hid, sh = w_out.shape[1], shared_out.shape[0]
    d8, half, gl_count = features // nt, 4 * hid, ne // 2
    rows, m32 = gl_count * SLOTS // 4, 2 * SLOTS
    vm = pl.BlockSpec(memory_space=pltpu.VMEM)
    hbm = pl.BlockSpec(memory_space=pl.ANY)
    scratch = [
        pltpu.VMEM((16, features), BF),
        pltpu.VMEM((16, 128), jnp.int32),
        pltpu.VMEM((nt * 16, 128), jnp.int32),
        pltpu.VMEM((nt * 16, d8), BF),
        pltpu.VMEM((nt * 16, features), BF),
        pltpu.VMEM((2, 2, 3, half, d8), BF),
        pltpu.VMEM((2, sh, features), BF),
        pltpu.VMEM((sh, features), BF),
        pltpu.VMEM((ne * m32, nt * 16), BF),
        pltpu.VMEM((ne, m32, d8), BF),
        pltpu.VMEM((2, 2, gl_count, m32, d8), BF),
        pltpu.VMEM((2, gl_count, m32, d8), BF),
        pltpu.VMEM((4, rows, 3 * half), F32),
        pltpu.VMEM((4, rows // 2, 3 * half), BF),
        pltpu.VMEM((4, rows // 2, 3 * half), BF),
        pltpu.VMEM((4, 2, rows // 2, 3 * half), BF),
        pltpu.VMEM((4, 2, rows // 2, 3 * half), BF),
        pltpu.VMEM((2, gl_count, m32, d8), BF),
        pltpu.VMEM((2, gl_count, m32, d8), BF),
        pltpu.VMEM((2, gl_count, m32, d8), F32),
        pltpu.VMEM((2, gl_count, m32, d8), BF),
        pltpu.VMEM((ne, m32, d8), BF),
        pltpu.VMEM((2, 3, half, d8), BF),
        pltpu.VMEM((chips, 2, 16, features), BF),
        pltpu.VMEM((chips, 16, features), BF),
        pltpu.VMEM((chips, 16, features), BF),
        pltpu.VMEM((nt, 16, d8), BF),
        pltpu.VMEM((nt, 16, d8), BF),
        pltpu.SemaphoreType.DMA((COUNT,)),
        pltpu.SemaphoreType.DMA((COUNT,)),
        pltpu.SemaphoreType.DMA((14,)),
    ]
    shapes = (
        jax.ShapeDtypeStruct((own, features), BF),
        jax.ShapeDtypeStruct((own, features), BF),
        jax.ShapeDtypeStruct((2, hid, features), BF),
        jax.ShapeDtypeStruct((hid, features), BF),
    )
    results = pl.pallas_call(
        functools.partial(kernel, topk),
        out_shape=shapes,
        in_specs=[vm, vm, vm, vm, hbm, hbm, hbm, hbm],
        out_specs=(vm, vm, hbm, hbm),
        scratch_shapes=scratch,
        compiler_params=pltpu.CompilerParams(
            collective_id=0, has_side_effects=True, vmem_limit_bytes=56 * 2**20
        ),
    )(tokens, cotangent, routes, gate_num, w_in[0], w_out[0], shared_in, shared_out)
    out, gtok, gin, gout = pl.pallas_call(
        hand_over,
        out_shape=shapes,
        in_specs=[hbm] * 4,
        out_specs=(hbm,) * 4,
        scratch_shapes=[
            pltpu.VMEM((2, own, features), BF),
            pltpu.VMEM((3, hid, features), BF),
            pltpu.SemaphoreType.DMA((2, 8)),
        ],
        compiler_params=pltpu.CompilerParams(vmem_limit_bytes=60 * 2**20),
    )(*results)
    return out, gtok, gin[None], gout[None]


def solution(mesh):
    in_specs = (
        P(("expert", "tensor"), None),
        P(("expert", "tensor"), None),
        P(("expert", "tensor"), None),
        P(("expert", "tensor"), None),
        P("expert", None, "tensor", None),
        P("expert", "tensor", None),
        P(None, "tensor", None),
        P("tensor", None),
    )
    out_specs = (
        P(("expert", "tensor"), None),
        P(("expert", "tensor"), None),
        P("expert", None, "tensor", None),
        P("expert", "tensor", None),
    )
    return jax.shard_map(
        on_device, mesh=mesh, in_specs=in_specs, out_specs=out_specs, check_vma=False
    )
```

```python
import functools

import jax
import jax.numpy as jnp
from jax import lax
from jax.experimental import pallas as pl
from jax.experimental.pallas import tpu as pltpu
from jax.sharding import PartitionSpec as P

MESH = pl.DeviceIdType.MESH
BF = jnp.bfloat16
F32 = jnp.float32
SLOTS = 16
NT = (((1,), (1,)), ((), ()))
TN = (((0,), (0,)), ((), ()))

TAB, SLICE, TOKX, TOKP, WPART, XP, ACTP, BACK, GRAD_IN, GRAD_OUT, SHP, SHARED, FINAL = range(13)
PRE, ACT, WX, WF, DISP, PAIR, HALF = 13, 17, 21, 23, 25, 29, 33
COUNT = 37


def dot(left, right, dims=None):
    dims = dims or (((1,), (0,)), ((), ()))
    return lax.dot_general(left, right, dims, preferred_element_type=F32)


def silu_parts(preact):
    sig_value = jax.nn.sigmoid(preact)
    return preact * sig_value, sig_value * (1.0 + preact * (1.0 - sig_value))


def kernel(
    topk,
    tok_ref, cot_ref, routes_ref, gates_ref, w_in, w_out, sh_in, sh_out,
    out_ref, gtok_ref, gin_ref, gout_ref,
    pair, table, tabs, gs, g, wt, sw_in, sw_out, t2, snd, xr, xp, pf, pb, rs, act, actp, ps, pr, po, ret, bk, gb,
    shs, shp, shr, fs, fr, ssem, rsem, lsem,
):
    ne, nt = lax.axis_size("expert"), lax.axis_size("tensor")
    e, t = lax.axis_index("expert"), lax.axis_index("tensor")
    chip, core = t // 2, t % 2
    chips = nt // 2
    a, q = chip // 2, chip % 2
    partner = t + 1 - 2 * core
    row_chip = 2 * a + 1 - q
    weight_chip = chips - 1 - chip
    row_dev, weight_dev = (e, 2 * row_chip + core), (e, 2 * weight_chip + core)
    first = e % 4
    stays = (e // 4) % 2 == core
    home = (e % 4) * (ne // 4) + e // 4
    local_group = (e % 4) * (ne // 8) + e // 8
    d8 = gs.shape[1]
    hid = w_out.shape[0]
    half = 4 * hid
    gl_count = ne // 2
    gq = gl_count // 4
    rows = gq * SLOTS
    own_rows = rows // 2
    m32 = 2 * SLOTS

    def rcopy(src, dst, which, dev):
        return pltpu.make_async_remote_copy(
            src_ref=src, dst_ref=dst, send_sem=ssem.at[which], recv_sem=rsem.at[which],
            device_id=dev, device_id_type=MESH,
        )

    def recv(ref, which):
        pltpu.make_async_copy(ref, ref, rsem.at[which]).wait()

    def sent(ref, which):
        pltpu.make_async_copy(ref, ref, ssem.at[which]).wait()

    def cols(piece):
        return pl.ds(pl.multiple_of(piece * d8, 128), d8)

    def block(index, size):
        return pl.ds(pl.multiple_of(index * size, 16), size)

    def source(m):
        return w_out if m == 2 else w_in.at[m]

    place = 2 * a + core
    own_shared = [
        pltpu.make_async_copy(sh_in, sw_in, lsem.at[0]),
        pltpu.make_async_copy(sh_out, sw_out, lsem.at[1]),
    ]
    own_weights = [
        pltpu.make_async_copy(
            source(m).at[:, cols(4 * a + 2 * n + h)], wt.at[n, h, m, block(place, hid)], lsem.at[2 + 6 * n + 3 * h + m])
        for n in range(2) for h in range(2) for m in range(3)]

    barrier = pltpu.get_barrier_semaphore()

    @pl.loop(1, nt)
    def _(k):
        pl.semaphore_signal(barrier, inc=1, device_id=(e, lax.rem(t + k, nt)), device_id_type=MESH)

    @pl.loop(1, ne)
    def _(k):
        for h in range(2):
            pl.semaphore_signal(barrier, inc=1, device_id=(lax.rem(e + k, ne), 2 * chip + h), device_id_type=MESH)

    for copy in own_weights + own_shared:
        copy.start()
    for n in range(nt):
        span = slice(n * d8, (n + 1) * d8)
        pair[:, span] = jnp.concatenate(
            [tok_ref[:, span].astype(F32), cot_ref[:, span].astype(F32)], axis=0).astype(BF)
    table[...] = jnp.zeros_like(table)
    for n in range(2):
        table[8 * n:8 * n + 8, :topk] = routes_ref[...]
        table[8 * n:8 * n + 8, topk:2 * topk] = gates_ref[...]

    pl.semaphore_wait(barrier, 2 * (ne - 1) + nt - 1)

    @pl.loop(1, nt)
    def _(k):
        p = lax.rem(t + k, nt)
        rcopy(table, tabs.at[block(t, 16)], TAB, (e, p)).start()
        rcopy(pair.at[:, cols(p)], gs.at[block(t, 16)], SLICE, (e, p)).start()

    for n in range(2):
        there = n * q + (1 - n) * (1 - q)
        for h in range(2):
            for m in range(3):
                rcopy(source(m).at[:, cols(4 * (1 - a) + 2 * there + h)], wt.at[there, h, m, block(place, hid)],
                      WX + n, weight_dev).start()
    for n in range(2):
        for h in range(2):
            for m in range(3):
                rcopy(source(m).at[:, cols(4 * a + 2 * n + h)], wt.at[n, h, m, block(place, hid)],
                      WPART, (e, partner)).start()

    rcopy(pair, g.at[block(t, 16)], TOKP, (e, partner)).start()

    tabs[block(t, 16), :] = table[...]
    gs[block(t, 16), :] = pair[:, cols(t)]
    g[block(t, 16), :] = pair[...]

    recv(tabs.at[pl.ds(0, (nt - 1) * 16)], TAB)
    lanes = nt * 16
    chosen = tabs[...].astype(F32).T
    lane_a = lax.broadcasted_iota(jnp.int32, (lanes, lanes), 0)
    lane_b = lax.broadcasted_iota(jnp.int32, (lanes, lanes), 1)
    token_a, token_b = (lane_a // 16) * 8 + lane_a % 8, (lane_b // 16) * 8 + lane_b % 8
    earlier = jnp.where((lane_a % 16 < 8) & (token_a < token_b), 1.0, 0.0).astype(BF)
    recv(gs.at[pl.ds(0, (nt - 1) * 16)], SLICE)
    tokens_here = gs[...]
    ec = ne // 4
    size = ec * m32
    for turn in range(4):
        chunk = lax.rem(first + turn, 4)
        row = lax.broadcasted_iota(jnp.int32, (size, lanes), 0)
        lane = lax.broadcasted_iota(jnp.int32, (size, lanes), 1)
        kind, slot = (row // SLOTS) % 2, (row % SLOTS).astype(F32)
        expert = (row // m32 * 4 + chunk).astype(F32)
        named = jnp.zeros((size, lanes), F32)
        gate = jnp.zeros((size, lanes), F32)
        for k in range(topk):
            hit = chosen[k:k + 1, :] == expert
            named = jnp.where(hit, 1.0, named)
            gate = jnp.where(hit, chosen[topk + k:topk + k + 1, :] * (1.0 / 64.0), gate)
        rank = dot(named.astype(BF), earlier)
        here = jnp.where((rank == slot) & ((lane // 8) % 2 == kind), named, 0.0)
        weighted = jnp.where(kind == 1, here * gate, here).astype(BF)
        t2[block(chunk, size), :] = jnp.where(kind == 1, here, here * gate).astype(BF)
        snd[pl.ds(chunk * ec, ec)] = dot(weighted, tokens_here).astype(BF).reshape(ec, m32, d8)

        @pl.loop(0, ec)
        def _(n):
            p = n * 4 + chunk
            from_here = snd.at[chunk * ec + n]
            target = xr.at[q, core, local_group]

            @pl.when(jnp.logical_and(p == e, stays))
            def _():
                pltpu.make_async_copy(from_here, target, rsem.at[DISP + first]).start()

            @pl.when(jnp.logical_not(jnp.logical_and(p == e, stays)))
            def _():
                rcopy(from_here, target, DISP + first, (p, 2 * chip + (e // 4) % 2)).start()

    def order(k):
        return lax.rem(first + 4 - k, 4)

    def pass_rows(k):
        chunk = order(k)
        part = xr.at[q, :, pl.ds(chunk * gq, gq)]
        recv(part, DISP + chunk)
        rcopy(part, part, PAIR + k, row_dev).start()

    def pass_weights(n):
        there = n * (1 - q) + (1 - n) * q
        part = wt.at[there, :, :, block(2 * (1 - a) + core, hid)]
        recv(part, WX + n)
        rcopy(part, part, WF + n, (e, partner)).start()

    pass_rows(0)
    pass_rows(1)
    pass_weights(0)
    pass_rows(2)
    pass_weights(1)

    def products(quarter, chunk):
        value = [None] * 3
        for h in range(2):
            part = xr[quarter, h, pl.ds(chunk * gq, gq)]
            x_rows = part[:, :SLOTS].reshape(rows, d8)
            dy_rows = part[:, SLOTS:].reshape(rows, d8)
            for m in range(3):
                term = dot(dy_rows if m == 2 else x_rows, wt[quarter, h, m], NT)
                value[m] = term if h == 0 else value[m] + term
        return value

    def begin(k):
        chunk = order(k)
        for m, value in enumerate(products(q, chunk)):
            pf[chunk, :, m * half:(m + 1) * half] = value

    def finish(k):
        chunk = order(k)
        recv(xr.at[0, :, pl.ds(0, gq)], PAIR + k)
        for m, value in enumerate(products(1 - q, chunk)):
            span = slice(m * half, (m + 1) * half)
            pf[chunk, :, span] = pf[chunk, :, span] + value
        pb[chunk] = pf[chunk, block(1 - a, own_rows)].astype(BF)
        rcopy(pb.at[chunk], rs.at[chunk], PRE + k, weight_dev).start()

    def activate(k):
        chunk = order(k)
        recv(rs.at[chunk], PRE + k)
        total = pf[chunk, block(a, own_rows)] + rs[chunk].astype(F32)
        gate_pre, up_pre, back = total[:, :half], total[:, half:2 * half], total[:, 2 * half:]
        active, slope = silu_parts(gate_pre)
        act[chunk, a, :, :half] = (active * up_pre).astype(BF)
        act[chunk, a, :, half:2 * half] = (back * up_pre * slope).astype(BF)
        act[chunk, a, :, 2 * half:] = (back * active).astype(BF)
        rcopy(act.at[chunk, a], act.at[chunk, a], ACT + k, weight_dev).start()

    def results(quarter, h, chunk):
        left = act[chunk].reshape(rows, 3 * half)
        y = dot(left[:, :half], wt[quarter, h, 2])
        dx = dot(left[:, half:], wt[quarter, h, 0:2].reshape(2 * half, d8))
        return jnp.concatenate([y.reshape(gq, SLOTS, d8), dx.reshape(gq, SLOTS, d8)], axis=1)

    def answer(k):
        chunk = order(k)
        part = pl.ds(chunk * gq, gq)
        recv(act.at[chunk, 1 - a], ACT + k)
        rcopy(act.at[chunk], actp.at[chunk], ACTP, (e, partner)).start()
        for h in range(2):
            ps[h, part] = results(1 - q, h, chunk).astype(BF)
        rcopy(ps.at[:, part], pr.at[:, part], HALF + k, row_dev).start()
        for h in range(2):
            po[h, part] = results(q, h, chunk)

    def give_back(k):
        chunk = order(k)
        part = pl.ds(chunk * gq, gq)
        recv(pr.at[:, part], HALF + k)
        ret[:, part] = (po[:, part] + pr[:, part].astype(F32)).astype(BF)

        @pl.loop(0, gq)
        def _(n):
            place_here = chunk * gq + n
            p = 4 * (2 * n + core) + chunk
            for h in range(2):
                local = jnp.logical_and(p == e, core == h)

                @pl.when(local)
                def _():
                    pltpu.make_async_copy(ret.at[h, place_here], bk.at[home], rsem.at[BACK]).start()

                @pl.when(jnp.logical_not(local))
                def _():
                    rcopy(ret.at[h, place_here], bk.at[home], BACK, (p, 2 * chip + h)).start()

    for copy in own_weights:
        copy.wait()
    recv(wt.at[:, :, :, pl.ds(0, hid)], WPART)
    recv(wt.at[0, :, :, pl.ds(0, hid)], WF)
    for k in range(3):
        begin(k)
    recv(wt.at[0, :, :, pl.ds(0, hid)], WF + 1)
    finish(0)

    @pl.loop(1, chips)
    def _(k):
        rcopy(pair, g.at[block(t, 16)], TOKX, (e, lax.rem(t + 2 * k, nt))).start()

    pass_rows(3)
    activate(0)
    begin(3)
    finish(1)
    answer(0)
    activate(1)
    finish(2)

    recv(g.at[pl.ds(0, (chips - 1) * 16)], TOKX)

    @pl.loop(1, chips)
    def _(k):
        part = g.at[block(lax.rem(t + 2 * k, nt), 16)]
        rcopy(part, part, TOKP, (e, partner)).start()

    answer(1)
    activate(2)
    finish(3)
    rcopy(xr.at[:, 1 - core], xp, XP, (e, partner)).start()
    answer(2)
    activate(3)
    give_back(0)
    answer(3)

    recv(xp, XP)
    recv(actp, ACTP)
    own_grads = []

    def gradient(n, m):
        span = slice(0, half) if m == 2 else slice((m + 1) * half, (m + 2) * half)
        kind = slice(SLOTS, m32) if m == 2 else slice(0, SLOTS)
        here = act[:, :, :, span].reshape(4 * rows, half)
        there = actp[:, :, :, span].reshape(4 * rows, half)
        x_here = xr[n, core, :, kind].reshape(4 * rows, d8)
        x_there = xp[n, :, kind].reshape(4 * rows, d8)
        gb[n, m] = (dot(here, x_here, TN) + dot(there, x_there, TN)).astype(BF)
        target = (gout_ref if m == 2 else gin_ref.at[m]).at[:, cols(4 * a + 2 * n + core)]
        which = GRAD_OUT if m == 2 else GRAD_IN
        for c in range(2):
            rcopy(gb.at[n, m, block(2 * (1 - a) + c, hid)], target, which, (e, 2 * weight_chip + c)).start()
        rcopy(gb.at[n, m, block(2 * a + 1 - core, hid)], target, which, (e, partner)).start()
        own = pltpu.make_async_copy(gb.at[n, m, block(place, hid)], target, lsem.at[2 + 3 * n + m])
        own.start()
        own_grads.append(own)

    give_back(1)
    for m in range(3):
        gradient(0, m)
    give_back(2)
    for m in range(3):
        gradient(1, m)
    give_back(3)

    recv(g.at[pl.ds(0, chips * 16)], TOKP)
    for copy in own_shared:
        copy.wait()
    sh = sw_out.shape[0]

    def shared_step(n, sums):
        piece = g[:, cols(n)]
        return tuple(
            total + dot(piece, weight[:, cols(n)], NT)
            for total, weight in zip(sums, (sw_in.at[0], sw_in.at[1], sw_out)))

    zero = jnp.zeros((nt * 16, sh), F32)
    sums = lax.fori_loop(0, nt, shared_step, (zero, zero, zero))
    s_gate, s_up = [v.reshape(nt, 16, sh)[:, :8].reshape(nt * 8, sh) for v in sums[:2]]
    s_back = sums[2].reshape(nt, 16, sh)[:, 8:].reshape(nt * 8, sh)
    s_act, s_slope = silu_parts(s_gate)
    s_hidden = (s_act * s_up).astype(BF)
    s_dgate = (s_back * s_up * s_slope).astype(BF)
    s_dup = (s_back * s_act).astype(BF)

    def shared_terms(low, high):
        @pl.loop(low, high)
        def _(n):
            y = dot(s_hidden, sw_out[:, cols(n)]).reshape(nt, 8, d8)
            dx = (dot(s_dgate, sw_in[0, :, cols(n)]) + dot(s_dup, sw_in[1, :, cols(n)])).reshape(nt, 8, d8)
            shs[:, :, :, cols(n)] = jnp.concatenate([y, dx], axis=1).astype(BF).reshape(chips, 2, 16, d8)

    shared_terms(0, nt)
    rcopy(shs.at[:, 1 - core], shp, SHP, (e, partner)).start()
    recv(shp, SHP)
    for n in range(chips):
        shs[n, core] = (shs[n, core].astype(F32) + shp[n].astype(F32)).astype(BF)

    @pl.loop(1, chips)
    def _(k):
        j = lax.rem(chip + k, chips)
        rcopy(shs.at[j, core], shr.at[chip], SHARED, (e, 2 * j + core)).start()


    recv(bk, BACK)
    routed = dot(t2[...], bk[...].reshape(ne * m32, d8), TN)
    fs[...] = routed.astype(BF).reshape(nt, 16, d8)

    @pl.loop(1, nt)
    def _(k):
        p = lax.rem(t + k, nt)
        rcopy(fs.at[p], fr.at[t], FINAL, (e, p)).start()

    fr[t] = fs[t]
    shr[chip] = shs[chip, core]
    recv(shr.at[pl.ds(0, chips - 1)], SHARED)
    recv(fr.at[pl.ds(0, nt - 1)], FINAL)

    for n in range(nt):
        span = slice(n * d8, (n + 1) * d8)
        total = fr[n].astype(F32) + jnp.sum(shr[:, :, span].astype(F32), axis=0)
        out_ref[:, span] = total[:8].astype(BF)
        gtok_ref[:, span] = total[8:].astype(BF)

    recv(gin_ref.at[:, :, pl.ds(0, 6 * d8)], GRAD_IN)
    recv(gout_ref.at[:, pl.ds(0, 6 * d8)], GRAD_OUT)
    for copy in own_grads:
        copy.wait()
    sent(tabs.at[pl.ds(0, (nt - 1) * 16)], TAB)
    sent(gs.at[pl.ds(0, (nt - 1) * 16)], SLICE)
    sent(g.at[pl.ds(0, (chips - 1) * 16)], TOKX)
    sent(g.at[pl.ds(0, chips * 16)], TOKP)
    sent(wt.at[:, :, :, pl.ds(0, hid)], WPART)
    for n in range(2):
        sent(wt.at[n, :, :, pl.ds(0, hid)], WX + n)
        sent(wt.at[n, :, :, pl.ds(0, hid)], WF + n)
    for k in range(4):
        sent(xr.at[0, :, pl.ds(0, gq)], PAIR + k)
        sent(ps.at[:, pl.ds(0, gq)], HALF + k)
    sent(xp, XP)
    for k in range(4):
        sent(rs.at[0], PRE + k)
        sent(rs.at[0], ACT + k)
    sent(actp, ACTP)
    sent(shp, SHP)
    sent(shr.at[pl.ds(0, chips - 1)], SHARED)
    sent(gin_ref.at[:, :, pl.ds(0, 6 * d8)], GRAD_IN)
    sent(gout_ref.at[:, pl.ds(0, 6 * d8)], GRAD_OUT)
    sent(fs.at[pl.ds(0, nt - 1)], FINAL)

    @pl.when(stays)
    def _():
        sent(bk.at[pl.ds(0, ne - 1)], BACK)
        sent(bk.at[pl.ds(0, ne - 1)], DISP + first)

    @pl.when(jnp.logical_not(stays))
    def _():
        sent(bk, BACK)
        sent(bk, DISP + first)


def hand_over(out_a, gtok_a, gin_a, gout_a, out_b, gtok_b, gin_b, gout_b, small, big, sem):
    hid = gout_a.shape[0]
    part = hid // 2
    moves = []
    for m in range(3):
        left, right = (gout_a, gout_b) if m == 2 else (gin_a.at[m], gin_b.at[m])
        for n in range(2):
            rows = pl.ds(n * part, part)
            moves.append((left.at[rows], big.at[m, rows], right.at[rows]))
    moves += [(out_a, small.at[0], out_b), (gtok_a, small.at[1], gtok_b)]
    inward = [pltpu.make_async_copy(src, mid, sem.at[0, n]) for n, (src, mid, _) in enumerate(moves)]
    outward = [pltpu.make_async_copy(mid, dst, sem.at[1, n]) for n, (_, mid, dst) in enumerate(moves)]
    for copy in inward:
        copy.start()
    for before, after in zip(inward, outward):
        before.wait()
        after.start()
    for copy in outward:
        copy.wait()


def on_device(tokens, routes, gate_num, cotangent, w_in, w_out, shared_in, shared_out):
    ne, nt = lax.axis_size("expert"), lax.axis_size("tensor")
    chips = nt // 2
    own, features = tokens.shape
    topk = routes.shape[1]
    hid, sh = w_out.shape[1], shared_out.shape[0]
    d8, half, gl_count = features // nt, 4 * hid, ne // 2
    rows, m32 = gl_count * SLOTS // 4, 2 * SLOTS
    vm = pl.BlockSpec(memory_space=pltpu.VMEM)
    hbm = pl.BlockSpec(memory_space=pl.ANY)
    scratch = [
        pltpu.VMEM((16, features), BF),
        pltpu.VMEM((16, 128), jnp.int32),
        pltpu.VMEM((nt * 16, 128), jnp.int32),
        pltpu.VMEM((nt * 16, d8), BF),
        pltpu.VMEM((nt * 16, features), BF),
        pltpu.VMEM((2, 2, 3, half, d8), BF),
        pltpu.VMEM((2, sh, features), BF),
        pltpu.VMEM((sh, features), BF),
        pltpu.VMEM((ne * m32, nt * 16), BF),
        pltpu.VMEM((ne, m32, d8), BF),
        pltpu.VMEM((2, 2, gl_count, m32, d8), BF),
        pltpu.VMEM((2, gl_count, m32, d8), BF),
        pltpu.VMEM((4, rows, 3 * half), F32),
        pltpu.VMEM((4, rows // 2, 3 * half), BF),
        pltpu.VMEM((4, rows // 2, 3 * half), BF),
        pltpu.VMEM((4, 2, rows // 2, 3 * half), BF),
        pltpu.VMEM((4, 2, rows // 2, 3 * half), BF),
        pltpu.VMEM((2, gl_count, m32, d8), BF),
        pltpu.VMEM((2, gl_count, m32, d8), BF),
        pltpu.VMEM((2, gl_count, m32, d8), F32),
        pltpu.VMEM((2, gl_count, m32, d8), BF),
        pltpu.VMEM((ne, m32, d8), BF),
        pltpu.VMEM((2, 3, half, d8), BF),
        pltpu.VMEM((chips, 2, 16, features), BF),
        pltpu.VMEM((chips, 16, features), BF),
        pltpu.VMEM((chips, 16, features), BF),
        pltpu.VMEM((nt, 16, d8), BF),
        pltpu.VMEM((nt, 16, d8), BF),
        pltpu.SemaphoreType.DMA((COUNT,)),
        pltpu.SemaphoreType.DMA((COUNT,)),
        pltpu.SemaphoreType.DMA((14,)),
    ]
    shapes = (
        jax.ShapeDtypeStruct((own, features), BF),
        jax.ShapeDtypeStruct((own, features), BF),
        jax.ShapeDtypeStruct((2, hid, features), BF),
        jax.ShapeDtypeStruct((hid, features), BF),
    )
    results = pl.pallas_call(
        functools.partial(kernel, topk),
        out_shape=shapes,
        in_specs=[vm, vm, vm, vm, hbm, hbm, hbm, hbm],
        out_specs=(vm, vm, hbm, hbm),
        scratch_shapes=scratch,
        compiler_params=pltpu.CompilerParams(
            collective_id=0, has_side_effects=True, vmem_limit_bytes=56 * 2**20
        ),
    )(tokens, cotangent, routes, gate_num, w_in[0], w_out[0], shared_in, shared_out)
    out, gtok, gin, gout = pl.pallas_call(
        hand_over,
        out_shape=shapes,
        in_specs=[hbm] * 4,
        out_specs=(hbm,) * 4,
        scratch_shapes=[
            pltpu.VMEM((2, own, features), BF),
            pltpu.VMEM((3, hid, features), BF),
            pltpu.SemaphoreType.DMA((2, 8)),
        ],
        compiler_params=pltpu.CompilerParams(vmem_limit_bytes=60 * 2**20),
    )(*results)
    return out, gtok, gin[None], gout[None]


def solution(mesh):
    in_specs = (
        P(("expert", "tensor"), None),
        P(("expert", "tensor"), None),
        P(("expert", "tensor"), None),
        P(("expert", "tensor"), None),
        P("expert", None, "tensor", None),
        P("expert", "tensor", None),
        P(None, "tensor", None),
        P("tensor", None),
    )
    out_specs = (
        P(("expert", "tensor"), None),
        P(("expert", "tensor"), None),
        P("expert", None, "tensor", None),
        P("expert", "tensor", None),
    )
    return jax.shard_map(
        on_device, mesh=mesh, in_specs=in_specs, out_specs=out_specs, check_vma=False
    )
```

```python
import functools

import jax
import jax.numpy as jnp
from jax import lax
from jax.experimental import pallas as pl
from jax.experimental.pallas import tpu as pltpu
from jax.sharding import PartitionSpec as P

MESH = pl.DeviceIdType.MESH
BF = jnp.bfloat16
F32 = jnp.float32
SLOTS = 16
NT = (((1,), (1,)), ((), ()))
TN = (((0,), (0,)), ((), ()))

TAB, SLICE, TOKX, TOKP, WPART, XP, ACTP, BACK, GRAD_IN, GRAD_OUT, SHP, SHARED, FINAL = range(13)
PRE, ACT, WX, WF, DISP, PAIR, HALF = 13, 17, 21, 23, 25, 29, 33
COUNT = 37


def dot(left, right, dims=None):
    dims = dims or (((1,), (0,)), ((), ()))
    return lax.dot_general(left, right, dims, preferred_element_type=F32)


def silu_parts(preact):
    sig_value = jax.nn.sigmoid(preact)
    return preact * sig_value, sig_value * (1.0 + preact * (1.0 - sig_value))


def kernel(
    topk,
    tok_ref, cot_ref, routes_ref, gates_ref, w_in, w_out, sh_in, sh_out,
    out_ref, gtok_ref, gin_ref, gout_ref,
    pair, table, tabs, gs, g, wt, sw_in, sw_out, t2, snd, xr, xp, pf, pb, rs, act, actp, ps, pr, po, ret, bk, gb,
    shs, shp, shr, fs, fr, ssem, rsem, lsem,
):
    ne, nt = lax.axis_size("expert"), lax.axis_size("tensor")
    e, t = lax.axis_index("expert"), lax.axis_index("tensor")
    chip, core = t // 2, t % 2
    chips = nt // 2
    a, q = chip // 2, chip % 2
    partner = t + 1 - 2 * core
    row_chip = 2 * a + 1 - q
    weight_chip = chips - 1 - chip
    row_dev, weight_dev = (e, 2 * row_chip + core), (e, 2 * weight_chip + core)
    first = e % 4
    stays = (e // 4) % 2 == core
    home = (e % 4) * (ne // 4) + e // 4
    local_group = (e % 4) * (ne // 8) + e // 8
    d8 = gs.shape[1]
    hid = w_out.shape[0]
    half = 4 * hid
    gl_count = ne // 2
    gq = gl_count // 4
    rows = gq * SLOTS
    own_rows = rows // 2
    m32 = 2 * SLOTS

    def rcopy(src, dst, which, dev):
        return pltpu.make_async_remote_copy(
            src_ref=src, dst_ref=dst, send_sem=ssem.at[which], recv_sem=rsem.at[which],
            device_id=dev, device_id_type=MESH,
        )

    def recv(ref, which):
        pltpu.make_async_copy(ref, ref, rsem.at[which]).wait()

    def sent(ref, which):
        pltpu.make_async_copy(ref, ref, ssem.at[which]).wait()

    def cols(piece):
        return pl.ds(pl.multiple_of(piece * d8, 128), d8)

    def block(index, size):
        return pl.ds(pl.multiple_of(index * size, 16), size)

    def source(m):
        return w_out if m == 2 else w_in.at[m]

    place = 2 * a + core
    own_shared = [
        pltpu.make_async_copy(sh_in, sw_in, lsem.at[0]),
        pltpu.make_async_copy(sh_out, sw_out, lsem.at[1]),
    ]
    own_weights = [
        pltpu.make_async_copy(
            source(m).at[:, cols(4 * a + 2 * n + h)], wt.at[n, h, m, block(place, hid)], lsem.at[2 + 6 * n + 3 * h + m])
        for n in range(2) for h in range(2) for m in range(3)]

    barrier = pltpu.get_barrier_semaphore()

    @pl.loop(1, nt)
    def _(k):
        pl.semaphore_signal(barrier, inc=1, device_id=(e, lax.rem(t + k, nt)), device_id_type=MESH)

    @pl.loop(1, ne)
    def _(k):
        for h in range(2):
            pl.semaphore_signal(barrier, inc=1, device_id=(lax.rem(e + k, ne), 2 * chip + h), device_id_type=MESH)

    for copy in own_weights + own_shared:
        copy.start()
    for n in range(nt):
        span = slice(n * d8, (n + 1) * d8)
        pair[:, span] = jnp.concatenate(
            [tok_ref[:, span].astype(F32), cot_ref[:, span].astype(F32)], axis=0).astype(BF)
    table[...] = jnp.zeros_like(table)
    for n in range(2):
        table[8 * n:8 * n + 8, :topk] = routes_ref[...]
        table[8 * n:8 * n + 8, topk:2 * topk] = gates_ref[...]

    pl.semaphore_wait(barrier, 2 * (ne - 1) + nt - 1)

    @pl.loop(1, nt)
    def _(k):
        p = lax.rem(t + k, nt)
        rcopy(table, tabs.at[block(t, 16)], TAB, (e, p)).start()
        rcopy(pair.at[:, cols(p)], gs.at[block(t, 16)], SLICE, (e, p)).start()

    for n in range(2):
        there = n * q + (1 - n) * (1 - q)
        for h in range(2):
            for m in range(3):
                rcopy(source(m).at[:, cols(4 * (1 - a) + 2 * there + h)], wt.at[there, h, m, block(place, hid)],
                      WX + n, weight_dev).start()
    for n in range(2):
        for h in range(2):
            for m in range(3):
                rcopy(source(m).at[:, cols(4 * a + 2 * n + h)], wt.at[n, h, m, block(place, hid)],
                      WPART, (e, partner)).start()

    rcopy(pair, g.at[block(t, 16)], TOKP, (e, partner)).start()

    tabs[block(t, 16), :] = table[...]
    gs[block(t, 16), :] = pair[:, cols(t)]
    g[block(t, 16), :] = pair[...]

    recv(tabs.at[pl.ds(0, (nt - 1) * 16)], TAB)
    lanes = nt * 16
    chosen = tabs[...].astype(F32).T
    lane_a = lax.broadcasted_iota(jnp.int32, (lanes, lanes), 0)
    lane_b = lax.broadcasted_iota(jnp.int32, (lanes, lanes), 1)
    token_a, token_b = (lane_a // 16) * 8 + lane_a % 8, (lane_b // 16) * 8 + lane_b % 8
    earlier = jnp.where((lane_a % 16 < 8) & (token_a < token_b), 1.0, 0.0).astype(BF)
    recv(gs.at[pl.ds(0, (nt - 1) * 16)], SLICE)
    tokens_here = gs[...]
    ec = ne // 4
    size = ec * m32
    for turn in range(4):
        chunk = lax.rem(first + turn, 4)
        row = lax.broadcasted_iota(jnp.int32, (size, lanes), 0)
        lane = lax.broadcasted_iota(jnp.int32, (size, lanes), 1)
        kind, slot = (row // SLOTS) % 2, (row % SLOTS).astype(F32)
        expert = (row // m32 * 4 + chunk).astype(F32)
        named = jnp.zeros((size, lanes), F32)
        gate = jnp.zeros((size, lanes), F32)
        for k in range(topk):
            hit = chosen[k:k + 1, :] == expert
            named = jnp.where(hit, 1.0, named)
            gate = jnp.where(hit, chosen[topk + k:topk + k + 1, :] * (1.0 / 64.0), gate)
        rank = dot(named.astype(BF), earlier)
        here = jnp.where((rank == slot) & ((lane // 8) % 2 == kind), named, 0.0)
        weighted = jnp.where(kind == 1, here * gate, here).astype(BF)
        t2[block(chunk, size), :] = jnp.where(kind == 1, here, here * gate).astype(BF)
        snd[pl.ds(chunk * ec, ec)] = dot(weighted, tokens_here).astype(BF).reshape(ec, m32, d8)

        @pl.loop(0, ec)
        def _(n):
            p = n * 4 + chunk
            from_here = snd.at[chunk * ec + n]
            target = xr.at[q, core, local_group]

            @pl.when(jnp.logical_and(p == e, stays))
            def _():
                pltpu.make_async_copy(from_here, target, rsem.at[DISP + first]).start()

            @pl.when(jnp.logical_not(jnp.logical_and(p == e, stays)))
            def _():
                rcopy(from_here, target, DISP + first, (p, 2 * chip + (e // 4) % 2)).start()

    def order(k):
        return lax.rem(first + 4 - k, 4)

    def pass_rows(k):
        chunk = order(k)
        part = xr.at[q, :, pl.ds(chunk * gq, gq)]
        recv(part, DISP + chunk)
        rcopy(part, part, PAIR + k, row_dev).start()

    def pass_weights(n):
        there = n * (1 - q) + (1 - n) * q
        part = wt.at[there, :, :, block(2 * (1 - a) + core, hid)]
        recv(part, WX + n)
        rcopy(part, part, WF + n, (e, partner)).start()

    pass_rows(0)
    pass_rows(1)
    pass_weights(0)
    pass_rows(2)
    pass_weights(1)

    def products(quarter, chunk):
        value = [None] * 3
        for h in range(2):
            part = xr[quarter, h, pl.ds(chunk * gq, gq)]
            x_rows = part[:, :SLOTS].reshape(rows, d8)
            dy_rows = part[:, SLOTS:].reshape(rows, d8)
            for m in range(3):
                term = dot(dy_rows if m == 2 else x_rows, wt[quarter, h, m], NT)
                value[m] = term if h == 0 else value[m] + term
        return value

    def begin(k):
        chunk = order(k)
        for m, value in enumerate(products(q, chunk)):
            pf[chunk, :, m * half:(m + 1) * half] = value

    def finish(k):
        chunk = order(k)
        recv(xr.at[0, :, pl.ds(0, gq)], PAIR + k)
        for m, value in enumerate(products(1 - q, chunk)):
            span = slice(m * half, (m + 1) * half)
            pf[chunk, :, span] = pf[chunk, :, span] + value
        pb[chunk] = pf[chunk, block(1 - a, own_rows)].astype(BF)
        rcopy(pb.at[chunk], rs.at[chunk], PRE + k, weight_dev).start()

    def activate(k):
        chunk = order(k)
        recv(rs.at[chunk], PRE + k)
        total = pf[chunk, block(a, own_rows)] + rs[chunk].astype(F32)
        gate_pre, up_pre, back = total[:, :half], total[:, half:2 * half], total[:, 2 * half:]
        active, slope = silu_parts(gate_pre)
        act[chunk, a, :, :half] = (active * up_pre).astype(BF)
        act[chunk, a, :, half:2 * half] = (back * up_pre * slope).astype(BF)
        act[chunk, a, :, 2 * half:] = (back * active).astype(BF)
        rcopy(act.at[chunk, a], act.at[chunk, a], ACT + k, weight_dev).start()

    def results(quarter, h, chunk):
        left = act[chunk].reshape(rows, 3 * half)
        y = dot(left[:, :half], wt[quarter, h, 2])
        dx = dot(left[:, half:], wt[quarter, h, 0:2].reshape(2 * half, d8))
        return jnp.concatenate([y.reshape(gq, SLOTS, d8), dx.reshape(gq, SLOTS, d8)], axis=1)

    def answer(k):
        chunk = order(k)
        part = pl.ds(chunk * gq, gq)
        recv(act.at[chunk, 1 - a], ACT + k)
        rcopy(act.at[chunk], actp.at[chunk], ACTP, (e, partner)).start()
        for h in range(2):
            ps[h, part] = results(1 - q, h, chunk).astype(BF)
        rcopy(ps.at[:, part], pr.at[:, part], HALF + k, row_dev).start()
        for h in range(2):
            po[h, part] = results(q, h, chunk)

    def give_back(k):
        chunk = order(k)
        part = pl.ds(chunk * gq, gq)
        recv(pr.at[:, part], HALF + k)
        ret[:, part] = (po[:, part] + pr[:, part].astype(F32)).astype(BF)

        @pl.loop(0, gq)
        def _(n):
            place_here = chunk * gq + n
            p = 4 * (2 * n + core) + chunk
            for h in range(2):
                local = jnp.logical_and(p == e, core == h)

                @pl.when(local)
                def _():
                    pltpu.make_async_copy(ret.at[h, place_here], bk.at[home], rsem.at[BACK]).start()

                @pl.when(jnp.logical_not(local))
                def _():
                    rcopy(ret.at[h, place_here], bk.at[home], BACK, (p, 2 * chip + h)).start()

    for copy in own_weights:
        copy.wait()
    recv(wt.at[:, :, :, pl.ds(0, hid)], WPART)
    recv(wt.at[0, :, :, pl.ds(0, hid)], WF)
    for k in range(3):
        begin(k)
    recv(wt.at[0, :, :, pl.ds(0, hid)], WF + 1)
    finish(0)

    @pl.loop(1, chips)
    def _(k):
        rcopy(pair, g.at[block(t, 16)], TOKX, (e, lax.rem(t + 2 * k, nt))).start()

    pass_rows(3)
    activate(0)
    begin(3)
    finish(1)
    answer(0)
    activate(1)
    finish(2)

    recv(g.at[pl.ds(0, (chips - 1) * 16)], TOKX)

    @pl.loop(1, chips)
    def _(k):
        part = g.at[block(lax.rem(t + 2 * k, nt), 16)]
        rcopy(part, part, TOKP, (e, partner)).start()

    answer(1)
    activate(2)
    finish(3)
    rcopy(xr.at[:, 1 - core], xp, XP, (e, partner)).start()
    answer(2)
    activate(3)
    give_back(0)
    answer(3)

    recv(xp, XP)
    recv(actp, ACTP)
    own_grads = []

    def gradient(n, m):
        span = slice(0, half) if m == 2 else slice((m + 1) * half, (m + 2) * half)
        kind = slice(SLOTS, m32) if m == 2 else slice(0, SLOTS)
        here = act[:, :, :, span].reshape(4 * rows, half)
        there = actp[:, :, :, span].reshape(4 * rows, half)
        x_here = xr[n, core, :, kind].reshape(4 * rows, d8)
        x_there = xp[n, :, kind].reshape(4 * rows, d8)
        gb[n, m] = (dot(here, x_here, TN) + dot(there, x_there, TN)).astype(BF)
        target = (gout_ref if m == 2 else gin_ref.at[m]).at[:, cols(4 * a + 2 * n + core)]
        which = GRAD_OUT if m == 2 else GRAD_IN
        for c in range(2):
            rcopy(gb.at[n, m, block(2 * (1 - a) + c, hid)], target, which, (e, 2 * weight_chip + c)).start()
        rcopy(gb.at[n, m, block(2 * a + 1 - core, hid)], target, which, (e, partner)).start()
        own = pltpu.make_async_copy(gb.at[n, m, block(place, hid)], target, lsem.at[2 + 3 * n + m])
        own.start()
        own_grads.append(own)

    for n in range(2):
        for m in range(3):
            gradient(n, m)
    give_back(1)

    recv(g.at[pl.ds(0, chips * 16)], TOKP)
    for copy in own_shared:
        copy.wait()
    sh = sw_out.shape[0]

    def shared_step(n, sums):
        piece = g[:, cols(n)]
        return tuple(
            total + dot(piece, weight[:, cols(n)], NT)
            for total, weight in zip(sums, (sw_in.at[0], sw_in.at[1], sw_out)))

    zero = jnp.zeros((nt * 16, sh), F32)
    sums = lax.fori_loop(0, nt, shared_step, (zero, zero, zero))
    s_gate, s_up = [v.reshape(nt, 16, sh)[:, :8].reshape(nt * 8, sh) for v in sums[:2]]
    s_back = sums[2].reshape(nt, 16, sh)[:, 8:].reshape(nt * 8, sh)
    s_act, s_slope = silu_parts(s_gate)
    s_hidden = (s_act * s_up).astype(BF)
    s_dgate = (s_back * s_up * s_slope).astype(BF)
    s_dup = (s_back * s_act).astype(BF)

    def shared_terms(low, high):
        @pl.loop(low, high)
        def _(n):
            y = dot(s_hidden, sw_out[:, cols(n)]).reshape(nt, 8, d8)
            dx = (dot(s_dgate, sw_in[0, :, cols(n)]) + dot(s_dup, sw_in[1, :, cols(n)])).reshape(nt, 8, d8)
            shs[:, :, :, cols(n)] = jnp.concatenate([y, dx], axis=1).astype(BF).reshape(chips, 2, 16, d8)

    give_back(2)
    shared_terms(0, nt)
    rcopy(shs.at[:, 1 - core], shp, SHP, (e, partner)).start()
    give_back(3)
    recv(shp, SHP)
    for n in range(chips):
        shs[n, core] = (shs[n, core].astype(F32) + shp[n].astype(F32)).astype(BF)

    @pl.loop(1, chips)
    def _(k):
        j = lax.rem(chip + k, chips)
        rcopy(shs.at[j, core], shr.at[chip], SHARED, (e, 2 * j + core)).start()


    recv(bk, BACK)
    routed = dot(t2[...], bk[...].reshape(ne * m32, d8), TN)
    fs[...] = routed.astype(BF).reshape(nt, 16, d8)

    @pl.loop(1, nt)
    def _(k):
        p = lax.rem(t + k, nt)
        rcopy(fs.at[p], fr.at[t], FINAL, (e, p)).start()

    fr[t] = fs[t]
    shr[chip] = shs[chip, core]
    recv(shr.at[pl.ds(0, chips - 1)], SHARED)
    recv(fr.at[pl.ds(0, nt - 1)], FINAL)

    for n in range(nt):
        span = slice(n * d8, (n + 1) * d8)
        total = fr[n].astype(F32) + jnp.sum(shr[:, :, span].astype(F32), axis=0)
        out_ref[:, span] = total[:8].astype(BF)
        gtok_ref[:, span] = total[8:].astype(BF)

    recv(gin_ref.at[:, :, pl.ds(0, 6 * d8)], GRAD_IN)
    recv(gout_ref.at[:, pl.ds(0, 6 * d8)], GRAD_OUT)
    for copy in own_grads:
        copy.wait()
    sent(tabs.at[pl.ds(0, (nt - 1) * 16)], TAB)
    sent(gs.at[pl.ds(0, (nt - 1) * 16)], SLICE)
    sent(g.at[pl.ds(0, (chips - 1) * 16)], TOKX)
    sent(g.at[pl.ds(0, chips * 16)], TOKP)
    sent(wt.at[:, :, :, pl.ds(0, hid)], WPART)
    for n in range(2):
        sent(wt.at[n, :, :, pl.ds(0, hid)], WX + n)
        sent(wt.at[n, :, :, pl.ds(0, hid)], WF + n)
    for k in range(4):
        sent(xr.at[0, :, pl.ds(0, gq)], PAIR + k)
        sent(ps.at[:, pl.ds(0, gq)], HALF + k)
    sent(xp, XP)
    for k in range(4):
        sent(rs.at[0], PRE + k)
        sent(rs.at[0], ACT + k)
    sent(actp, ACTP)
    sent(shp, SHP)
    sent(shr.at[pl.ds(0, chips - 1)], SHARED)
    sent(gin_ref.at[:, :, pl.ds(0, 6 * d8)], GRAD_IN)
    sent(gout_ref.at[:, pl.ds(0, 6 * d8)], GRAD_OUT)
    sent(fs.at[pl.ds(0, nt - 1)], FINAL)

    @pl.when(stays)
    def _():
        sent(bk.at[pl.ds(0, ne - 1)], BACK)
        sent(bk.at[pl.ds(0, ne - 1)], DISP + first)

    @pl.when(jnp.logical_not(stays))
    def _():
        sent(bk, BACK)
        sent(bk, DISP + first)


def hand_over(out_a, gtok_a, gin_a, gout_a, out_b, gtok_b, gin_b, gout_b, small, big, sem):
    hid = gout_a.shape[0]
    part = hid // 2
    moves = []
    for m in range(3):
        left, right = (gout_a, gout_b) if m == 2 else (gin_a.at[m], gin_b.at[m])
        for n in range(2):
            rows = pl.ds(n * part, part)
            moves.append((left.at[rows], big.at[m, rows], right.at[rows]))
    moves += [(out_a, small.at[0], out_b), (gtok_a, small.at[1], gtok_b)]
    inward = [pltpu.make_async_copy(src, mid, sem.at[0, n]) for n, (src, mid, _) in enumerate(moves)]
    outward = [pltpu.make_async_copy(mid, dst, sem.at[1, n]) for n, (_, mid, dst) in enumerate(moves)]
    for copy in inward:
        copy.start()
    for before, after in zip(inward, outward):
        before.wait()
        after.start()
    for copy in outward:
        copy.wait()


def on_device(tokens, routes, gate_num, cotangent, w_in, w_out, shared_in, shared_out):
    ne, nt = lax.axis_size("expert"), lax.axis_size("tensor")
    chips = nt // 2
    own, features = tokens.shape
    topk = routes.shape[1]
    hid, sh = w_out.shape[1], shared_out.shape[0]
    d8, half, gl_count = features // nt, 4 * hid, ne // 2
    rows, m32 = gl_count * SLOTS // 4, 2 * SLOTS
    vm = pl.BlockSpec(memory_space=pltpu.VMEM)
    hbm = pl.BlockSpec(memory_space=pl.ANY)
    scratch = [
        pltpu.VMEM((16, features), BF),
        pltpu.VMEM((16, 128), jnp.int32),
        pltpu.VMEM((nt * 16, 128), jnp.int32),
        pltpu.VMEM((nt * 16, d8), BF),
        pltpu.VMEM((nt * 16, features), BF),
        pltpu.VMEM((2, 2, 3, half, d8), BF),
        pltpu.VMEM((2, sh, features), BF),
        pltpu.VMEM((sh, features), BF),
        pltpu.VMEM((ne * m32, nt * 16), BF),
        pltpu.VMEM((ne, m32, d8), BF),
        pltpu.VMEM((2, 2, gl_count, m32, d8), BF),
        pltpu.VMEM((2, gl_count, m32, d8), BF),
        pltpu.VMEM((4, rows, 3 * half), F32),
        pltpu.VMEM((4, rows // 2, 3 * half), BF),
        pltpu.VMEM((4, rows // 2, 3 * half), BF),
        pltpu.VMEM((4, 2, rows // 2, 3 * half), BF),
        pltpu.VMEM((4, 2, rows // 2, 3 * half), BF),
        pltpu.VMEM((2, gl_count, m32, d8), BF),
        pltpu.VMEM((2, gl_count, m32, d8), BF),
        pltpu.VMEM((2, gl_count, m32, d8), F32),
        pltpu.VMEM((2, gl_count, m32, d8), BF),
        pltpu.VMEM((ne, m32, d8), BF),
        pltpu.VMEM((2, 3, half, d8), BF),
        pltpu.VMEM((chips, 2, 16, features), BF),
        pltpu.VMEM((chips, 16, features), BF),
        pltpu.VMEM((chips, 16, features), BF),
        pltpu.VMEM((nt, 16, d8), BF),
        pltpu.VMEM((nt, 16, d8), BF),
        pltpu.SemaphoreType.DMA((COUNT,)),
        pltpu.SemaphoreType.DMA((COUNT,)),
        pltpu.SemaphoreType.DMA((14,)),
    ]
    shapes = (
        jax.ShapeDtypeStruct((own, features), BF),
        jax.ShapeDtypeStruct((own, features), BF),
        jax.ShapeDtypeStruct((2, hid, features), BF),
        jax.ShapeDtypeStruct((hid, features), BF),
    )
    results = pl.pallas_call(
        functools.partial(kernel, topk),
        out_shape=shapes,
        in_specs=[vm, vm, vm, vm, hbm, hbm, hbm, hbm],
        out_specs=(vm, vm, hbm, hbm),
        scratch_shapes=scratch,
        compiler_params=pltpu.CompilerParams(
            collective_id=0, has_side_effects=True, vmem_limit_bytes=56 * 2**20
        ),
    )(tokens, cotangent, routes, gate_num, w_in[0], w_out[0], shared_in, shared_out)
    out, gtok, gin, gout = pl.pallas_call(
        hand_over,
        out_shape=shapes,
        in_specs=[hbm] * 4,
        out_specs=(hbm,) * 4,
        scratch_shapes=[
            pltpu.VMEM((2, own, features), BF),
            pltpu.VMEM((3, hid, features), BF),
            pltpu.SemaphoreType.DMA((2, 8)),
        ],
        compiler_params=pltpu.CompilerParams(vmem_limit_bytes=60 * 2**20),
    )(*results)
    return out, gtok, gin[None], gout[None]


def solution(mesh):
    in_specs = (
        P(("expert", "tensor"), None),
        P(("expert", "tensor"), None),
        P(("expert", "tensor"), None),
        P(("expert", "tensor"), None),
        P("expert", None, "tensor", None),
        P("expert", "tensor", None),
        P(None, "tensor", None),
        P("tensor", None),
    )
    out_specs = (
        P(("expert", "tensor"), None),
        P(("expert", "tensor"), None),
        P("expert", None, "tensor", None),
        P("expert", "tensor", None),
    )
    return jax.shard_map(
        on_device, mesh=mesh, in_specs=in_specs, out_specs=out_specs, check_vma=False
    )
```

```python
import functools

import jax
import jax.numpy as jnp
from jax import lax
from jax.experimental import pallas as pl
from jax.experimental.pallas import tpu as pltpu
from jax.sharding import PartitionSpec as P

MESH = pl.DeviceIdType.MESH
BF = jnp.bfloat16
F32 = jnp.float32
SLOTS = 16
NT = (((1,), (1,)), ((), ()))
TN = (((0,), (0,)), ((), ()))

TAB, SLICE, TOKX, TOKP, WPART, XP, ACTP, BACK, GRAD_IN, GRAD_OUT, SHP, SHARED, FINAL = range(13)
PRE, ACT, WX, WF, DISP, PAIR, HALF = 13, 17, 21, 23, 25, 29, 33
SUMS = 37
COUNT = 38


def dot(left, right, dims=None):
    dims = dims or (((1,), (0,)), ((), ()))
    return lax.dot_general(left, right, dims, preferred_element_type=F32)


def silu_parts(preact):
    sig_value = jax.nn.sigmoid(preact)
    return preact * sig_value, sig_value * (1.0 + preact * (1.0 - sig_value))


def kernel(
    topk,
    tok_ref, cot_ref, routes_ref, gates_ref, w_in, w_out, sh_in, sh_out,
    out_ref, gtok_ref, gin_ref, gout_ref,
    pair, table, tabs, gs, g, wt, sw_in, sw_out, t2, snd, xr, xp, pf, pb, rs, act, actp, ps, pr, po, ret, bk, gb,
    shs, shp, shr, fs, fr, ssem, rsem, lsem,
):
    ne, nt = lax.axis_size("expert"), lax.axis_size("tensor")
    e, t = lax.axis_index("expert"), lax.axis_index("tensor")
    chip, core = t // 2, t % 2
    chips = nt // 2
    a, q = chip // 2, chip % 2
    partner = t + 1 - 2 * core
    row_chip = 2 * a + 1 - q
    weight_chip = chips - 1 - chip
    row_dev, weight_dev = (e, 2 * row_chip + core), (e, 2 * weight_chip + core)
    first = e % 4
    stays = (e // 4) % 2 == core
    home = (e % 4) * (ne // 4) + e // 4
    local_group = (e % 4) * (ne // 8) + e // 8
    d8 = gs.shape[1]
    hid = w_out.shape[0]
    half = 4 * hid
    gl_count = ne // 2
    gq = gl_count // 4
    rows = gq * SLOTS
    own_rows = rows // 2
    m32 = 2 * SLOTS

    def rcopy(src, dst, which, dev):
        return pltpu.make_async_remote_copy(
            src_ref=src, dst_ref=dst, send_sem=ssem.at[which], recv_sem=rsem.at[which],
            device_id=dev, device_id_type=MESH,
        )

    def recv(ref, which):
        pltpu.make_async_copy(ref, ref, rsem.at[which]).wait()

    def sent(ref, which):
        pltpu.make_async_copy(ref, ref, ssem.at[which]).wait()

    def cols(piece):
        return pl.ds(pl.multiple_of(piece * d8, 128), d8)

    def block(index, size):
        return pl.ds(pl.multiple_of(index * size, 16), size)

    def source(m):
        return w_out if m == 2 else w_in.at[m]

    place = 2 * a + core
    own_shared = [
        pltpu.make_async_copy(sh_in, sw_in, lsem.at[0]),
        pltpu.make_async_copy(sh_out, sw_out, lsem.at[1]),
    ]
    own_weights = [
        pltpu.make_async_copy(
            source(m).at[:, cols(4 * a + 2 * n + h)], wt.at[n, h, m, block(place, hid)], lsem.at[2 + 6 * n + 3 * h + m])
        for n in range(2) for h in range(2) for m in range(3)]

    barrier = pltpu.get_barrier_semaphore()

    @pl.loop(1, nt)
    def _(k):
        pl.semaphore_signal(barrier, inc=1, device_id=(e, lax.rem(t + k, nt)), device_id_type=MESH)

    @pl.loop(1, ne)
    def _(k):
        for h in range(2):
            pl.semaphore_signal(barrier, inc=1, device_id=(lax.rem(e + k, ne), 2 * chip + h), device_id_type=MESH)

    for copy in own_weights + own_shared:
        copy.start()
    for n in range(nt):
        span = slice(n * d8, (n + 1) * d8)
        pair[:, span] = jnp.concatenate(
            [tok_ref[:, span].astype(F32), cot_ref[:, span].astype(F32)], axis=0).astype(BF)
    table[...] = jnp.zeros_like(table)
    for n in range(2):
        table[8 * n:8 * n + 8, :topk] = routes_ref[...]
        table[8 * n:8 * n + 8, topk:2 * topk] = gates_ref[...]

    pl.semaphore_wait(barrier, 2 * (ne - 1) + nt - 1)

    @pl.loop(1, nt)
    def _(k):
        p = lax.rem(t + k, nt)
        rcopy(table, tabs.at[block(t, 16)], TAB, (e, p)).start()
        rcopy(pair.at[:, cols(p)], gs.at[block(t, 16)], SLICE, (e, p)).start()

    rcopy(pair, g.at[block(t, 16)], TOKX, row_dev).start()
    for n in range(2):
        there = n * q + (1 - n) * (1 - q)
        for h in range(2):
            for m in range(3):
                rcopy(source(m).at[:, cols(4 * (1 - a) + 2 * there + h)], wt.at[there, h, m, block(place, hid)],
                      WX + n, weight_dev).start()
    for n in range(2):
        for h in range(2):
            for m in range(3):
                rcopy(source(m).at[:, cols(4 * a + 2 * n + h)], wt.at[n, h, m, block(place, hid)],
                      WPART, (e, partner)).start()

    rcopy(pair, g.at[block(t, 16)], TOKP, (e, partner)).start()

    tabs[block(t, 16), :] = table[...]
    gs[block(t, 16), :] = pair[:, cols(t)]
    g[block(t, 16), :] = pair[...]

    recv(tabs.at[pl.ds(0, (nt - 1) * 16)], TAB)
    lanes = nt * 16
    chosen = tabs[...].astype(F32).T
    lane_a = lax.broadcasted_iota(jnp.int32, (lanes, lanes), 0)
    lane_b = lax.broadcasted_iota(jnp.int32, (lanes, lanes), 1)
    token_a, token_b = (lane_a // 16) * 8 + lane_a % 8, (lane_b // 16) * 8 + lane_b % 8
    earlier = jnp.where((lane_a % 16 < 8) & (token_a < token_b), 1.0, 0.0).astype(BF)
    recv(gs.at[pl.ds(0, (nt - 1) * 16)], SLICE)
    tokens_here = gs[...]
    ec = ne // 4
    size = ec * m32
    for turn in range(4):
        chunk = lax.rem(first + turn, 4)
        row = lax.broadcasted_iota(jnp.int32, (size, lanes), 0)
        lane = lax.broadcasted_iota(jnp.int32, (size, lanes), 1)
        kind, slot = (row // SLOTS) % 2, (row % SLOTS).astype(F32)
        expert = (row // m32 * 4 + chunk).astype(F32)
        named = jnp.zeros((size, lanes), F32)
        gate = jnp.zeros((size, lanes), F32)
        for k in range(topk):
            hit = chosen[k:k + 1, :] == expert
            named = jnp.where(hit, 1.0, named)
            gate = jnp.where(hit, chosen[topk + k:topk + k + 1, :] * (1.0 / 64.0), gate)
        rank = dot(named.astype(BF), earlier)
        here = jnp.where((rank == slot) & ((lane // 8) % 2 == kind), named, 0.0)
        weighted = jnp.where(kind == 1, here * gate, here).astype(BF)
        t2[block(chunk, size), :] = jnp.where(kind == 1, here, here * gate).astype(BF)
        snd[pl.ds(chunk * ec, ec)] = dot(weighted, tokens_here).astype(BF).reshape(ec, m32, d8)

        @pl.loop(0, ec)
        def _(n):
            p = n * 4 + chunk
            from_here = snd.at[chunk * ec + n]
            target = xr.at[q, core, local_group]

            @pl.when(jnp.logical_and(p == e, stays))
            def _():
                pltpu.make_async_copy(from_here, target, rsem.at[DISP + first]).start()

            @pl.when(jnp.logical_not(jnp.logical_and(p == e, stays)))
            def _():
                rcopy(from_here, target, DISP + first, (p, 2 * chip + (e // 4) % 2)).start()

    def order(k):
        return lax.rem(first + 4 - k, 4)

    def pass_rows(k):
        chunk = order(k)
        part = xr.at[q, :, pl.ds(chunk * gq, gq)]
        recv(part, DISP + chunk)
        rcopy(part, part, PAIR + k, row_dev).start()

    def pass_weights(n):
        there = n * (1 - q) + (1 - n) * q
        part = wt.at[there, :, :, block(2 * (1 - a) + core, hid)]
        recv(part, WX + n)
        rcopy(part, part, WF + n, (e, partner)).start()

    pass_rows(0)
    pass_rows(1)
    pass_weights(0)
    pass_rows(2)
    pass_weights(1)

    def products(quarter, chunk):
        value = [None] * 3
        for h in range(2):
            part = xr[quarter, h, pl.ds(chunk * gq, gq)]
            x_rows = part[:, :SLOTS].reshape(rows, d8)
            dy_rows = part[:, SLOTS:].reshape(rows, d8)
            for m in range(3):
                term = dot(dy_rows if m == 2 else x_rows, wt[quarter, h, m], NT)
                value[m] = term if h == 0 else value[m] + term
        return value

    def begin(k):
        chunk = order(k)
        for m, value in enumerate(products(q, chunk)):
            pf[chunk, :, m * half:(m + 1) * half] = value

    def finish(k):
        chunk = order(k)
        recv(xr.at[0, :, pl.ds(0, gq)], PAIR + k)
        for m, value in enumerate(products(1 - q, chunk)):
            span = slice(m * half, (m + 1) * half)
            pf[chunk, :, span] = pf[chunk, :, span] + value
        pb[chunk] = pf[chunk, block(1 - a, own_rows)].astype(BF)
        rcopy(pb.at[chunk], rs.at[chunk], PRE + k, weight_dev).start()

    def activate(k):
        chunk = order(k)
        recv(rs.at[chunk], PRE + k)
        total = pf[chunk, block(a, own_rows)] + rs[chunk].astype(F32)
        gate_pre, up_pre, back = total[:, :half], total[:, half:2 * half], total[:, 2 * half:]
        active, slope = silu_parts(gate_pre)
        act[chunk, a, :, :half] = (active * up_pre).astype(BF)
        act[chunk, a, :, half:2 * half] = (back * up_pre * slope).astype(BF)
        act[chunk, a, :, 2 * half:] = (back * active).astype(BF)
        rcopy(act.at[chunk, a], act.at[chunk, a], ACT + k, weight_dev).start()

    def results(quarter, h, chunk):
        left = act[chunk].reshape(rows, 3 * half)
        y = dot(left[:, :half], wt[quarter, h, 2])
        dx = dot(left[:, half:], wt[quarter, h, 0:2].reshape(2 * half, d8))
        return jnp.concatenate([y.reshape(gq, SLOTS, d8), dx.reshape(gq, SLOTS, d8)], axis=1)

    def answer(k):
        chunk = order(k)
        part = pl.ds(chunk * gq, gq)
        recv(act.at[chunk, 1 - a], ACT + k)
        rcopy(act.at[chunk], actp.at[chunk], ACTP, (e, partner)).start()
        for h in range(2):
            ps[h, part] = results(1 - q, h, chunk).astype(BF)
        rcopy(ps.at[:, part], pr.at[:, part], HALF + k, row_dev).start()
        for h in range(2):
            po[h, part] = results(q, h, chunk)

    def give_back(k):
        chunk = order(k)
        part = pl.ds(chunk * gq, gq)
        recv(pr.at[:, part], HALF + k)
        ret[:, part] = (po[:, part] + pr[:, part].astype(F32)).astype(BF)

        @pl.loop(0, gq)
        def _(n):
            place_here = chunk * gq + n
            p = 4 * (2 * n + core) + chunk
            for h in range(2):
                local = jnp.logical_and(p == e, core == h)

                @pl.when(local)
                def _():
                    pltpu.make_async_copy(ret.at[h, place_here], bk.at[home], rsem.at[BACK]).start()

                @pl.when(jnp.logical_not(local))
                def _():
                    rcopy(ret.at[h, place_here], bk.at[home], BACK, (p, 2 * chip + h)).start()

    for copy in own_weights:
        copy.wait()
    recv(wt.at[:, :, :, pl.ds(0, hid)], WPART)
    recv(wt.at[0, :, :, pl.ds(0, hid)], WF)
    for k in range(3):
        begin(k)
    recv(wt.at[0, :, :, pl.ds(0, hid)], WF + 1)
    finish(0)

    pass_rows(3)
    activate(0)
    begin(3)
    finish(1)
    answer(0)
    activate(1)
    finish(2)

    answer(1)
    activate(2)
    finish(3)
    rcopy(xr.at[:, 1 - core], xp, XP, (e, partner)).start()
    answer(2)
    activate(3)
    for j in (weight_chip, lax.rem(chip + 2, chips)):
        rcopy(pair, g.at[block(t, 16)], TOKX, (e, 2 * j + core)).start()
    give_back(0)
    answer(3)

    recv(xp, XP)
    recv(actp, ACTP)
    own_grads = []

    def gradient(n, m):
        span = slice(0, half) if m == 2 else slice((m + 1) * half, (m + 2) * half)
        kind = slice(SLOTS, m32) if m == 2 else slice(0, SLOTS)
        here = act[:, :, :, span].reshape(4 * rows, half)
        there = actp[:, :, :, span].reshape(4 * rows, half)
        x_here = xr[n, core, :, kind].reshape(4 * rows, d8)
        x_there = xp[n, :, kind].reshape(4 * rows, d8)
        gb[n, m] = (dot(here, x_here, TN) + dot(there, x_there, TN)).astype(BF)
        target = (gout_ref if m == 2 else gin_ref.at[m]).at[:, cols(4 * a + 2 * n + core)]
        which = GRAD_OUT if m == 2 else GRAD_IN
        for c in range(2):
            rcopy(gb.at[n, m, block(2 * (1 - a) + c, hid)], target, which, (e, 2 * weight_chip + c)).start()
        rcopy(gb.at[n, m, block(2 * a + 1 - core, hid)], target, which, (e, partner)).start()
        own = pltpu.make_async_copy(gb.at[n, m, block(place, hid)], target, lsem.at[2 + 3 * n + m])
        own.start()
        own_grads.append(own)

    for n in range(2):
        for m in range(3):
            gradient(n, m)
    give_back(1)
    recv(g.at[pl.ds(0, (chips - 1) * 16)], TOKX)

    @pl.loop(1, chips)
    def _(k):
        part = g.at[block(lax.rem(t + 2 * k, nt), 16)]
        rcopy(part, part, TOKP, (e, partner)).start()

    give_back(2)
    recv(g.at[pl.ds(0, chips * 16)], TOKP)
    for copy in own_shared:
        copy.wait()
    sh = sw_out.shape[0]

    def shared_step(n, sums):
        piece = g[:, cols(n)]
        return tuple(
            total + dot(piece, weight[:, cols(n)], NT)
            for total, weight in zip(sums, (sw_in.at[0], sw_in.at[1], sw_out)))

    zero = jnp.zeros((nt * 16, sh), F32)
    sums = lax.fori_loop(0, nt, shared_step, (zero, zero, zero))
    s_gate, s_up = [v.reshape(nt, 16, sh)[:, :8].reshape(nt * 8, sh) for v in sums[:2]]
    s_back = sums[2].reshape(nt, 16, sh)[:, 8:].reshape(nt * 8, sh)
    s_act, s_slope = silu_parts(s_gate)
    s_hidden = (s_act * s_up).astype(BF)
    s_dgate = (s_back * s_up * s_slope).astype(BF)
    s_dup = (s_back * s_act).astype(BF)

    def shared_terms(low, high):
        @pl.loop(low, high)
        def _(n):
            y = dot(s_hidden, sw_out[:, cols(n)]).reshape(nt, 8, d8)
            dx = (dot(s_dgate, sw_in[0, :, cols(n)]) + dot(s_dup, sw_in[1, :, cols(n)])).reshape(nt, 8, d8)
            shs[:, :, :, cols(n)] = jnp.concatenate([y, dx], axis=1).astype(BF).reshape(chips, 2, 16, d8)

    shared_terms(0, nt)
    rcopy(shs.at[:, 1 - core], shp, SHP, (e, partner)).start()
    give_back(3)
    recv(shp, SHP)
    for n in range(chips):
        shs[n, core] = (shs[n, core].astype(F32) + shp[n].astype(F32)).astype(BF)

    rcopy(shs.at[row_chip, core], shr.at[0], SHARED, row_dev).start()
    rcopy(shs.at[chips - 1 - row_chip, core], shr.at[1], SHARED, row_dev).start()
    recv(shr.at[pl.ds(0, 2)], SHARED)
    shs[weight_chip, core] = (shs[weight_chip, core].astype(F32) + shr[1].astype(F32)).astype(BF)
    rcopy(shs.at[weight_chip, core], shr.at[2], SUMS, weight_dev).start()
    shr[1] = shs[chip, core]

    recv(bk, BACK)
    routed = dot(t2[...], bk[...].reshape(ne * m32, d8), TN)
    fs[...] = routed.astype(BF).reshape(nt, 16, d8)

    @pl.loop(1, nt)
    def _(k):
        p = lax.rem(t + k, nt)
        rcopy(fs.at[p], fr.at[t], FINAL, (e, p)).start()

    fr[t] = fs[t]
    recv(shr.at[2], SUMS)
    recv(fr.at[pl.ds(0, nt - 1)], FINAL)

    for n in range(nt):
        span = slice(n * d8, (n + 1) * d8)
        total = fr[n].astype(F32) + jnp.sum(shr[:, :, span].astype(F32), axis=0)
        out_ref[:, span] = total[:8].astype(BF)
        gtok_ref[:, span] = total[8:].astype(BF)

    recv(gin_ref.at[:, :, pl.ds(0, 6 * d8)], GRAD_IN)
    recv(gout_ref.at[:, pl.ds(0, 6 * d8)], GRAD_OUT)
    for copy in own_grads:
        copy.wait()
    sent(tabs.at[pl.ds(0, (nt - 1) * 16)], TAB)
    sent(gs.at[pl.ds(0, (nt - 1) * 16)], SLICE)
    sent(g.at[pl.ds(0, (chips - 1) * 16)], TOKX)
    sent(g.at[pl.ds(0, chips * 16)], TOKP)
    sent(wt.at[:, :, :, pl.ds(0, hid)], WPART)
    for n in range(2):
        sent(wt.at[n, :, :, pl.ds(0, hid)], WX + n)
        sent(wt.at[n, :, :, pl.ds(0, hid)], WF + n)
    for k in range(4):
        sent(xr.at[0, :, pl.ds(0, gq)], PAIR + k)
        sent(ps.at[:, pl.ds(0, gq)], HALF + k)
    sent(xp, XP)
    for k in range(4):
        sent(rs.at[0], PRE + k)
        sent(rs.at[0], ACT + k)
    sent(actp, ACTP)
    sent(shp, SHP)
    sent(shr.at[pl.ds(0, 2)], SHARED)
    sent(shr.at[0], SUMS)
    sent(gin_ref.at[:, :, pl.ds(0, 6 * d8)], GRAD_IN)
    sent(gout_ref.at[:, pl.ds(0, 6 * d8)], GRAD_OUT)
    sent(fs.at[pl.ds(0, nt - 1)], FINAL)

    @pl.when(stays)
    def _():
        sent(bk.at[pl.ds(0, ne - 1)], BACK)
        sent(bk.at[pl.ds(0, ne - 1)], DISP + first)

    @pl.when(jnp.logical_not(stays))
    def _():
        sent(bk, BACK)
        sent(bk, DISP + first)


def hand_over(out_a, gtok_a, gin_a, gout_a, out_b, gtok_b, gin_b, gout_b, small, big, sem):
    hid = gout_a.shape[0]
    part = hid // 2
    moves = []
    for m in range(3):
        left, right = (gout_a, gout_b) if m == 2 else (gin_a.at[m], gin_b.at[m])
        for n in range(2):
            rows = pl.ds(n * part, part)
            moves.append((left.at[rows], big.at[m, rows], right.at[rows]))
    moves += [(out_a, small.at[0], out_b), (gtok_a, small.at[1], gtok_b)]
    inward = [pltpu.make_async_copy(src, mid, sem.at[0, n]) for n, (src, mid, _) in enumerate(moves)]
    outward = [pltpu.make_async_copy(mid, dst, sem.at[1, n]) for n, (_, mid, dst) in enumerate(moves)]
    for copy in inward:
        copy.start()
    for before, after in zip(inward, outward):
        before.wait()
        after.start()
    for copy in outward:
        copy.wait()


def on_device(tokens, routes, gate_num, cotangent, w_in, w_out, shared_in, shared_out):
    ne, nt = lax.axis_size("expert"), lax.axis_size("tensor")
    chips = nt // 2
    own, features = tokens.shape
    topk = routes.shape[1]
    hid, sh = w_out.shape[1], shared_out.shape[0]
    d8, half, gl_count = features // nt, 4 * hid, ne // 2
    rows, m32 = gl_count * SLOTS // 4, 2 * SLOTS
    vm = pl.BlockSpec(memory_space=pltpu.VMEM)
    hbm = pl.BlockSpec(memory_space=pl.ANY)
    scratch = [
        pltpu.VMEM((16, features), BF),
        pltpu.VMEM((16, 128), jnp.int32),
        pltpu.VMEM((nt * 16, 128), jnp.int32),
        pltpu.VMEM((nt * 16, d8), BF),
        pltpu.VMEM((nt * 16, features), BF),
        pltpu.VMEM((2, 2, 3, half, d8), BF),
        pltpu.VMEM((2, sh, features), BF),
        pltpu.VMEM((sh, features), BF),
        pltpu.VMEM((ne * m32, nt * 16), BF),
        pltpu.VMEM((ne, m32, d8), BF),
        pltpu.VMEM((2, 2, gl_count, m32, d8), BF),
        pltpu.VMEM((2, gl_count, m32, d8), BF),
        pltpu.VMEM((4, rows, 3 * half), F32),
        pltpu.VMEM((4, rows // 2, 3 * half), BF),
        pltpu.VMEM((4, rows // 2, 3 * half), BF),
        pltpu.VMEM((4, 2, rows // 2, 3 * half), BF),
        pltpu.VMEM((4, 2, rows // 2, 3 * half), BF),
        pltpu.VMEM((2, gl_count, m32, d8), BF),
        pltpu.VMEM((2, gl_count, m32, d8), BF),
        pltpu.VMEM((2, gl_count, m32, d8), F32),
        pltpu.VMEM((2, gl_count, m32, d8), BF),
        pltpu.VMEM((ne, m32, d8), BF),
        pltpu.VMEM((2, 3, half, d8), BF),
        pltpu.VMEM((chips, 2, 16, features), BF),
        pltpu.VMEM((chips, 16, features), BF),
        pltpu.VMEM((3, 16, features), BF),
        pltpu.VMEM((nt, 16, d8), BF),
        pltpu.VMEM((nt, 16, d8), BF),
        pltpu.SemaphoreType.DMA((COUNT,)),
        pltpu.SemaphoreType.DMA((COUNT,)),
        pltpu.SemaphoreType.DMA((14,)),
    ]
    shapes = (
        jax.ShapeDtypeStruct((own, features), BF),
        jax.ShapeDtypeStruct((own, features), BF),
        jax.ShapeDtypeStruct((2, hid, features), BF),
        jax.ShapeDtypeStruct((hid, features), BF),
    )
    results = pl.pallas_call(
        functools.partial(kernel, topk),
        out_shape=shapes,
        in_specs=[vm, vm, vm, vm, hbm, hbm, hbm, hbm],
        out_specs=(vm, vm, hbm, hbm),
        scratch_shapes=scratch,
        compiler_params=pltpu.CompilerParams(
            collective_id=0, has_side_effects=True, vmem_limit_bytes=56 * 2**20
        ),
    )(tokens, cotangent, routes, gate_num, w_in[0], w_out[0], shared_in, shared_out)
    out, gtok, gin, gout = pl.pallas_call(
        hand_over,
        out_shape=shapes,
        in_specs=[hbm] * 4,
        out_specs=(hbm,) * 4,
        scratch_shapes=[
            pltpu.VMEM((2, own, features), BF),
            pltpu.VMEM((3, hid, features), BF),
            pltpu.SemaphoreType.DMA((2, 8)),
        ],
        compiler_params=pltpu.CompilerParams(vmem_limit_bytes=60 * 2**20),
    )(*results)
    return out, gtok, gin[None], gout[None]


def solution(mesh):
    in_specs = (
        P(("expert", "tensor"), None),
        P(("expert", "tensor"), None),
        P(("expert", "tensor"), None),
        P(("expert", "tensor"), None),
        P("expert", None, "tensor", None),
        P("expert", "tensor", None),
        P(None, "tensor", None),
        P("tensor", None),
    )
    out_specs = (
        P(("expert", "tensor"), None),
        P(("expert", "tensor"), None),
        P("expert", None, "tensor", None),
        P("expert", "tensor", None),
    )
    return jax.shard_map(
        on_device, mesh=mesh, in_specs=in_specs, out_specs=out_specs, check_vma=False
    )
```

```python
import functools

import jax
import jax.numpy as jnp
from jax import lax
from jax.experimental import pallas as pl
from jax.experimental.pallas import tpu as pltpu
from jax.sharding import PartitionSpec as P

MESH = pl.DeviceIdType.MESH
BF = jnp.bfloat16
F32 = jnp.float32
SLOTS = 16
NT = (((1,), (1,)), ((), ()))
TN = (((0,), (0,)), ((), ()))

TAB, SLICE, TOKX, TOKP, WPART, XP, ACTP, BACK, GRAD_IN, GRAD_OUT, SHP, SHARED, FINAL = range(13)
PRE, ACT, WX, WF, DISP, PAIR, HALF = 13, 17, 21, 23, 25, 29, 33
SUMS = 37
COUNT = 38


def dot(left, right, dims=None):
    dims = dims or (((1,), (0,)), ((), ()))
    return lax.dot_general(left, right, dims, preferred_element_type=F32)


def silu_parts(preact):
    sig_value = jax.nn.sigmoid(preact)
    return preact * sig_value, sig_value * (1.0 + preact * (1.0 - sig_value))


def kernel(
    topk,
    tok_ref, cot_ref, routes_ref, gates_ref, w_in, w_out, sh_in, sh_out,
    out_ref, gtok_ref, gin_ref, gout_ref,
    pair, table, tabs, gs, g, wt, sw_in, sw_out, t2, snd, xr, xp, pf, pb, rs, act, actp, ps, pr, po, ret, bk, gb,
    shs, shp, shr, fs, fr, ssem, rsem, lsem,
):
    ne, nt = lax.axis_size("expert"), lax.axis_size("tensor")
    e, t = lax.axis_index("expert"), lax.axis_index("tensor")
    chip, core = t // 2, t % 2
    chips = nt // 2
    a, q = chip // 2, chip % 2
    partner = t + 1 - 2 * core
    row_chip = 2 * a + 1 - q
    weight_chip = chips - 1 - chip
    row_dev, weight_dev = (e, 2 * row_chip + core), (e, 2 * weight_chip + core)
    first = e % 4
    stays = (e // 4) % 2 == core
    home = (e % 4) * (ne // 4) + e // 4
    local_group = (e % 4) * (ne // 8) + e // 8
    d8 = gs.shape[1]
    hid = w_out.shape[0]
    half = 4 * hid
    gl_count = ne // 2
    gq = gl_count // 4
    rows = gq * SLOTS
    own_rows = rows // 2
    m32 = 2 * SLOTS

    def rcopy(src, dst, which, dev):
        return pltpu.make_async_remote_copy(
            src_ref=src, dst_ref=dst, send_sem=ssem.at[which], recv_sem=rsem.at[which],
            device_id=dev, device_id_type=MESH,
        )

    def recv(ref, which):
        pltpu.make_async_copy(ref, ref, rsem.at[which]).wait()

    def sent(ref, which):
        pltpu.make_async_copy(ref, ref, ssem.at[which]).wait()

    def cols(piece):
        return pl.ds(pl.multiple_of(piece * d8, 128), d8)

    def block(index, size):
        return pl.ds(pl.multiple_of(index * size, 16), size)

    def source(m):
        return w_out if m == 2 else w_in.at[m]

    place = 2 * a + core
    own_shared = [
        pltpu.make_async_copy(sh_in, sw_in, lsem.at[0]),
        pltpu.make_async_copy(sh_out, sw_out, lsem.at[1]),
    ]
    own_weights = [
        pltpu.make_async_copy(
            source(m).at[:, cols(4 * a + 2 * n + h)], wt.at[n, h, m, block(place, hid)], lsem.at[2 + 6 * n + 3 * h + m])
        for n in range(2) for h in range(2) for m in range(3)]

    barrier = pltpu.get_barrier_semaphore()

    @pl.loop(1, nt)
    def _(k):
        pl.semaphore_signal(barrier, inc=1, device_id=(e, lax.rem(t + k, nt)), device_id_type=MESH)

    @pl.loop(1, ne)
    def _(k):
        for h in range(2):
            pl.semaphore_signal(barrier, inc=1, device_id=(lax.rem(e + k, ne), 2 * chip + h), device_id_type=MESH)

    for copy in own_weights + own_shared:
        copy.start()
    for n in range(nt):
        span = slice(n * d8, (n + 1) * d8)
        pair[:, span] = jnp.concatenate(
            [tok_ref[:, span].astype(F32), cot_ref[:, span].astype(F32)], axis=0).astype(BF)
    table[...] = jnp.zeros_like(table)
    for n in range(2):
        table[8 * n:8 * n + 8, :topk] = routes_ref[...]
        table[8 * n:8 * n + 8, topk:2 * topk] = gates_ref[...]

    pl.semaphore_wait(barrier, 2 * (ne - 1) + nt - 1)

    @pl.loop(1, nt)
    def _(k):
        p = lax.rem(t + k, nt)
        rcopy(table, tabs.at[block(t, 16)], TAB, (e, p)).start()
        rcopy(pair.at[:, cols(p)], gs.at[block(t, 16)], SLICE, (e, p)).start()

    rcopy(pair, g.at[block(t, 16)], TOKX, row_dev).start()
    for n in range(2):
        there = n * q + (1 - n) * (1 - q)
        for h in range(2):
            for m in range(3):
                rcopy(source(m).at[:, cols(4 * (1 - a) + 2 * there + h)], wt.at[there, h, m, block(place, hid)],
                      WX + n, weight_dev).start()
    for n in range(2):
        for h in range(2):
            for m in range(3):
                rcopy(source(m).at[:, cols(4 * a + 2 * n + h)], wt.at[n, h, m, block(place, hid)],
                      WPART, (e, partner)).start()

    rcopy(pair, g.at[block(t, 16)], TOKP, (e, partner)).start()

    tabs[block(t, 16), :] = table[...]
    gs[block(t, 16), :] = pair[:, cols(t)]
    g[block(t, 16), :] = pair[...]

    recv(tabs.at[pl.ds(0, (nt - 1) * 16)], TAB)
    lanes = nt * 16
    chosen = tabs[...].astype(F32).T
    lane_a = lax.broadcasted_iota(jnp.int32, (lanes, lanes), 0)
    lane_b = lax.broadcasted_iota(jnp.int32, (lanes, lanes), 1)
    token_a, token_b = (lane_a // 16) * 8 + lane_a % 8, (lane_b // 16) * 8 + lane_b % 8
    earlier = jnp.where((lane_a % 16 < 8) & (token_a < token_b), 1.0, 0.0).astype(BF)
    recv(gs.at[pl.ds(0, (nt - 1) * 16)], SLICE)
    tokens_here = gs[...]
    ec = ne // 4
    size = ec * m32
    for turn in range(4):
        chunk = lax.rem(first + turn, 4)
        row = lax.broadcasted_iota(jnp.int32, (size, lanes), 0)
        lane = lax.broadcasted_iota(jnp.int32, (size, lanes), 1)
        kind, slot = (row // SLOTS) % 2, (row % SLOTS).astype(F32)
        expert = (row // m32 * 4 + chunk).astype(F32)
        named = jnp.zeros((size, lanes), F32)
        gate = jnp.zeros((size, lanes), F32)
        for k in range(topk):
            hit = chosen[k:k + 1, :] == expert
            named = jnp.where(hit, 1.0, named)
            gate = jnp.where(hit, chosen[topk + k:topk + k + 1, :] * (1.0 / 64.0), gate)
        rank = dot(named.astype(BF), earlier)
        here = jnp.where((rank == slot) & ((lane // 8) % 2 == kind), named, 0.0)
        weighted = jnp.where(kind == 1, here * gate, here).astype(BF)
        t2[block(chunk, size), :] = jnp.where(kind == 1, here, here * gate).astype(BF)
        snd[pl.ds(chunk * ec, ec)] = dot(weighted, tokens_here).astype(BF).reshape(ec, m32, d8)

        @pl.loop(0, ec)
        def _(n):
            p = n * 4 + chunk
            from_here = snd.at[chunk * ec + n]
            target = xr.at[q, core, local_group]

            @pl.when(jnp.logical_and(p == e, stays))
            def _():
                pltpu.make_async_copy(from_here, target, rsem.at[DISP + first]).start()

            @pl.when(jnp.logical_not(jnp.logical_and(p == e, stays)))
            def _():
                rcopy(from_here, target, DISP + first, (p, 2 * chip + (e // 4) % 2)).start()

    def order(k):
        return lax.rem(first + 4 - k, 4)

    def pass_rows(k):
        chunk = order(k)
        part = xr.at[q, :, pl.ds(chunk * gq, gq)]
        recv(part, DISP + chunk)
        rcopy(part, part, PAIR + k, row_dev).start()

    def pass_weights(n):
        there = n * (1 - q) + (1 - n) * q
        part = wt.at[there, :, :, block(2 * (1 - a) + core, hid)]
        recv(part, WX + n)
        rcopy(part, part, WF + n, (e, partner)).start()

    pass_rows(0)
    pass_rows(1)
    pass_weights(0)
    pass_rows(2)

    def products(quarter, chunk):
        value = [None] * 3
        for h in range(2):
            part = xr[quarter, h, pl.ds(chunk * gq, gq)]
            x_rows = part[:, :SLOTS].reshape(rows, d8)
            dy_rows = part[:, SLOTS:].reshape(rows, d8)
            for m in range(3):
                term = dot(dy_rows if m == 2 else x_rows, wt[quarter, h, m], NT)
                value[m] = term if h == 0 else value[m] + term
        return value

    def begin(k):
        chunk = order(k)
        for m, value in enumerate(products(q, chunk)):
            pf[chunk, :, m * half:(m + 1) * half] = value

    def finish(k):
        chunk = order(k)
        recv(xr.at[0, :, pl.ds(0, gq)], PAIR + k)
        for m, value in enumerate(products(1 - q, chunk)):
            span = slice(m * half, (m + 1) * half)
            pf[chunk, :, span] = pf[chunk, :, span] + value
        pb[chunk] = pf[chunk, block(1 - a, own_rows)].astype(BF)
        rcopy(pb.at[chunk], rs.at[chunk], PRE + k, weight_dev).start()

    def activate(k):
        chunk = order(k)
        recv(rs.at[chunk], PRE + k)
        total = pf[chunk, block(a, own_rows)] + rs[chunk].astype(F32)
        gate_pre, up_pre, back = total[:, :half], total[:, half:2 * half], total[:, 2 * half:]
        active, slope = silu_parts(gate_pre)
        act[chunk, a, :, :half] = (active * up_pre).astype(BF)
        act[chunk, a, :, half:2 * half] = (back * up_pre * slope).astype(BF)
        act[chunk, a, :, 2 * half:] = (back * active).astype(BF)
        rcopy(act.at[chunk, a], act.at[chunk, a], ACT + k, weight_dev).start()

    def results(quarter, h, chunk):
        left = act[chunk].reshape(rows, 3 * half)
        y = dot(left[:, :half], wt[quarter, h, 2])
        dx = dot(left[:, half:], wt[quarter, h, 0:2].reshape(2 * half, d8))
        return jnp.concatenate([y.reshape(gq, SLOTS, d8), dx.reshape(gq, SLOTS, d8)], axis=1)

    def answer(k):
        chunk = order(k)
        part = pl.ds(chunk * gq, gq)
        recv(act.at[chunk, 1 - a], ACT + k)
        rcopy(act.at[chunk], actp.at[chunk], ACTP, (e, partner)).start()
        for h in range(2):
            ps[h, part] = results(1 - q, h, chunk).astype(BF)
        rcopy(ps.at[:, part], pr.at[:, part], HALF + k, row_dev).start()
        for h in range(2):
            po[h, part] = results(q, h, chunk)

    def give_back(k):
        chunk = order(k)
        part = pl.ds(chunk * gq, gq)
        recv(pr.at[:, part], HALF + k)
        ret[:, part] = (po[:, part] + pr[:, part].astype(F32)).astype(BF)

        @pl.loop(0, gq)
        def _(n):
            place_here = chunk * gq + n
            p = 4 * (2 * n + core) + chunk
            for h in range(2):
                local = jnp.logical_and(p == e, core == h)

                @pl.when(local)
                def _():
                    pltpu.make_async_copy(ret.at[h, place_here], bk.at[home], rsem.at[BACK]).start()

                @pl.when(jnp.logical_not(local))
                def _():
                    rcopy(ret.at[h, place_here], bk.at[home], BACK, (p, 2 * chip + h)).start()

    for copy in own_weights:
        copy.wait()
    recv(wt.at[:, :, :, pl.ds(0, hid)], WPART)
    recv(wt.at[0, :, :, pl.ds(0, hid)], WF)
    for k in range(3):
        begin(k)
    pass_weights(1)
    recv(wt.at[0, :, :, pl.ds(0, hid)], WF + 1)
    finish(0)

    pass_rows(3)
    activate(0)
    begin(3)
    finish(1)
    answer(0)
    activate(1)
    finish(2)

    answer(1)
    activate(2)
    finish(3)
    rcopy(xr.at[:, 1 - core], xp, XP, (e, partner)).start()
    answer(2)
    activate(3)
    for j in (weight_chip, lax.rem(chip + 2, chips)):
        rcopy(pair, g.at[block(t, 16)], TOKX, (e, 2 * j + core)).start()
    give_back(0)
    answer(3)

    recv(xp, XP)
    recv(actp, ACTP)
    own_grads = []

    def gradient(n, m):
        span = slice(0, half) if m == 2 else slice((m + 1) * half, (m + 2) * half)
        kind = slice(SLOTS, m32) if m == 2 else slice(0, SLOTS)
        here = act[:, :, :, span].reshape(4 * rows, half)
        there = actp[:, :, :, span].reshape(4 * rows, half)
        x_here = xr[n, core, :, kind].reshape(4 * rows, d8)
        x_there = xp[n, :, kind].reshape(4 * rows, d8)
        gb[n, m] = (dot(here, x_here, TN) + dot(there, x_there, TN)).astype(BF)
        target = (gout_ref if m == 2 else gin_ref.at[m]).at[:, cols(4 * a + 2 * n + core)]
        which = GRAD_OUT if m == 2 else GRAD_IN
        for c in range(2):
            rcopy(gb.at[n, m, block(2 * (1 - a) + c, hid)], target, which, (e, 2 * weight_chip + c)).start()
        rcopy(gb.at[n, m, block(2 * a + 1 - core, hid)], target, which, (e, partner)).start()
        own = pltpu.make_async_copy(gb.at[n, m, block(place, hid)], target, lsem.at[2 + 3 * n + m])
        own.start()
        own_grads.append(own)

    for m in range(3):
        gradient(0, m)
    give_back(1)
    for m in range(3):
        gradient(1, m)
    recv(g.at[pl.ds(0, (chips - 1) * 16)], TOKX)

    @pl.loop(1, chips)
    def _(k):
        part = g.at[block(lax.rem(t + 2 * k, nt), 16)]
        rcopy(part, part, TOKP, (e, partner)).start()

    give_back(2)
    recv(g.at[pl.ds(0, chips * 16)], TOKP)
    for copy in own_shared:
        copy.wait()
    sh = sw_out.shape[0]

    def shared_step(n, sums):
        piece = g[:, cols(n)]
        return tuple(
            total + dot(piece, weight[:, cols(n)], NT)
            for total, weight in zip(sums, (sw_in.at[0], sw_in.at[1], sw_out)))

    zero = jnp.zeros((nt * 16, sh), F32)
    sums = lax.fori_loop(0, nt, shared_step, (zero, zero, zero))
    s_gate, s_up = [v.reshape(nt, 16, sh)[:, :8].reshape(nt * 8, sh) for v in sums[:2]]
    s_back = sums[2].reshape(nt, 16, sh)[:, 8:].reshape(nt * 8, sh)
    s_act, s_slope = silu_parts(s_gate)
    s_hidden = (s_act * s_up).astype(BF)
    s_dgate = (s_back * s_up * s_slope).astype(BF)
    s_dup = (s_back * s_act).astype(BF)

    def shared_terms(low, high):
        @pl.loop(low, high)
        def _(n):
            y = dot(s_hidden, sw_out[:, cols(n)]).reshape(nt, 8, d8)
            dx = (dot(s_dgate, sw_in[0, :, cols(n)]) + dot(s_dup, sw_in[1, :, cols(n)])).reshape(nt, 8, d8)
            shs[:, :, :, cols(n)] = jnp.concatenate([y, dx], axis=1).astype(BF).reshape(chips, 2, 16, d8)

    shared_terms(0, nt)
    rcopy(shs.at[:, 1 - core], shp, SHP, (e, partner)).start()
    give_back(3)
    recv(shp, SHP)
    for n in range(chips):
        shs[n, core] = (shs[n, core].astype(F32) + shp[n].astype(F32)).astype(BF)

    rcopy(shs.at[row_chip, core], shr.at[0], SHARED, row_dev).start()
    rcopy(shs.at[chips - 1 - row_chip, core], shr.at[1], SHARED, row_dev).start()
    recv(shr.at[pl.ds(0, 2)], SHARED)
    shs[weight_chip, core] = (shs[weight_chip, core].astype(F32) + shr[1].astype(F32)).astype(BF)
    rcopy(shs.at[weight_chip, core], shr.at[2], SUMS, weight_dev).start()
    shr[1] = shs[chip, core]

    recv(bk, BACK)
    routed = dot(t2[...], bk[...].reshape(ne * m32, d8), TN)
    fs[...] = routed.astype(BF).reshape(nt, 16, d8)

    @pl.loop(1, nt)
    def _(k):
        p = lax.rem(t + k, nt)
        rcopy(fs.at[p], fr.at[t], FINAL, (e, p)).start()

    fr[t] = fs[t]
    recv(shr.at[2], SUMS)
    recv(fr.at[pl.ds(0, nt - 1)], FINAL)

    for n in range(nt):
        span = slice(n * d8, (n + 1) * d8)
        total = fr[n].astype(F32) + jnp.sum(shr[:, :, span].astype(F32), axis=0)
        out_ref[:, span] = total[:8].astype(BF)
        gtok_ref[:, span] = total[8:].astype(BF)

    recv(gin_ref.at[:, :, pl.ds(0, 6 * d8)], GRAD_IN)
    recv(gout_ref.at[:, pl.ds(0, 6 * d8)], GRAD_OUT)
    for copy in own_grads:
        copy.wait()
    sent(tabs.at[pl.ds(0, (nt - 1) * 16)], TAB)
    sent(gs.at[pl.ds(0, (nt - 1) * 16)], SLICE)
    sent(g.at[pl.ds(0, (chips - 1) * 16)], TOKX)
    sent(g.at[pl.ds(0, chips * 16)], TOKP)
    sent(wt.at[:, :, :, pl.ds(0, hid)], WPART)
    for n in range(2):
        sent(wt.at[n, :, :, pl.ds(0, hid)], WX + n)
        sent(wt.at[n, :, :, pl.ds(0, hid)], WF + n)
    for k in range(4):
        sent(xr.at[0, :, pl.ds(0, gq)], PAIR + k)
        sent(ps.at[:, pl.ds(0, gq)], HALF + k)
    sent(xp, XP)
    for k in range(4):
        sent(rs.at[0], PRE + k)
        sent(rs.at[0], ACT + k)
    sent(actp, ACTP)
    sent(shp, SHP)
    sent(shr.at[pl.ds(0, 2)], SHARED)
    sent(shr.at[0], SUMS)
    sent(gin_ref.at[:, :, pl.ds(0, 6 * d8)], GRAD_IN)
    sent(gout_ref.at[:, pl.ds(0, 6 * d8)], GRAD_OUT)
    sent(fs.at[pl.ds(0, nt - 1)], FINAL)

    @pl.when(stays)
    def _():
        sent(bk.at[pl.ds(0, ne - 1)], BACK)
        sent(bk.at[pl.ds(0, ne - 1)], DISP + first)

    @pl.when(jnp.logical_not(stays))
    def _():
        sent(bk, BACK)
        sent(bk, DISP + first)


def hand_over(out_a, gtok_a, gin_a, gout_a, out_b, gtok_b, gin_b, gout_b, small, big, sem):
    hid = gout_a.shape[0]
    part = hid // 2
    moves = []
    for m in range(3):
        left, right = (gout_a, gout_b) if m == 2 else (gin_a.at[m], gin_b.at[m])
        for n in range(2):
            rows = pl.ds(n * part, part)
            moves.append((left.at[rows], big.at[m, rows], right.at[rows]))
    moves += [(out_a, small.at[0], out_b), (gtok_a, small.at[1], gtok_b)]
    inward = [pltpu.make_async_copy(src, mid, sem.at[0, n]) for n, (src, mid, _) in enumerate(moves)]
    outward = [pltpu.make_async_copy(mid, dst, sem.at[1, n]) for n, (_, mid, dst) in enumerate(moves)]
    for copy in inward:
        copy.start()
    for before, after in zip(inward, outward):
        before.wait()
        after.start()
    for copy in outward:
        copy.wait()


def on_device(tokens, routes, gate_num, cotangent, w_in, w_out, shared_in, shared_out):
    ne, nt = lax.axis_size("expert"), lax.axis_size("tensor")
    chips = nt // 2
    own, features = tokens.shape
    topk = routes.shape[1]
    hid, sh = w_out.shape[1], shared_out.shape[0]
    d8, half, gl_count = features // nt, 4 * hid, ne // 2
    rows, m32 = gl_count * SLOTS // 4, 2 * SLOTS
    vm = pl.BlockSpec(memory_space=pltpu.VMEM)
    hbm = pl.BlockSpec(memory_space=pl.ANY)
    scratch = [
        pltpu.VMEM((16, features), BF),
        pltpu.VMEM((16, 128), jnp.int32),
        pltpu.VMEM((nt * 16, 128), jnp.int32),
        pltpu.VMEM((nt * 16, d8), BF),
        pltpu.VMEM((nt * 16, features), BF),
        pltpu.VMEM((2, 2, 3, half, d8), BF),
        pltpu.VMEM((2, sh, features), BF),
        pltpu.VMEM((sh, features), BF),
        pltpu.VMEM((ne * m32, nt * 16), BF),
        pltpu.VMEM((ne, m32, d8), BF),
        pltpu.VMEM((2, 2, gl_count, m32, d8), BF),
        pltpu.VMEM((2, gl_count, m32, d8), BF),
        pltpu.VMEM((4, rows, 3 * half), F32),
        pltpu.VMEM((4, rows // 2, 3 * half), BF),
        pltpu.VMEM((4, rows // 2, 3 * half), BF),
        pltpu.VMEM((4, 2, rows // 2, 3 * half), BF),
        pltpu.VMEM((4, 2, rows // 2, 3 * half), BF),
        pltpu.VMEM((2, gl_count, m32, d8), BF),
        pltpu.VMEM((2, gl_count, m32, d8), BF),
        pltpu.VMEM((2, gl_count, m32, d8), F32),
        pltpu.VMEM((2, gl_count, m32, d8), BF),
        pltpu.VMEM((ne, m32, d8), BF),
        pltpu.VMEM((2, 3, half, d8), BF),
        pltpu.VMEM((chips, 2, 16, features), BF),
        pltpu.VMEM((chips, 16, features), BF),
        pltpu.VMEM((3, 16, features), BF),
        pltpu.VMEM((nt, 16, d8), BF),
        pltpu.VMEM((nt, 16, d8), BF),
        pltpu.SemaphoreType.DMA((COUNT,)),
        pltpu.SemaphoreType.DMA((COUNT,)),
        pltpu.SemaphoreType.DMA((14,)),
    ]
    shapes = (
        jax.ShapeDtypeStruct((own, features), BF),
        jax.ShapeDtypeStruct((own, features), BF),
        jax.ShapeDtypeStruct((2, hid, features), BF),
        jax.ShapeDtypeStruct((hid, features), BF),
    )
    results = pl.pallas_call(
        functools.partial(kernel, topk),
        out_shape=shapes,
        in_specs=[vm, vm, vm, vm, hbm, hbm, hbm, hbm],
        out_specs=(vm, vm, hbm, hbm),
        scratch_shapes=scratch,
        compiler_params=pltpu.CompilerParams(
            collective_id=0, has_side_effects=True, vmem_limit_bytes=56 * 2**20
        ),
    )(tokens, cotangent, routes, gate_num, w_in[0], w_out[0], shared_in, shared_out)
    out, gtok, gin, gout = pl.pallas_call(
        hand_over,
        out_shape=shapes,
        in_specs=[hbm] * 4,
        out_specs=(hbm,) * 4,
        scratch_shapes=[
            pltpu.VMEM((2, own, features), BF),
            pltpu.VMEM((3, hid, features), BF),
            pltpu.SemaphoreType.DMA((2, 8)),
        ],
        compiler_params=pltpu.CompilerParams(vmem_limit_bytes=60 * 2**20),
    )(*results)
    return out, gtok, gin[None], gout[None]


def solution(mesh):
    in_specs = (
        P(("expert", "tensor"), None),
        P(("expert", "tensor"), None),
        P(("expert", "tensor"), None),
        P(("expert", "tensor"), None),
        P("expert", None, "tensor", None),
        P("expert", "tensor", None),
        P(None, "tensor", None),
        P("tensor", None),
    )
    out_specs = (
        P(("expert", "tensor"), None),
        P(("expert", "tensor"), None),
        P("expert", None, "tensor", None),
        P("expert", "tensor", None),
    )
    return jax.shard_map(
        on_device, mesh=mesh, in_specs=in_specs, out_specs=out_specs, check_vma=False
    )
```

```python
import functools

import jax
import jax.numpy as jnp
from jax import lax
from jax.experimental import pallas as pl
from jax.experimental.pallas import tpu as pltpu
from jax.sharding import PartitionSpec as P

MESH = pl.DeviceIdType.MESH
BF = jnp.bfloat16
F32 = jnp.float32
SLOTS = 16
NT = (((1,), (1,)), ((), ()))
TN = (((0,), (0,)), ((), ()))

TAB, SLICE, TOKX, TOKP, WPART, XP, ACTP, BACK, GRAD_IN, GRAD_OUT, SHP, SHARED, FINAL = range(13)
PRE, ACT, WX, WF, DISP, PAIR, HALF = 13, 17, 21, 23, 25, 29, 33
SUMS = 37
COUNT = 38


def dot(left, right, dims=None):
    dims = dims or (((1,), (0,)), ((), ()))
    return lax.dot_general(left, right, dims, preferred_element_type=F32)


def silu_parts(preact):
    sig_value = jax.nn.sigmoid(preact)
    return preact * sig_value, sig_value * (1.0 + preact * (1.0 - sig_value))


def kernel(
    topk,
    tok_ref, cot_ref, routes_ref, gates_ref, w_in, w_out, sh_in, sh_out,
    out_ref, gtok_ref, gin_ref, gout_ref,
    pair, table, tabs, gs, g, wt, sw_in, sw_out, t2, snd, xr, xp, pf, pb, rs, act, actp, ps, pr, po, ret, bk, gb,
    shs, shp, shr, fs, fr, ssem, rsem, lsem,
):
    ne, nt = lax.axis_size("expert"), lax.axis_size("tensor")
    e, t = lax.axis_index("expert"), lax.axis_index("tensor")
    chip, core = t // 2, t % 2
    chips = nt // 2
    a, q = chip // 2, chip % 2
    partner = t + 1 - 2 * core
    row_chip = 2 * a + 1 - q
    weight_chip = chips - 1 - chip
    row_dev, weight_dev = (e, 2 * row_chip + core), (e, 2 * weight_chip + core)
    first = e % 4
    stays = (e // 4) % 2 == core
    home = (e % 4) * (ne // 4) + e // 4
    local_group = (e % 4) * (ne // 8) + e // 8
    d8 = gs.shape[1]
    hid = w_out.shape[0]
    half = 4 * hid
    gl_count = ne // 2
    gq = gl_count // 4
    rows = gq * SLOTS
    own_rows = rows // 2
    m32 = 2 * SLOTS

    def rcopy(src, dst, which, dev):
        return pltpu.make_async_remote_copy(
            src_ref=src, dst_ref=dst, send_sem=ssem.at[which], recv_sem=rsem.at[which],
            device_id=dev, device_id_type=MESH,
        )

    def recv(ref, which):
        pltpu.make_async_copy(ref, ref, rsem.at[which]).wait()

    def sent(ref, which):
        pltpu.make_async_copy(ref, ref, ssem.at[which]).wait()

    def cols(piece):
        return pl.ds(pl.multiple_of(piece * d8, 128), d8)

    def block(index, size):
        return pl.ds(pl.multiple_of(index * size, 16), size)

    def source(m):
        return w_out if m == 2 else w_in.at[m]

    place = 2 * a + core
    own_shared = [
        pltpu.make_async_copy(sh_in, sw_in, lsem.at[0]),
        pltpu.make_async_copy(sh_out, sw_out, lsem.at[1]),
    ]
    own_weights = [
        pltpu.make_async_copy(
            source(m).at[:, cols(4 * a + 2 * n + h)], wt.at[n, h, m, block(place, hid)], lsem.at[2 + 6 * n + 3 * h + m])
        for n in range(2) for h in range(2) for m in range(3)]

    barrier = pltpu.get_barrier_semaphore()

    @pl.loop(1, nt)
    def _(k):
        pl.semaphore_signal(barrier, inc=1, device_id=(e, lax.rem(t + k, nt)), device_id_type=MESH)

    @pl.loop(1, ne)
    def _(k):
        for h in range(2):
            pl.semaphore_signal(barrier, inc=1, device_id=(lax.rem(e + k, ne), 2 * chip + h), device_id_type=MESH)

    for copy in own_weights + own_shared:
        copy.start()
    for n in range(nt):
        span = slice(n * d8, (n + 1) * d8)
        pair[:, span] = jnp.concatenate(
            [tok_ref[:, span].astype(F32), cot_ref[:, span].astype(F32)], axis=0).astype(BF)
    table[...] = jnp.zeros_like(table)
    for n in range(2):
        table[8 * n:8 * n + 8, :topk] = routes_ref[...]
        table[8 * n:8 * n + 8, topk:2 * topk] = gates_ref[...]

    pl.semaphore_wait(barrier, 2 * (ne - 1) + nt - 1)

    @pl.loop(1, nt)
    def _(k):
        p = lax.rem(t + k, nt)
        rcopy(table, tabs.at[block(t, 16)], TAB, (e, p)).start()
        rcopy(pair.at[:, cols(p)], gs.at[block(t, 16)], SLICE, (e, p)).start()

    rcopy(pair, g.at[block(t, 16)], TOKX, row_dev).start()
    for n in range(2):
        there = n * q + (1 - n) * (1 - q)
        for h in range(2):
            for m in range(3):
                rcopy(source(m).at[:, cols(4 * (1 - a) + 2 * there + h)], wt.at[there, h, m, block(place, hid)],
                      WX + n, weight_dev).start()
    for n in range(2):
        for h in range(2):
            for m in range(3):
                rcopy(source(m).at[:, cols(4 * a + 2 * n + h)], wt.at[n, h, m, block(place, hid)],
                      WPART, (e, partner)).start()

    rcopy(pair, g.at[block(t, 16)], TOKP, (e, partner)).start()

    tabs[block(t, 16), :] = table[...]
    gs[block(t, 16), :] = pair[:, cols(t)]
    g[block(t, 16), :] = pair[...]

    recv(tabs.at[pl.ds(0, (nt - 1) * 16)], TAB)
    lanes = nt * 16
    chosen = tabs[...].astype(F32).T
    lane_a = lax.broadcasted_iota(jnp.int32, (lanes, lanes), 0)
    lane_b = lax.broadcasted_iota(jnp.int32, (lanes, lanes), 1)
    token_a, token_b = (lane_a // 16) * 8 + lane_a % 8, (lane_b // 16) * 8 + lane_b % 8
    earlier = jnp.where((lane_a % 16 < 8) & (token_a < token_b), 1.0, 0.0).astype(BF)
    recv(gs.at[pl.ds(0, (nt - 1) * 16)], SLICE)
    tokens_here = gs[...]
    ec = ne // 4
    size = ec * m32
    for turn in range(4):
        chunk = lax.rem(first + turn, 4)
        row = lax.broadcasted_iota(jnp.int32, (size, lanes), 0)
        lane = lax.broadcasted_iota(jnp.int32, (size, lanes), 1)
        kind, slot = (row // SLOTS) % 2, (row % SLOTS).astype(F32)
        expert = (row // m32 * 4 + chunk).astype(F32)
        named = jnp.zeros((size, lanes), F32)
        gate = jnp.zeros((size, lanes), F32)
        for k in range(topk):
            hit = chosen[k:k + 1, :] == expert
            named = jnp.where(hit, 1.0, named)
            gate = jnp.where(hit, chosen[topk + k:topk + k + 1, :] * (1.0 / 64.0), gate)
        rank = dot(named.astype(BF), earlier)
        here = jnp.where((rank == slot) & ((lane // 8) % 2 == kind), named, 0.0)
        weighted = jnp.where(kind == 1, here * gate, here).astype(BF)
        t2[block(chunk, size), :] = jnp.where(kind == 1, here, here * gate).astype(BF)
        snd[pl.ds(chunk * ec, ec)] = dot(weighted, tokens_here).astype(BF).reshape(ec, m32, d8)

        @pl.loop(0, ec)
        def _(n):
            p = n * 4 + chunk
            from_here = snd.at[chunk * ec + n]
            target = xr.at[q, core, local_group]

            @pl.when(jnp.logical_and(p == e, stays))
            def _():
                pltpu.make_async_copy(from_here, target, rsem.at[DISP + first]).start()

            @pl.when(jnp.logical_not(jnp.logical_and(p == e, stays)))
            def _():
                rcopy(from_here, target, DISP + first, (p, 2 * chip + (e // 4) % 2)).start()

    def order(k):
        return lax.rem(first + 4 - k, 4)

    def pass_rows(k):
        chunk = order(k)
        part = xr.at[q, :, pl.ds(chunk * gq, gq)]
        recv(part, DISP + chunk)
        rcopy(part, part, PAIR + k, row_dev).start()

    def pass_weights(n):
        there = n * (1 - q) + (1 - n) * q
        part = wt.at[there, :, :, block(2 * (1 - a) + core, hid)]
        recv(part, WX + n)
        rcopy(part, part, WF + n, (e, partner)).start()

    pass_rows(0)
    pass_rows(1)
    pass_weights(0)
    pass_rows(2)

    def products(quarter, chunk):
        value = [None] * 3
        for h in range(2):
            part = xr[quarter, h, pl.ds(chunk * gq, gq)]
            x_rows = part[:, :SLOTS].reshape(rows, d8)
            dy_rows = part[:, SLOTS:].reshape(rows, d8)
            for m in range(3):
                term = dot(dy_rows if m == 2 else x_rows, wt[quarter, h, m], NT)
                value[m] = term if h == 0 else value[m] + term
        return value

    def begin(k):
        chunk = order(k)
        for m, value in enumerate(products(q, chunk)):
            pf[chunk, :, m * half:(m + 1) * half] = value

    def finish(k):
        chunk = order(k)
        recv(xr.at[0, :, pl.ds(0, gq)], PAIR + k)
        for m, value in enumerate(products(1 - q, chunk)):
            span = slice(m * half, (m + 1) * half)
            pf[chunk, :, span] = pf[chunk, :, span] + value
        pb[chunk] = pf[chunk, block(1 - a, own_rows)].astype(BF)
        rcopy(pb.at[chunk], rs.at[chunk], PRE + k, weight_dev).start()

    def activate(k):
        chunk = order(k)
        recv(rs.at[chunk], PRE + k)
        total = pf[chunk, block(a, own_rows)] + rs[chunk].astype(F32)
        gate_pre, up_pre, back = total[:, :half], total[:, half:2 * half], total[:, 2 * half:]
        active, slope = silu_parts(gate_pre)
        act[chunk, a, :, :half] = (active * up_pre).astype(BF)
        act[chunk, a, :, half:2 * half] = (back * up_pre * slope).astype(BF)
        act[chunk, a, :, 2 * half:] = (back * active).astype(BF)
        rcopy(act.at[chunk, a], act.at[chunk, a], ACT + k, weight_dev).start()

    def results(quarter, h, chunk):
        left = act[chunk].reshape(rows, 3 * half)
        y = dot(left[:, :half], wt[quarter, h, 2])
        dx = dot(left[:, half:], wt[quarter, h, 0:2].reshape(2 * half, d8))
        return jnp.concatenate([y.reshape(gq, SLOTS, d8), dx.reshape(gq, SLOTS, d8)], axis=1)

    def answer(k):
        chunk = order(k)
        part = pl.ds(chunk * gq, gq)
        recv(act.at[chunk, 1 - a], ACT + k)
        rcopy(act.at[chunk], actp.at[chunk], ACTP, (e, partner)).start()
        for h in range(2):
            ps[h, part] = results(1 - q, h, chunk).astype(BF)
        rcopy(ps.at[:, part], pr.at[:, part], HALF + k, row_dev).start()
        for h in range(2):
            po[h, part] = results(q, h, chunk)

    def give_back(k):
        chunk = order(k)
        part = pl.ds(chunk * gq, gq)
        recv(pr.at[:, part], HALF + k)
        ret[:, part] = (po[:, part] + pr[:, part].astype(F32)).astype(BF)

        @pl.loop(0, gq)
        def _(n):
            place_here = chunk * gq + n
            p = 4 * (2 * n + core) + chunk
            for h in range(2):
                local = jnp.logical_and(p == e, core == h)

                @pl.when(local)
                def _():
                    pltpu.make_async_copy(ret.at[h, place_here], bk.at[home], rsem.at[BACK]).start()

                @pl.when(jnp.logical_not(local))
                def _():
                    rcopy(ret.at[h, place_here], bk.at[home], BACK, (p, 2 * chip + h)).start()

    for copy in own_weights:
        copy.wait()
    recv(wt.at[:, :, :, pl.ds(0, hid)], WPART)
    recv(wt.at[0, :, :, pl.ds(0, hid)], WF)
    for k in range(3):
        begin(k)
    pass_weights(1)
    pass_rows(3)
    begin(3)
    recv(wt.at[0, :, :, pl.ds(0, hid)], WF + 1)
    finish(0)

    activate(0)
    finish(1)
    answer(0)
    activate(1)
    finish(2)

    answer(1)
    activate(2)
    finish(3)
    rcopy(xr.at[:, 1 - core], xp, XP, (e, partner)).start()
    answer(2)
    activate(3)
    for j in (weight_chip, lax.rem(chip + 2, chips)):
        rcopy(pair, g.at[block(t, 16)], TOKX, (e, 2 * j + core)).start()
    give_back(0)
    answer(3)

    recv(xp, XP)
    recv(actp, ACTP)
    own_grads = []

    def gradient(n, m):
        span = slice(0, half) if m == 2 else slice((m + 1) * half, (m + 2) * half)
        kind = slice(SLOTS, m32) if m == 2 else slice(0, SLOTS)
        here = act[:, :, :, span].reshape(4 * rows, half)
        there = actp[:, :, :, span].reshape(4 * rows, half)
        x_here = xr[n, core, :, kind].reshape(4 * rows, d8)
        x_there = xp[n, :, kind].reshape(4 * rows, d8)
        gb[n, m] = (dot(here, x_here, TN) + dot(there, x_there, TN)).astype(BF)
        target = (gout_ref if m == 2 else gin_ref.at[m]).at[:, cols(4 * a + 2 * n + core)]
        which = GRAD_OUT if m == 2 else GRAD_IN
        for c in range(2):
            rcopy(gb.at[n, m, block(2 * (1 - a) + c, hid)], target, which, (e, 2 * weight_chip + c)).start()
        rcopy(gb.at[n, m, block(2 * a + 1 - core, hid)], target, which, (e, partner)).start()
        own = pltpu.make_async_copy(gb.at[n, m, block(place, hid)], target, lsem.at[2 + 3 * n + m])
        own.start()
        own_grads.append(own)

    for m in range(3):
        gradient(0, m)
    give_back(1)
    for m in range(3):
        gradient(1, m)
    recv(g.at[pl.ds(0, (chips - 1) * 16)], TOKX)

    @pl.loop(1, chips)
    def _(k):
        part = g.at[block(lax.rem(t + 2 * k, nt), 16)]
        rcopy(part, part, TOKP, (e, partner)).start()

    give_back(2)
    recv(g.at[pl.ds(0, chips * 16)], TOKP)
    for copy in own_shared:
        copy.wait()
    sh = sw_out.shape[0]

    def shared_step(n, sums):
        piece = g[:, cols(n)]
        return tuple(
            total + dot(piece, weight[:, cols(n)], NT)
            for total, weight in zip(sums, (sw_in.at[0], sw_in.at[1], sw_out)))

    zero = jnp.zeros((nt * 16, sh), F32)
    sums = lax.fori_loop(0, nt, shared_step, (zero, zero, zero))
    s_gate, s_up = [v.reshape(nt, 16, sh)[:, :8].reshape(nt * 8, sh) for v in sums[:2]]
    s_back = sums[2].reshape(nt, 16, sh)[:, 8:].reshape(nt * 8, sh)
    s_act, s_slope = silu_parts(s_gate)
    s_hidden = (s_act * s_up).astype(BF)
    s_dgate = (s_back * s_up * s_slope).astype(BF)
    s_dup = (s_back * s_act).astype(BF)

    def shared_terms(low, high):
        @pl.loop(low, high)
        def _(n):
            y = dot(s_hidden, sw_out[:, cols(n)]).reshape(nt, 8, d8)
            dx = (dot(s_dgate, sw_in[0, :, cols(n)]) + dot(s_dup, sw_in[1, :, cols(n)])).reshape(nt, 8, d8)
            shs[:, :, :, cols(n)] = jnp.concatenate([y, dx], axis=1).astype(BF).reshape(chips, 2, 16, d8)

    shared_terms(0, nt)
    rcopy(shs.at[:, 1 - core], shp, SHP, (e, partner)).start()
    give_back(3)
    recv(shp, SHP)
    for n in range(chips):
        shs[n, core] = (shs[n, core].astype(F32) + shp[n].astype(F32)).astype(BF)

    rcopy(shs.at[row_chip, core], shr.at[0], SHARED, row_dev).start()
    rcopy(shs.at[chips - 1 - row_chip, core], shr.at[1], SHARED, row_dev).start()
    recv(shr.at[pl.ds(0, 2)], SHARED)
    shs[weight_chip, core] = (shs[weight_chip, core].astype(F32) + shr[1].astype(F32)).astype(BF)
    rcopy(shs.at[weight_chip, core], shr.at[2], SUMS, weight_dev).start()
    shr[1] = shs[chip, core]

    recv(bk, BACK)
    routed = dot(t2[...], bk[...].reshape(ne * m32, d8), TN)
    fs[...] = routed.astype(BF).reshape(nt, 16, d8)

    @pl.loop(1, nt)
    def _(k):
        p = lax.rem(t + k, nt)
        rcopy(fs.at[p], fr.at[t], FINAL, (e, p)).start()

    fr[t] = fs[t]
    recv(shr.at[2], SUMS)
    recv(fr.at[pl.ds(0, nt - 1)], FINAL)

    for n in range(nt):
        span = slice(n * d8, (n + 1) * d8)
        total = fr[n].astype(F32) + jnp.sum(shr[:, :, span].astype(F32), axis=0)
        out_ref[:, span] = total[:8].astype(BF)
        gtok_ref[:, span] = total[8:].astype(BF)

    recv(gin_ref.at[:, :, pl.ds(0, 6 * d8)], GRAD_IN)
    recv(gout_ref.at[:, pl.ds(0, 6 * d8)], GRAD_OUT)
    for copy in own_grads:
        copy.wait()
    sent(tabs.at[pl.ds(0, (nt - 1) * 16)], TAB)
    sent(gs.at[pl.ds(0, (nt - 1) * 16)], SLICE)
    sent(g.at[pl.ds(0, (chips - 1) * 16)], TOKX)
    sent(g.at[pl.ds(0, chips * 16)], TOKP)
    sent(wt.at[:, :, :, pl.ds(0, hid)], WPART)
    for n in range(2):
        sent(wt.at[n, :, :, pl.ds(0, hid)], WX + n)
        sent(wt.at[n, :, :, pl.ds(0, hid)], WF + n)
    for k in range(4):
        sent(xr.at[0, :, pl.ds(0, gq)], PAIR + k)
        sent(ps.at[:, pl.ds(0, gq)], HALF + k)
    sent(xp, XP)
    for k in range(4):
        sent(rs.at[0], PRE + k)
        sent(rs.at[0], ACT + k)
    sent(actp, ACTP)
    sent(shp, SHP)
    sent(shr.at[pl.ds(0, 2)], SHARED)
    sent(shr.at[0], SUMS)
    sent(gin_ref.at[:, :, pl.ds(0, 6 * d8)], GRAD_IN)
    sent(gout_ref.at[:, pl.ds(0, 6 * d8)], GRAD_OUT)
    sent(fs.at[pl.ds(0, nt - 1)], FINAL)

    @pl.when(stays)
    def _():
        sent(bk.at[pl.ds(0, ne - 1)], BACK)
        sent(bk.at[pl.ds(0, ne - 1)], DISP + first)

    @pl.when(jnp.logical_not(stays))
    def _():
        sent(bk, BACK)
        sent(bk, DISP + first)


def hand_over(out_a, gtok_a, gin_a, gout_a, out_b, gtok_b, gin_b, gout_b, small, big, sem):
    hid = gout_a.shape[0]
    part = hid // 2
    moves = []
    for m in range(3):
        left, right = (gout_a, gout_b) if m == 2 else (gin_a.at[m], gin_b.at[m])
        for n in range(2):
            rows = pl.ds(n * part, part)
            moves.append((left.at[rows], big.at[m, rows], right.at[rows]))
    moves += [(out_a, small.at[0], out_b), (gtok_a, small.at[1], gtok_b)]
    inward = [pltpu.make_async_copy(src, mid, sem.at[0, n]) for n, (src, mid, _) in enumerate(moves)]
    outward = [pltpu.make_async_copy(mid, dst, sem.at[1, n]) for n, (_, mid, dst) in enumerate(moves)]
    for copy in inward:
        copy.start()
    for before, after in zip(inward, outward):
        before.wait()
        after.start()
    for copy in outward:
        copy.wait()


def on_device(tokens, routes, gate_num, cotangent, w_in, w_out, shared_in, shared_out):
    ne, nt = lax.axis_size("expert"), lax.axis_size("tensor")
    chips = nt // 2
    own, features = tokens.shape
    topk = routes.shape[1]
    hid, sh = w_out.shape[1], shared_out.shape[0]
    d8, half, gl_count = features // nt, 4 * hid, ne // 2
    rows, m32 = gl_count * SLOTS // 4, 2 * SLOTS
    vm = pl.BlockSpec(memory_space=pltpu.VMEM)
    hbm = pl.BlockSpec(memory_space=pl.ANY)
    scratch = [
        pltpu.VMEM((16, features), BF),
        pltpu.VMEM((16, 128), jnp.int32),
        pltpu.VMEM((nt * 16, 128), jnp.int32),
        pltpu.VMEM((nt * 16, d8), BF),
        pltpu.VMEM((nt * 16, features), BF),
        pltpu.VMEM((2, 2, 3, half, d8), BF),
        pltpu.VMEM((2, sh, features), BF),
        pltpu.VMEM((sh, features), BF),
        pltpu.VMEM((ne * m32, nt * 16), BF),
        pltpu.VMEM((ne, m32, d8), BF),
        pltpu.VMEM((2, 2, gl_count, m32, d8), BF),
        pltpu.VMEM((2, gl_count, m32, d8), BF),
        pltpu.VMEM((4, rows, 3 * half), F32),
        pltpu.VMEM((4, rows // 2, 3 * half), BF),
        pltpu.VMEM((4, rows // 2, 3 * half), BF),
        pltpu.VMEM((4, 2, rows // 2, 3 * half), BF),
        pltpu.VMEM((4, 2, rows // 2, 3 * half), BF),
        pltpu.VMEM((2, gl_count, m32, d8), BF),
        pltpu.VMEM((2, gl_count, m32, d8), BF),
        pltpu.VMEM((2, gl_count, m32, d8), F32),
        pltpu.VMEM((2, gl_count, m32, d8), BF),
        pltpu.VMEM((ne, m32, d8), BF),
        pltpu.VMEM((2, 3, half, d8), BF),
        pltpu.VMEM((chips, 2, 16, features), BF),
        pltpu.VMEM((chips, 16, features), BF),
        pltpu.VMEM((3, 16, features), BF),
        pltpu.VMEM((nt, 16, d8), BF),
        pltpu.VMEM((nt, 16, d8), BF),
        pltpu.SemaphoreType.DMA((COUNT,)),
        pltpu.SemaphoreType.DMA((COUNT,)),
        pltpu.SemaphoreType.DMA((14,)),
    ]
    shapes = (
        jax.ShapeDtypeStruct((own, features), BF),
        jax.ShapeDtypeStruct((own, features), BF),
        jax.ShapeDtypeStruct((2, hid, features), BF),
        jax.ShapeDtypeStruct((hid, features), BF),
    )
    results = pl.pallas_call(
        functools.partial(kernel, topk),
        out_shape=shapes,
        in_specs=[vm, vm, vm, vm, hbm, hbm, hbm, hbm],
        out_specs=(vm, vm, hbm, hbm),
        scratch_shapes=scratch,
        compiler_params=pltpu.CompilerParams(
            collective_id=0, has_side_effects=True, vmem_limit_bytes=56 * 2**20
        ),
    )(tokens, cotangent, routes, gate_num, w_in[0], w_out[0], shared_in, shared_out)
    out, gtok, gin, gout = pl.pallas_call(
        hand_over,
        out_shape=shapes,
        in_specs=[hbm] * 4,
        out_specs=(hbm,) * 4,
        scratch_shapes=[
            pltpu.VMEM((2, own, features), BF),
            pltpu.VMEM((3, hid, features), BF),
            pltpu.SemaphoreType.DMA((2, 8)),
        ],
        compiler_params=pltpu.CompilerParams(vmem_limit_bytes=60 * 2**20),
    )(*results)
    return out, gtok, gin[None], gout[None]


def solution(mesh):
    in_specs = (
        P(("expert", "tensor"), None),
        P(("expert", "tensor"), None),
        P(("expert", "tensor"), None),
        P(("expert", "tensor"), None),
        P("expert", None, "tensor", None),
        P("expert", "tensor", None),
        P(None, "tensor", None),
        P("tensor", None),
    )
    out_specs = (
        P(("expert", "tensor"), None),
        P(("expert", "tensor"), None),
        P("expert", None, "tensor", None),
        P("expert", "tensor", None),
    )
    return jax.shard_map(
        on_device, mesh=mesh, in_specs=in_specs, out_specs=out_specs, check_vma=False
    )
```
